32 devices in a mesh: rep: 4 (over y, core), fsdp: 8 (over z, x).
Axes of the slice: x: 2, y: 2, z: 4, core: 2. Of those that a mesh axis runs over, the one named last changes fastest.
Arguments:
- hidden_in: bfloat16 [32, 128, 1536], P(('rep', 'fsdp')), may hold values from -6 to 6
- doc_lengths: int32 [32, 5], P(('rep', 'fsdp')), may hold values from 1 to 64, 128 in all within a row
- w_query: bfloat16 [1536, 1536], P('fsdp'), may hold values from -0.15625 to 0.15625
- w_key: bfloat16 [1536, 1536], P('fsdp'), may hold values from -0.15625 to 0.15625
- w_value: bfloat16 [1536, 1536], P('fsdp'), may hold values from -0.15625 to 0.15625
- w_output: bfloat16 [1536, 1536], P('fsdp'), may hold values from -0.15625 to 0.15625
- w_gate: bfloat16 [1536, 4096], P('fsdp'), may hold values from -0.15625 to 0.15625
- w_up: bfloat16 [1536, 4096], P('fsdp'), may hold values from -0.15625 to 0.15625
- w_down: bfloat16 [4096, 1536], P('fsdp'), may hold values from -0.09375 to 0.09375
- attn_norm: float32 [1536], replicated, may hold values from 0.25 to 1.75
- mlp_norm: float32 [1536], replicated, may hold values from 0.25 to 1.75
- head_norm: float32 [1536], replicated, may hold values from 0.25 to 1.75
- score_kernel: float32 [16, 6, 11], replicated, may hold values from -1.2 to 1.2
- head_mixing: float32 [16, 2], replicated, may hold values from 0.25 to 1
- grad_out: bfloat16 [32, 128, 1536], P(('rep', 'fsdp')), may hold values from -6 to 6
Outputs:
- block_out: bfloat16 [32, 128, 1536], P(('rep', 'fsdp'))
- grad_in: bfloat16 [32, 128, 1536], P(('rep', 'fsdp'))
- grad_query: float32 [1536, 1536], P('fsdp')
- grad_key: float32 [1536, 1536], P('fsdp')
- grad_value: float32 [1536, 1536], P('fsdp')
- grad_output: float32 [1536, 1536], P('fsdp')
- grad_gate: float32 [1536, 4096], P('fsdp')
- grad_up: float32 [1536, 4096], P('fsdp')
- grad_down: float32 [4096, 1536], P('fsdp')
- grad_attn_norm: float32 [1536], replicated
- grad_mlp_norm: float32 [1536], replicated
- grad_head_norm: float32 [1536], replicated
- grad_score_kernel: float32 [16, 6, 11], replicated
- grad_head_mixing: float32 [16, 2], replicated
- root_means: float32 [3], replicated
The draws below stay inside these ranges and needn't reach their ends.
Inputs may be any that keep to these rules, and one draw needn't show every extreme that they name: `doc_lengths`: each row lists the lengths of its 4 documents in order and then the length of the padding that ends the row; a row's entries sum to 128 and its largest entry is 64.
All inputs are finite; a program needn't handle non-finite values.
Results may differ from the reference program's by a relative error of at most 0.019.
Values may be sent and summed in bfloat16 or wider, within the bound.
A program may use at most 448 MiB of HBM per device.

```python
import math
import jax
import jax.numpy as jnp
import numpy as np
from jax import lax

D = 1536
H = 16
HD = 96
FF = 4096
CQ = 6
CK = 11
DOCS = 4
ROW_LEN = 128
ROWS = 32


def with_spikes(values, own_key, source, target, shards_of, factor):
    def block_of(axis_at):
        return (jnp.arange(values.shape[axis_at]) // (values.shape[axis_at] // shards_of)).reshape((-1,) + (1,) * (values.ndim - 1 - axis_at))

    near = jax.random.permutation(own_key, shards_of)[block_of(target)]
    far = (block_of(target) + shards_of // 2) % shards_of
    return jnp.where((block_of(source) == near) | (block_of(source) == far), factor * values, values)


def block_levels(rng, dims, split, least, high):
    loudness, own = 1.0, jax.random.fold_in(rng, 6)
    for axis_at, parts in split:
        heights = jnp.exp(jax.random.uniform(jax.random.fold_in(own, axis_at), (parts,), jnp.float32, least / len(split), high / len(split)))
        loudness = loudness * jnp.repeat(heights, dims[axis_at] // parts).reshape([-1 if axis == axis_at else 1 for axis in range(len(dims))])
    return loudness


def length_profile(number_of, total, limit, lean):
    loads = [(1 << 20) // math.isqrt(rank ** lean) + 1 for rank in range(2, number_of + 1)]
    surplus, given = total - limit - (number_of - 1), [1] * (number_of - 1)
    while surplus > 0:
        candidates = [i for i in range(number_of - 1) if given[i] < limit]
        pool, left = sum([loads[i] for i in candidates]), surplus
        for i in candidates:
            addition = min(limit - given[i], max(1, left * loads[i] // pool), surplus)
            given[i] = given[i] + addition
            surplus = surplus - addition
    return np.array([limit] + given)


def ragged_sizes(stream_key, number_of, total, reach, slope):
    if number_of == 2:
        one = jax.random.randint(stream_key, (), max(1, total - reach), min(reach, total - 1) + 1)
        return jnp.stack([one, total - one])
    lengths = jnp.asarray(length_profile(number_of, total, reach, slope), jnp.int32)
    couples = (number_of - 1) // 2
    giver, receiver = lengths[1:1 + 2 * couples:2], lengths[2:2 + 2 * couples:2]
    slack = jnp.minimum(giver - 1, reach - receiver)
    passed = jax.random.randint(jax.random.fold_in(stream_key, 1), (couples,), 0, 1 << 20) % (slack + 1)
    lengths = lengths.at[1:1 + 2 * couples:2].set(giver - passed).at[2:2 + 2 * couples:2].set(receiver + passed)
    return lengths[jax.random.permutation(jax.random.fold_in(stream_key, 2), number_of)]


def normal_values(rng, shape, deviation, most, split=(), held_as=jnp.bfloat16):
    values = deviation * jax.random.normal(rng, shape, jnp.float32)
    if split:
        values = values * block_levels(rng, shape, split, -0.22, 0.18)
    return jnp.clip(values, -most, most).astype(held_as)


def heavy_noise(own_key, dims, deviation, reach, shards, heavy, held_as=jnp.bfloat16):
    array = deviation * jax.random.normal(own_key, dims, jnp.float32)
    if shards:
        array = array * block_levels(own_key, dims, shards, -0.22, 0.18)
    return jnp.clip(with_spikes(array, jax.random.fold_in(own_key, 3), *heavy), -reach, reach).astype(held_as)


def setup_inputs(seed: int = 0) -> dict:
    splits = jax.random.split(jax.random.key(seed), 16)
    hidden_in = heavy_noise(splits[0], (ROWS, ROW_LEN, D), 1.0, 6.0, ((0, 32),), (0, 2, 32, 2.75))
    doc_lengths = jax.vmap(lambda own: ragged_sizes(own, DOCS + 1, ROW_LEN, ROW_LEN // 2, 2))(jax.random.split(splits[1], ROWS)).reshape((ROWS, DOCS + 1)).astype(jnp.int32)
    w_query = normal_values(splits[2], (D, D), D ** -0.5, 0.15625, ((0, 8),))
    w_key = normal_values(splits[3], (D, D), D ** -0.5, 0.15625, ((0, 8),))
    w_value = normal_values(splits[4], (D, D), D ** -0.5, 0.15625, ((0, 8),))
    w_output = normal_values(splits[5], (D, D), D ** -0.5, 0.15625, ((0, 8),))
    w_gate = normal_values(splits[6], (D, FF), D ** -0.5, 0.15625, ((0, 8),))
    w_up = normal_values(splits[7], (D, FF), D ** -0.5, 0.15625, ((0, 8),))
    w_down = normal_values(splits[8], (FF, D), FF ** -0.5, 0.09375, ((0, 8),))
    attn_norm = jnp.clip(1.0 + 0.15 * jax.random.normal(splits[9], (D,), jnp.float32), 0.25, 1.75)
    mlp_norm = jnp.clip(1.0 + 0.15 * jax.random.normal(splits[10], (D,), jnp.float32), 0.25, 1.75)
    head_norm = jnp.clip(1.0 + 0.15 * jax.random.normal(splits[11], (D,), jnp.float32), 0.25, 1.75)
    score_kernel = normal_values(splits[12], (H, CQ, CK), 0.2, 1.2, (), jnp.float32)
    head_mixing = jnp.clip(jax.random.uniform(splits[13], (H, 2), jnp.float32, 0.25, 1.0), 0.25, 1.0)
    grad_out = normal_values(splits[14], (ROWS, ROW_LEN, D), 1.0, 6.0, ((0, 32),))
    return {"hidden_in": hidden_in, "doc_lengths": doc_lengths, "w_query": w_query, "w_key": w_key, "w_value": w_value, "w_output": w_output, "w_gate": w_gate, "w_up": w_up, "w_down": w_down, "attn_norm": attn_norm, "mlp_norm": mlp_norm, "head_norm": head_norm, "score_kernel": score_kernel, "head_mixing": head_mixing, "grad_out": grad_out}


@jax.custom_vjp
def low(v):
    return lax.optimization_barrier(v.astype(jnp.bfloat16)).astype(jnp.float32)

@jax.custom_vjp
def low_back(v):
    return v

def low_keep(v):
    return (low(v), None)

def low_pass(kept, grad):
    return (grad,)

def back_keep(v):
    return (v, None)

def back_low(kept, grad):
    return (low(grad),)
low.defvjp(low_keep, low_pass)
low_back.defvjp(back_keep, back_low)
HIGHEST = lax.Precision.HIGHEST

def segment_ids(doc_lengths, row_len):
    boundary = jnp.cumsum(doc_lengths[:, :-1], axis=1)
    places = jnp.arange(row_len, dtype=jnp.int32)
    return lax.optimization_barrier(jnp.sum((places[None, :, None] >= boundary[:, None, :]).astype(jnp.int32), axis=2))

def conv_forward(masked, kernel):
    row_taps = kernel.shape[1]
    col_taps = kernel.shape[2]
    margin = (col_taps - 1) // 2
    extent = masked.shape[-1]
    padded = jnp.pad(masked, ((0, 0), (0, 0), (row_taps - 1, 0), (margin, margin)))
    summed = jnp.zeros_like(masked)
    for row_lag in range(row_taps):
        for col_lag in range(col_taps):
            row_start = row_taps - 1 - row_lag
            col_start = col_taps - 1 - col_lag
            summed = summed + kernel[None, :, row_lag, col_lag, None, None] * padded[:, :, row_start:row_start + extent, col_start:col_start + extent]
    return summed

def attend_row(packed, kernel, mixing):
    queries, keys_in, values, allowed = packed
    raw_scores = low_back(jnp.einsum('ihd,jhd->hij', queries, keys_in, precision=HIGHEST) * HD ** (-0.5))
    masked = jnp.where(allowed[None], raw_scores, 0.0)
    convolved = conv_forward(masked[None], kernel)[0]
    softmaxed = jax.nn.softmax(jnp.where(allowed[None], convolved, -1e+30), axis=-1)
    paired = softmaxed.reshape(H // 2, 2, ROW_LEN, ROW_LEN)
    mixed_heads = jnp.einsum('gcij,gec->geij', paired, mixing.reshape(H // 2, 2, 2), precision=HIGHEST)
    mixed_heads = low(mixed_heads.reshape(H, ROW_LEN, ROW_LEN))
    return low_back(jnp.einsum('hij,jhd->ihd', mixed_heads, values, precision=HIGHEST))

def layer(hidden_f, w_query, w_key, w_value, w_output, w_gate, w_up, w_down, attn_norm, mlp_norm, head_norm, score_kernel, head_mixing, valid_rows, allowed):
    row_count = hidden_f.shape[0]
    resid_in = hidden_f.reshape(-1, D)
    inv_first = lax.rsqrt(lax.optimization_barrier(jnp.mean(resid_in * resid_in, axis=1, keepdims=True)) + 1e-06)
    attn_in = low(resid_in * inv_first * attn_norm)
    queries = low_back(low(jnp.dot(attn_in, w_query, precision=HIGHEST)))
    keys_all = low_back(low(jnp.dot(attn_in, w_key, precision=HIGHEST)))
    values = low_back(low(jnp.dot(attn_in, w_value, precision=HIGHEST)))

    def one_row(packed):
        return attend_row(packed, score_kernel, head_mixing)
    heads_shape = (row_count, ROW_LEN, H, HD)
    heads_out = lax.map(jax.checkpoint(one_row), (queries.reshape(heads_shape), keys_all.reshape(heads_shape), values.reshape(heads_shape), allowed))
    heads_out = heads_out.reshape(-1, H, HD)
    centred = heads_out - lax.optimization_barrier(jnp.mean(heads_out, axis=2, keepdims=True))
    head_hat = centred * lax.rsqrt(lax.optimization_barrier(jnp.mean(centred * centred, axis=2, keepdims=True)) + 1e-05)
    head_in = low(head_hat.reshape(-1, D) * head_norm)
    attn_out = low_back(jnp.dot(head_in, w_output, precision=HIGHEST))
    attn_part = valid_rows * attn_out
    middle = resid_in + attn_part
    inv_second = lax.rsqrt(lax.optimization_barrier(jnp.mean(middle * middle, axis=1, keepdims=True)) + 1e-06)
    mlp_in = low(middle * inv_second * mlp_norm)
    gate = low_back(jnp.dot(mlp_in, w_gate, precision=HIGHEST))
    upper = low_back(jnp.dot(mlp_in, w_up, precision=HIGHEST))
    hidden_act = low(jax.nn.silu(gate) * upper)
    mlp_out = low_back(jnp.dot(hidden_act, w_down, precision=HIGHEST))
    mlp_part = valid_rows * mlp_out
    result = middle + mlp_part
    return (result.reshape(row_count, ROW_LEN, D), (attn_part, mlp_part))

def reference(hidden_in, doc_lengths, w_query, w_key, w_value, w_output, w_gate, w_up, w_down, attn_norm, mlp_norm, head_norm, score_kernel, head_mixing, grad_out):
    group_rows = min(ROWS, max(1, 4096 // ROW_LEN))
    group_count = ROWS // group_rows
    params = tuple((weight.astype(jnp.float32) for weight in (w_query, w_key, w_value, w_output, w_gate, w_up, w_down, attn_norm, mlp_norm, head_norm, score_kernel, head_mixing)))
    places = jnp.arange(ROW_LEN, dtype=jnp.int32)

    def scan_step(running, packed):
        grads_sum, stat_sums = running
        hidden_rows, length_rows, cotangent = packed
        seg_ids = segment_ids(length_rows, ROW_LEN)
        valid_rows = (seg_ids < DOCS).astype(jnp.float32).reshape(-1, 1)
        allowed = (seg_ids[:, :, None] == seg_ids[:, None, :]) & (places[None, None, :] <= places[None, :, None])

        def apply_layer(hidden_f, *weights):
            return layer(hidden_f, *weights, valid_rows, allowed)
        result, pullback, branches = jax.vjp(apply_layer, hidden_rows.astype(jnp.float32), *params, has_aux=True)
        gradients = pullback(cotangent.astype(jnp.float32))
        flat_out = result.reshape(-1, D)
        sums_now = jnp.stack([jnp.sum(valid_rows * flat_out * flat_out), jnp.sum(branches[0] * branches[0]), jnp.sum(branches[1] * branches[1]), jnp.sum(valid_rows)])
        grads_sum = jax.tree.map(jnp.add, grads_sum, tuple(gradients[1:]))
        return ((grads_sum, stat_sums + sums_now), (result.astype(jnp.bfloat16), gradients[0].astype(jnp.bfloat16)))
    start_state = (tuple((jnp.zeros_like(weight) for weight in params)), jnp.zeros((4,), jnp.float32))
    inputs_grouped = (hidden_in.reshape(group_count, group_rows, ROW_LEN, D), doc_lengths.reshape(group_count, group_rows, DOCS + 1), grad_out.reshape(group_count, group_rows, ROW_LEN, D))
    (grad_total, stat_total), (block_out, grad_in) = lax.scan(scan_step, start_state, inputs_grouped)
    root_means = jnp.sqrt(stat_total[:3] / (stat_total[3] * D))
    return (block_out.reshape(ROWS, ROW_LEN, D), grad_in.reshape(ROWS, ROW_LEN, D), grad_total[0], grad_total[1], grad_total[2], grad_total[3], grad_total[4], grad_total[5], grad_total[6], grad_total[7], grad_total[8], grad_total[9], grad_total[10], grad_total[11], root_means)
```

```python
import functools

import jax
import jax.numpy as jnp
from jax import lax
from jax.experimental import pallas as pl
from jax.experimental.pallas import tpu as pltpu
from jax.sharding import PartitionSpec as P

H = 16
BF = jnp.bfloat16
F32 = jnp.float32
MESH = pl.DeviceIdType.MESH
VMEM_LIMIT = 48 * 1024 * 1024
NN = (((1,), (0,)), ((), ()))
NT = (((1,), (1,)), ((), ()))
TN = (((0,), (0,)), ((), ()))


def dot(a, b, dims=NN):
    return lax.dot_general(a, b, dims, preferred_element_type=F32)


def vmem_spec():
    return pl.BlockSpec(memory_space=pltpu.VMEM)


def smem_spec():
    return pl.BlockSpec(memory_space=pltpu.SMEM)


def hbm_spec():
    return pl.BlockSpec(memory_space=pl.ANY)


def rep_places():
    me = lax.axis_index("rep")
    shard = lax.axis_index("fsdp")
    plane = me // 2
    core = me % 2
    sibling = plane * 2 + (1 - core)
    across = (1 - plane) * 2 + core
    return me, shard, plane, core, sibling, across


def rep_barrier(shard, sibling, across):
    barrier = pltpu.get_barrier_semaphore()
    for peer in (sibling, across):
        pl.semaphore_signal(barrier, inc=1, device_id=(peer, shard), device_id_type=MESH)
    pl.semaphore_wait(barrier, 2)


def remote(src, dst, sems, slot, shard, peer):
    send_sem, recv_sem = sems
    return pltpu.make_async_remote_copy(
        src_ref=src,
        dst_ref=dst,
        send_sem=send_sem.at[slot],
        recv_sem=recv_sem.at[slot],
        device_id=(peer, shard),
        device_id_type=MESH,
    )


def gather_over_rep(full_refs, own_refs, sems, first_slot):
    me, shard, _, _, sibling, across = rep_places()
    slot = first_slot
    to_across, to_sibling, passed_on = [], [], []
    for full, own in zip(full_refs, own_refs):
        a = remote(own, full.at[me], sems, slot, shard, across)
        b = remote(own, full.at[me], sems, slot + 1, shard, sibling)
        a.start()
        b.start()
        to_across.append(a)
        to_sibling.append(b)
        slot += 2
    for full, a in zip(full_refs, to_across):
        a.wait_recv()
        c = remote(full.at[across], full.at[across], sems, slot, shard, sibling)
        c.start()
        passed_on.append(c)
        slot += 1
    for b, c in zip(to_sibling, passed_on):
        b.wait_recv()
        c.wait_recv()
    for c in to_across + to_sibling + passed_on:
        c.wait_send()


def inputs_kernel(x_ref, g_ref, seg_ref, norm_ref, attn_in_ref, g_mlp_ref, seg_all_ref, x_all, g_all, send, recv):
    me, shard, _, _, sibling, across = rep_places()
    rep_barrier(shard, sibling, across)
    x_all[me] = x_ref[...]
    g_all[me] = g_ref[...]
    seg_all_ref[me] = seg_ref[...]
    fulls = (seg_all_ref, x_all, g_all)
    gather_over_rep(fulls, tuple(f.at[me] for f in fulls), (send, recv), 0)

    @pl.loop(0, 4)
    def _(r):
        rows = x_all[r].astype(F32)
        inv = lax.rsqrt(jnp.mean(rows * rows, axis=1, keepdims=True) + 1e-06)
        attn_in_ref[r] = (rows * inv * norm_ref[...]).astype(BF)
        valid = jnp.transpose(jnp.broadcast_to(seg_all_ref[r][0:1, :], (128, 128)))[:, 0:1] < 4.0
        g_mlp_ref[r] = jnp.where(valid, g_all[r].astype(F32), 0.0).astype(BF)


def gather_inputs(x, g, seg, norm):
    t, d = x.shape
    return pl.pallas_call(
        inputs_kernel,
        out_shape=(
            jax.ShapeDtypeStruct((4, t, d), BF),
            jax.ShapeDtypeStruct((4, t, d), BF),
            jax.ShapeDtypeStruct((4,) + seg.shape, F32),
        ),
        in_specs=[vmem_spec()] * 4,
        out_specs=(vmem_spec(),) * 3,
        scratch_shapes=[
            pltpu.VMEM((4, t, d), BF),
            pltpu.VMEM((4, t, d), BF),
            pltpu.SemaphoreType.DMA((9,)),
            pltpu.SemaphoreType.DMA((9,)),
        ],
        compiler_params=pltpu.CompilerParams(
            collective_id=0, has_side_effects=True, vmem_limit_bytes=VMEM_LIMIT
        ),
    )(x, g, seg, norm)


def grads_kernel(count, *refs):
    owns = refs[:count]
    fulls = refs[count : 2 * count]
    local, send, recv = refs[2 * count :]
    me, shard, _, _, sibling, across = rep_places()
    rep_barrier(shard, sibling, across)
    copies = []
    for k in range(count):
        copy = pltpu.make_async_copy(owns[k], fulls[k].at[me], local.at[k])
        copy.start()
        copies.append(copy)
    gather_over_rep(fulls, owns, (send, recv), 0)
    for copy in copies:
        copy.wait()


def gather_grads(*shards):
    count = len(shards)
    return pl.pallas_call(
        functools.partial(grads_kernel, count),
        out_shape=tuple(jax.ShapeDtypeStruct((4,) + s.shape, s.dtype) for s in shards),
        in_specs=[hbm_spec()] * count,
        out_specs=(hbm_spec(),) * count,
        scratch_shapes=[
            pltpu.SemaphoreType.DMA((count,)),
            pltpu.SemaphoreType.DMA((3 * count,)),
            pltpu.SemaphoreType.DMA((3 * count,)),
        ],
        compiler_params=pltpu.CompilerParams(
            collective_id=1, has_side_effects=True, vmem_limit_bytes=VMEM_LIMIT
        ),
    )(*shards)


def exchange_kernel(dims, post, gather, extra_count, out_count, lhs_ref, rhs_ref, *refs):
    extras = refs[:extra_count]
    outs = refs[extra_count : extra_count + out_count]
    psend, pown, r1, ysend, r2, send, recv = refs[extra_count + out_count :]
    sems = (send, recv)
    me, shard, plane, core, sibling, across = rep_places()
    rep_barrier(shard, sibling, across)
    other = 1 - core
    theirs = jnp.concatenate([lhs_ref[other], lhs_ref[2 + other]], axis=0)
    product = dot(theirs, rhs_ref[...], dims)
    t = lhs_ref.shape[1]
    psend[0] = product[:t].astype(BF)
    psend[1] = product[t:].astype(BF)
    first = remote(psend, r1, sems, 0, shard, sibling)
    first.start()
    ours = jnp.concatenate([lhs_ref[across], lhs_ref[me]], axis=0)
    product = dot(ours, rhs_ref[...], dims)
    pown[0] = product[:t]
    pown[1] = product[t:]
    first.wait_recv()
    ysend[...] = (pown[0] + r1[1 - plane].astype(F32)).astype(BF)
    second = remote(ysend, r2, sems, 1, shard, across)
    second.start()
    mine = pown[1] + r1[plane].astype(F32)
    pown[1] = mine
    second.wait_recv()
    total = pown[1] + r2[...].astype(F32)
    if gather:
        full = outs[0]
        full[me] = post(total, extras, outs[1:])
        gather_over_rep((full,), (full.at[me],), sems, 2)
    else:
        post(total, extras, outs)
    first.wait_send()
    second.wait_send()


def exchange(cid, lhs, rhs, dims, extras, post, gather, outs):
    _, t, _ = lhs.shape
    width = rhs.shape[1] if dims is NN else rhs.shape[0]
    if gather:
        outs = (jax.ShapeDtypeStruct((4, t, width), BF),) + tuple(outs)
    return pl.pallas_call(
        functools.partial(exchange_kernel, dims, post, gather, len(extras), len(outs)),
        out_shape=tuple(outs),
        in_specs=[vmem_spec()] * (2 + len(extras)),
        out_specs=(vmem_spec(),) * len(outs),
        scratch_shapes=[
            pltpu.VMEM((2, t, width), BF),
            pltpu.VMEM((2, t, width), F32),
            pltpu.VMEM((2, t, width), BF),
            pltpu.VMEM((t, width), BF),
            pltpu.VMEM((t, width), BF),
            pltpu.SemaphoreType.DMA((5,)),
            pltpu.SemaphoreType.DMA((5,)),
        ],
        compiler_params=pltpu.CompilerParams(
            collective_id=cid, has_side_effects=True, vmem_limit_bytes=VMEM_LIMIT
        ),
    )(lhs, rhs, *extras)


def total_of(value):
    rows = jnp.sum(value, axis=0, keepdims=True)
    return jnp.broadcast_to(jnp.sum(rows, axis=1, keepdims=True), (1, 128))


def post_attn_out(total, extras, outs):
    x_ref, valid_ref, norm_ref = extras
    middle_ref, stat_ref = outs
    attn_part = valid_ref[...] * total
    middle = x_ref[...].astype(F32) + attn_part
    middle_ref[...] = middle
    stat_ref[...] = jnp.sum(attn_part * attn_part, axis=0, keepdims=True)
    inv = lax.rsqrt(jnp.mean(middle * middle, axis=1, keepdims=True) + 1e-06)
    return (middle * inv * norm_ref[...]).astype(BF)


def post_mlp_grad(total, extras, outs):
    middle_ref, g_ref, valid_ref, norm_ref = extras
    g_middle_ref, g_norm_ref = outs
    middle = middle_ref[...]
    inv = lax.rsqrt(jnp.mean(middle * middle, axis=1, keepdims=True) + 1e-06)
    normed = middle * inv
    prod = total * normed
    g_norm_ref[...] = jnp.sum(prod, axis=0, keepdims=True)
    scaled = total * norm_ref[...]
    mean = jnp.mean(prod * norm_ref[...], axis=1, keepdims=True)
    g_middle = g_ref[...].astype(F32) + inv * (scaled - normed * mean)
    g_middle_ref[...] = g_middle
    return (valid_ref[...] * g_middle).astype(BF)


def post_input_grad(total, extras, outs):
    x_ref, g_middle_ref, norm_ref = extras
    grad_in_ref, g_norm_ref = outs
    x = x_ref[...].astype(F32)
    inv = lax.rsqrt(jnp.mean(x * x, axis=1, keepdims=True) + 1e-06)
    normed = x * inv
    prod = total * normed
    g_norm_ref[...] = jnp.sum(prod, axis=0, keepdims=True)
    scaled = total * norm_ref[...]
    mean = jnp.mean(prod * norm_ref[...], axis=1, keepdims=True)
    grad_in_ref[...] = (g_middle_ref[...] + inv * (scaled - normed * mean)).astype(BF)


def post_block_out(total, extras, outs):
    middle_ref, valid_ref = extras
    out_ref, stat_ref = outs
    mlp_part = valid_ref[...] * total
    result = middle_ref[...] + mlp_part
    out_ref[...] = result.astype(BF)
    stat_ref[0:1, :] = jnp.sum(valid_ref[...] * result * result, axis=0, keepdims=True)
    stat_ref[1:2, :] = jnp.sum(mlp_part * mlp_part, axis=0, keepdims=True)


def grids(t):
    rows = lax.broadcasted_iota(jnp.int32, (t, t), 0)
    cols = lax.broadcasted_iota(jnp.int32, (t, t), 1)
    return rows, cols


def allowed_of(seg_row, rows, cols):
    t = rows.shape[0]
    along = jnp.broadcast_to(seg_row, (t, t))
    return (along == jnp.transpose(along)) & (cols <= rows)


def build_bands(score_ref, bands, heads, taps, span, rows, cols):
    t = rows.shape[0]
    diff = cols - rows + (span - 1) // 2

    @pl.loop(0, heads)
    def _(h):
        for a in range(taps):
            band = jnp.zeros((t, t), F32)
            for b in range(span):
                band = jnp.where(diff == b, score_ref[h, a * span + b], band)
            bands[h, a * t : (a + 1) * t, :] = band.astype(BF)


def lagged(masked, taps, rows):
    parts = [masked.astype(BF)]
    for a in range(1, taps):
        parts.append(jnp.where(rows >= a, pltpu.roll(masked, a, 0), 0.0).astype(BF))
    return jnp.concatenate(parts, axis=1)


def attend_kernel(heads, hd, taps, span, score_ref, mix_ref, qkv_ref, seg_ref, gain_ref, head_in_ref, hat_ref, inv_ref, probs_ref, masked_ref, bands):
    t = qkv_ref.shape[1]
    width = heads * hd
    rows, cols = grids(t)

    @pl.when(pl.program_id(0) == 0)
    def _():
        build_bands(score_ref, bands, heads, taps, span, rows, cols)

    allowed = allowed_of(seg_ref[0, 0:1, :], rows, cols)
    for pair in range(heads // 2):
        probs = []
        for c in range(2):
            h = 2 * pair + c
            q = qkv_ref[0, :, h * hd : (h + 1) * hd]
            k = qkv_ref[0, :, width + h * hd : width + (h + 1) * hd]
            masked = jnp.where(allowed, dot(q, k, NT) * hd**-0.5, 0.0)
            masked_ref[0, h] = masked.astype(BF)
            conv = dot(lagged(masked, taps, rows), bands[h])
            logits = jnp.where(allowed, conv, -1e30)
            e = jnp.exp(logits - jnp.max(logits, axis=1, keepdims=True))
            p = e / jnp.sum(e, axis=1, keepdims=True)
            probs_ref[0, h] = p
            probs.append(p)
        for e in range(2):
            h = 2 * pair + e
            mixed = (mix_ref[h, 0] * probs[0] + mix_ref[h, 1] * probs[1]).astype(BF)
            v = qkv_ref[0, :, 2 * width + h * hd : 2 * width + (h + 1) * hd]
            out = dot(mixed, v)
            centred = out - jnp.mean(out, axis=1, keepdims=True)
            inv = lax.rsqrt(jnp.mean(centred * centred, axis=1, keepdims=True) + 1e-05)
            hat_ref[0, :, h * hd : (h + 1) * hd] = centred * inv
            inv_ref[0, :, h * hd : (h + 1) * hd] = jnp.broadcast_to(inv, (t, hd))
    head_in_ref[0] = (hat_ref[0] * gain_ref[...]).astype(BF)


def attend(score, mix, qkv, seg, gain, heads, hd, taps, span):
    n, t, _ = qkv.shape
    width = heads * hd

    def row(*shape):
        return pl.BlockSpec((1,) + shape, lambda i: (i,) + (0,) * len(shape))

    def out(dtype, *shape):
        return jax.ShapeDtypeStruct((n,) + shape, dtype)

    return pl.pallas_call(
        functools.partial(attend_kernel, heads, hd, taps, span),
        grid=(n,),
        out_shape=(out(BF, t, width), out(F32, t, width), out(F32, t, width), out(F32, heads, t, t), out(BF, heads, t, t)),
        in_specs=[smem_spec(), smem_spec(), row(t, 3 * width), row(8, t), pl.BlockSpec((1, width), lambda i: (0, 0))],
        out_specs=(row(t, width), row(t, width), row(t, width), row(heads, t, t), row(heads, t, t)),
        scratch_shapes=[pltpu.VMEM((heads, taps * t, t), BF)],
        compiler_params=pltpu.CompilerParams(vmem_limit_bytes=VMEM_LIMIT),
    )(score, mix, qkv, seg, gain)


def attend_back_kernel(heads, hd, taps, span, score_ref, mix_ref, qkv_ref, seg_ref, gain_ref, g_in_ref, hat_ref, inv_ref, probs_ref, masked_ref, g_qkv_ref, g_gain_ref, g_score_ref, g_mix_ref, bands, corr, g_wide):
    t = qkv_ref.shape[1]
    width = heads * hd
    rows, cols = grids(t)
    step = pl.program_id(0)

    @pl.when(step == 0)
    def _():
        build_bands(score_ref, bands, heads, taps, span, rows, cols)
        corr[...] = jnp.zeros_like(corr)
        g_gain_ref[...] = jnp.zeros_like(g_gain_ref)
        g_mix_ref[...] = jnp.zeros_like(g_mix_ref)

    allowed = allowed_of(seg_ref[0, 0:1, :], rows, cols)
    g_in = g_in_ref[0]
    g_gain_ref[...] += jnp.sum(g_in * hat_ref[0], axis=0, keepdims=True)
    g_wide[:, :width] = g_in * gain_ref[...]
    for pair in range(heads // 2):
        g_heads = []
        g_mixed = []
        probs = [probs_ref[0, 2 * pair + c] for c in range(2)]
        for e in range(2):
            h = 2 * pair + e
            scaled = g_wide[:, h * hd : (h + 1) * hd]
            hat = hat_ref[0, :, h * hd : (h + 1) * hd]
            inv = inv_ref[0, :, h * hd : (h + 1) * hd]
            g = inv * (scaled - jnp.mean(scaled, axis=1, keepdims=True) - hat * jnp.mean(scaled * hat, axis=1, keepdims=True))
            g = g.astype(BF)
            g_heads.append(g)
            v = qkv_ref[0, :, 2 * width + h * hd : 2 * width + (h + 1) * hd]
            g_mixed.append(dot(g, v, NT))
        for e in range(2):
            h = 2 * pair + e
            mixed = (mix_ref[h, 0] * probs[0] + mix_ref[h, 1] * probs[1]).astype(BF)
            g_wide[:, 2 * width + h * hd : 2 * width + (h + 1) * hd] = dot(mixed, g_heads[e], TN)
            for c in range(2):
                place = (2 * pair + e) * 2 + c
                g_mix_ref[place : place + 1, :] += jnp.sum(g_mixed[e] * probs[c], axis=0, keepdims=True)
        for c in range(2):
            h = 2 * pair + c
            g_probs = mix_ref[2 * pair, c] * g_mixed[0] + mix_ref[2 * pair + 1, c] * g_mixed[1]
            weighted = probs[c] * g_probs
            g_conv = weighted - probs[c] * jnp.sum(weighted, axis=1, keepdims=True)
            corr[h] += dot(lagged(masked_ref[0, h].astype(F32), taps, rows), g_conv.astype(BF), TN)
            parts = [g_conv.astype(BF)]
            for a in range(1, taps):
                parts.append(jnp.where(rows < t - a, pltpu.roll(g_conv, t - a, 0), 0.0).astype(BF))
            g_masked = jnp.zeros((t, t), F32)
            for a in range(taps):
                g_masked += dot(parts[a], bands[h, a * t : (a + 1) * t, :], NT)
            g_raw = jnp.where(allowed, g_masked, 0.0).astype(BF)
            q = qkv_ref[0, :, h * hd : (h + 1) * hd]
            k = qkv_ref[0, :, width + h * hd : width + (h + 1) * hd]
            g_k = dot(g_raw, q, TN) * hd**-0.5
            g_wide[:, width + h * hd : width + (h + 1) * hd] = g_k
            g_q = dot(g_raw, k) * hd**-0.5
            g_qkv_ref[0, :, h * hd : (h + 1) * hd] = g_q.astype(BF)
    g_qkv_ref[0, :, width:] = g_wide[:, width:].astype(BF)

    @pl.when(step == pl.num_programs(0) - 1)
    def _():
        diff = cols - rows + (span - 1) // 2

        @pl.loop(0, heads)
        def _(h):
            for a in range(taps):
                tile = corr[h, a * t : (a + 1) * t, :]
                for b in range(span):
                    g_score_ref[h, a * span + b : a * span + b + 1, :] = jnp.sum(
                        jnp.where(diff == b, tile, 0.0), axis=0, keepdims=True
                    )


def attend_back(score, mix, qkv, seg, gain, g_in, hat, inv, probs, masked, heads, hd, taps, span):
    n, t, _ = qkv.shape
    width = heads * hd
    lines = -(-taps * span // 8) * 8

    def row(*shape):
        return pl.BlockSpec((1,) + shape, lambda i: (i,) + (0,) * len(shape))

    def whole(*shape):
        return pl.BlockSpec(shape, lambda i: (0,) * len(shape))

    return pl.pallas_call(
        functools.partial(attend_back_kernel, heads, hd, taps, span),
        grid=(n,),
        out_shape=(
            jax.ShapeDtypeStruct((n, t, 3 * width), BF),
            jax.ShapeDtypeStruct((1, width), F32),
            jax.ShapeDtypeStruct((heads, lines, t), F32),
            jax.ShapeDtypeStruct((2 * heads, t), F32),
        ),
        in_specs=[
            smem_spec(),
            smem_spec(),
            row(t, 3 * width),
            row(8, t),
            whole(1, width),
            row(t, width),
            row(t, width),
            row(t, width),
            row(heads, t, t),
            row(heads, t, t),
        ],
        out_specs=(row(t, 3 * width), whole(1, width), whole(heads, lines, t), whole(2 * heads, t)),
        scratch_shapes=[
            pltpu.VMEM((heads, taps * t, t), BF),
            pltpu.VMEM((heads, taps * t, t), F32),
            pltpu.VMEM((t, 3 * width), F32),
        ],
        compiler_params=pltpu.CompilerParams(vmem_limit_bytes=VMEM_LIMIT),
    )(score, mix, qkv, seg, gain, g_in, hat, inv, probs, masked)


def per_device(
    hidden_in,
    doc_lengths,
    w_query,
    w_key,
    w_value,
    w_output,
    w_gate,
    w_up,
    w_down,
    attn_norm,
    mlp_norm,
    head_norm,
    score_kernel,
    head_mixing,
    grad_out,
):
    _, t, d = hidden_in.shape
    reps = lax.axis_size("rep")
    shards = lax.axis_size("fsdp")
    me = lax.axis_index("rep")
    hidden = w_gate.shape[1]
    heads = H // reps
    hd = d // H
    quarter = d // reps
    units = hidden // reps
    strip = units // shards
    taps, span = score_kernel.shape[1:]
    docs = doc_lengths.shape[1] - 1
    shape_of = jax.ShapeDtypeStruct

    def mine(array, size, axis):
        return lax.dynamic_slice_in_dim(array, me * size, size, axis)

    first_shard = jnp.concatenate([mine(w, quarter, 1) for w in (w_query, w_key, w_value, w_output)], axis=1)
    rows_here = w_gate.shape[0]

    def strips(w):
        return mine(w.reshape(rows_here, shards, reps, strip), 1, 2).reshape(rows_here, units)

    mlp_shard = jnp.concatenate([strips(w_gate), strips(w_up)], axis=1)
    down_shard = mine(w_down, strip, 0)
    w_first = lax.all_gather(first_shard, "fsdp", axis=0, tiled=True)
    w_mlp = lax.all_gather(mlp_shard, "fsdp", axis=0, tiled=True)
    w_dn = lax.all_gather(down_shard, "fsdp", axis=0, tiled=True)

    boundary = jnp.cumsum(doc_lengths[:, :-1], axis=1)
    places = jnp.arange(t, dtype=jnp.int32)
    seg_ids = jnp.sum((places[None, :, None] >= boundary[:, None, :]).astype(jnp.int32), axis=2)
    seg_own = jnp.broadcast_to(seg_ids.astype(F32), (8, t))
    valid = (seg_ids < docs).astype(F32).reshape(t, 1)
    x = hidden_in.reshape(t, d)
    g_out = grad_out.reshape(t, d)
    gain_first, gain_second = attn_norm.reshape(1, d), mlp_norm.reshape(1, d)
    gain_head = mine(head_norm, quarter, 0).reshape(1, quarter)
    score = mine(score_kernel.reshape(H, taps * span), heads, 0)
    mix = mine(head_mixing, heads, 0)

    attn_in, g_mlp, seg = gather_inputs(x, g_out, seg_own, gain_first)
    tokens = reps * t
    flat = lambda a: a.reshape(tokens, a.shape[-1])
    stacked = lambda a: a.reshape(reps, t, a.shape[-1])

    qkv = dot(flat(attn_in), w_first[:, : 3 * quarter]).astype(BF)
    head_in, hat, inv, probs, masked = attend(score, mix, stacked(qkv), seg, gain_head, heads, hd, taps, span)
    w_out_cols = w_first[:, 3 * quarter :].reshape(reps, quarter, quarter)
    w_out = lax.all_to_all(w_out_cols, "rep", 0, 0, tiled=True)
    w_out = jnp.moveaxis(w_out, 0, 1).reshape(quarter, d)

    mlp_in, middle, stat_attn = exchange(
        2, head_in, w_out, NN, (x, valid, gain_second), post_attn_out, True,
        (shape_of((t, d), F32), shape_of((1, d), F32)),
    )
    gate_up = dot(flat(mlp_in), w_mlp)
    gate, upper = gate_up[:, :units], gate_up[:, units:]
    sig = jax.nn.sigmoid(gate)
    silu = gate * sig
    hidden_act = (silu * upper).astype(BF)
    d_down = dot(hidden_act, flat(g_mlp), TN).astype(BF)
    s_down = lax.psum_scatter(d_down, "fsdp", scatter_dimension=0, tiled=True)
    g_hidden = dot(flat(g_mlp), w_dn, NT)
    g_gate = g_hidden * upper * sig * (1.0 + gate * (1.0 - sig))
    g_upper = g_hidden * silu
    g_gu = jnp.concatenate([g_gate, g_upper], axis=1).astype(BF)
    d_mlp = dot(flat(mlp_in), g_gu, TN).astype(BF)
    s_mlp = lax.psum_scatter(d_mlp, "fsdp", scatter_dimension=0, tiled=True)

    g_attn, g_middle, g_second = exchange(
        3, stacked(g_gu), w_mlp, NT, (middle, g_out, valid, gain_second), post_mlp_grad, True,
        (shape_of((t, d), F32), shape_of((1, d), F32)),
    )
    g_head_in = dot(flat(g_attn), w_out, NT)
    g_qkv, g_gain, g_score, g_mix = attend_back(
        score, mix, stacked(qkv), seg, gain_head, stacked(g_head_in), hat, inv, probs, masked, heads, hd, taps, span
    )
    d_out_rows = dot(flat(head_in), flat(g_attn), TN).astype(BF)
    d_out = lax.all_to_all(
        jnp.moveaxis(d_out_rows.reshape(quarter, reps, quarter), 1, 0), "rep", 0, 0, tiled=True
    ).reshape(d, quarter)
    d_qkv = dot(flat(attn_in), flat(g_qkv), TN).astype(BF)
    s_first = lax.psum_scatter(jnp.concatenate([d_qkv, d_out], axis=1), "fsdp", scatter_dimension=0, tiled=True)

    grad_in, g_first = exchange(
        4, g_qkv, w_first[:, : 3 * quarter], NT, (x, g_middle, gain_first), post_input_grad, False,
        (shape_of((t, d), BF), shape_of((1, d), F32)),
    )
    block_out, stat_out = exchange(
        5, stacked(hidden_act), w_dn, NN, (middle, valid), post_block_out, False,
        (shape_of((t, d), BF), shape_of((8, d), F32)),
    )

    spread = lambda a: lax.dynamic_update_slice_in_dim(
        jnp.zeros((reps * a.shape[0],), F32), a, me * a.shape[0], 0
    )
    packed = jnp.concatenate(
        [
            g_first[0],
            g_second[0],
            spread(g_gain[0]),
            spread(jnp.sum(g_score[:, : taps * span], axis=2).reshape(-1)),
            spread(jnp.sum(g_mix, axis=1)),
            jnp.stack([jnp.sum(stat_out[0]), jnp.sum(stat_attn), jnp.sum(stat_out[1]), jnp.sum(valid)]),
        ]
    )
    packed = lax.psum(packed, ("rep", "fsdp"))
    ends = [d, 2 * d, 3 * d, 3 * d + H * taps * span, 3 * d + H * taps * span + 2 * H]
    small_first, small_second, small_head, small_score, small_mix, stats = jnp.split(packed, ends)
    root_means = jnp.sqrt(stats[:3] / (stats[3] * d))

    a_first, a_mlp, a_down = gather_grads(s_first, s_mlp, s_down)
    first = a_first.astype(F32).reshape(reps, rows_here, 4, quarter)
    first = jnp.moveaxis(first, 0, 2).reshape(rows_here, 4, d)
    mlp = a_mlp.astype(F32).reshape(reps, rows_here, 2, shards, strip)
    mlp = jnp.moveaxis(mlp, 0, 3).reshape(rows_here, 2, hidden)
    down = a_down.astype(F32).reshape(w_down.shape)
    return (
        block_out.reshape(hidden_in.shape),
        grad_in.reshape(hidden_in.shape),
        first[:, 0],
        first[:, 1],
        first[:, 2],
        first[:, 3],
        mlp[:, 0],
        mlp[:, 1],
        down,
        small_first,
        small_second,
        small_head,
        small_score.reshape(score_kernel.shape),
        small_mix.reshape(head_mixing.shape),
        root_means,
    )


def solution(mesh):
    rows = P(("rep", "fsdp"), None, None)
    split = P("fsdp", None)
    placed = (rows, P(("rep", "fsdp"), None)) + (split,) * 7 + (P(),) * 5 + (rows,)
    return jax.shard_map(
        per_device,
        mesh=mesh,
        in_specs=placed,
        out_specs=(rows, rows) + (split,) * 7 + (P(),) * 6,
        check_vma=False,
    )
```

```python
import functools

import jax
import jax.numpy as jnp
from jax import lax
from jax.experimental import pallas as pl
from jax.experimental.pallas import tpu as pltpu
from jax.sharding import PartitionSpec as P

H = 16
BF = jnp.bfloat16
F32 = jnp.float32
MESH = pl.DeviceIdType.MESH
VMEM_LIMIT = 61 * 1024 * 1024
NN = (((1,), (0,)), ((), ()))
NT = (((1,), (1,)), ((), ()))
TN = (((0,), (0,)), ((), ()))
FIRST, MLP, DOWN = 0, 1, 2
UP, DN, SIDE = 0, 1, 2
STATS = 4


def dot(a, b, dims=NN):
    return lax.dot_general(a, b, dims, preferred_element_type=F32)


def merge(value):
    n, rows, width = value.shape
    if rows % 16 == 0:
        return value.reshape(n * rows, width)
    return value.astype(F32).reshape(n * rows, width).astype(value.dtype)


def vmem_spec():
    return pl.BlockSpec(memory_space=pltpu.VMEM)


def smem_spec():
    return pl.BlockSpec(memory_space=pltpu.SMEM)


def hbm_spec():
    return pl.BlockSpec(memory_space=pl.ANY)


def grids(t):
    rows = lax.broadcasted_iota(jnp.int32, (t, t), 0)
    cols = lax.broadcasted_iota(jnp.int32, (t, t), 1)
    return rows, cols


def allowed_of(seg_row, rows, cols):
    t = rows.shape[0]
    along = jnp.broadcast_to(seg_row, (t, t))
    return (along == jnp.transpose(along)) & (cols <= rows)


def lagged(masked, taps, rows):
    parts = [masked.astype(BF)]
    for a in range(1, taps):
        parts.append(jnp.where(rows >= a, pltpu.roll(masked, a, 0), 0.0).astype(BF))
    return jnp.concatenate(parts, axis=1)


def row_sum(value):
    return jnp.sum(value, axis=0, keepdims=True)


def mean_of(value):
    return jnp.mean(value, axis=1, keepdims=True)


def layer_kernel(cfg, *refs):
    heads, hd, taps, span, docs, shards, units = cfg
    (
        x_ref, g_ref, seg_ref, valid_ref, gain_first, gain_second, gain_head, score_ref, mix_ref,
        own_first, own_mlp, own_down,
        out_ref, grad_in_ref, small_ref, all_first, all_mlp, all_down,
        land_first, land_mlp, land_down,
        w_first, w_mlp, w_down, wide, g_mlp, seg_all, attn_in, qkv, hat, inv, probs, masked, head_in, w_out,
        middle, slope, silu, hidden, g_gu, g_attn, g_middle, g_qkv, g_hin, d_out, d_out_in,
        psend, pown, r1, ysend, r2, psend2, pown2, r1b, r2b, bands, corr, g_wide, lanes, g_mix,
        stage, small_send, small_recv,
        ag_send, ag_recv, rs_send, rs_recv, rep_send, rep_recv, local,
    ) = refs
    t, d = x_ref.shape
    width = heads * hd
    quarter = d // 4
    lines = shards // 2
    me = lax.axis_index("rep")
    f = lax.axis_index("fsdp")
    plane, core = me // 2, me % 2
    sibling, across = plane * 2 + (1 - core), (1 - plane) * 2 + core
    diagonal = (1 - plane) * 2 + (1 - core)
    z, side = f // 2, f % 2
    partner = 2 * z + (1 - side)
    weights = (w_first, w_mlp, w_down)
    lands = (land_first, land_mlp, land_down)
    peer_of = (f + 2, f - 2, partner)
    tokens = 4 * t
    part = shards // 4
    rows, cols = grids(t)

    def flip(bit):
        return f + (1 - 2 * ((f // bit) % 2)) * bit

    bits = []
    bit = 1
    while bit < shards:
        bits.append(bit)
        bit *= 2

    barrier = pltpu.get_barrier_semaphore()

    def greet(r, s):
        pl.semaphore_signal(barrier, inc=1, device_id=(r, s), device_id_type=MESH)

    for r in (sibling, across, diagonal):
        greet(r, f)
    for bit in bits:
        greet(me, flip(bit))

    @pl.when(z < lines - 1)
    def _():
        greet(me, f + 2)

    @pl.when(z > 0)
    def _():
        greet(me, f - 2)

    ends = (z > 0).astype(jnp.int32) + (z < lines - 1).astype(jnp.int32)
    pl.semaphore_wait(barrier, 3 + len(bits) + ends)

    def rep_copy(src, dst, slot, peer):
        return pltpu.make_async_remote_copy(
            src_ref=src, dst_ref=dst, send_sem=rep_send.at[slot], recv_sem=rep_recv.at[slot],
            device_id=(peer, f), device_id_type=MESH,
        )

    def ag(k, block, way):
        return pltpu.make_async_remote_copy(
            src_ref=weights[k].at[block], dst_ref=weights[k].at[block],
            send_sem=ag_send.at[k, way, block], recv_sem=ag_recv.at[k, block],
            device_id=(me, peer_of[way]), device_id_type=MESH,
        )

    def ag_walk(k, s, first, act):
        sides = (side, 1 - side) if k == DOWN else (side,)
        if isinstance(s, int) and s == 0:
            for q in sides:
                block = 2 * z + q
                if k == DOWN and q is not side:
                    first(k, block)

                @pl.when(z < lines - 1)
                def _():
                    act(k, block, UP)

                @pl.when(z > 0)
                def _():
                    act(k, block, DN)

                if k != DOWN:
                    act(k, block, SIDE)
            return

        @pl.when(z - s >= 0)
        def _():
            for q in sides:
                block = 2 * (z - s) + q
                first(k, block)

                @pl.when(z < lines - 1)
                def _():
                    act(k, block, UP)

                if k != DOWN:
                    act(k, block, SIDE)

        @pl.when(z + s < lines)
        def _():
            for q in sides:
                block = 2 * (z + s) + q
                first(k, block)

                @pl.when(z > 0)
                def _():
                    act(k, block, DN)

                if k != DOWN:
                    act(k, block, SIDE)

    def arrived(k, block):
        ag(k, block, SIDE).wait_recv()

    def go(k, block, way):
        ag(k, block, way).start()

    def gone(k, block, way):
        ag(k, block, way).wait_send()

    def ag_steps(k, low, high):
        if low == 0:
            ag_walk(k, 0, arrived, go)
        else:
            pl.loop(low, high)(lambda s: ag_walk(k, s, arrived, go))

    def ag_done(k):
        if k != DOWN:
            pl.loop(0, lines)(lambda zz: arrived(k, 2 * zz + (1 - side)))

    def ag_drain(k):
        nothing = lambda *_: None
        if k == DOWN:
            gone(k, f, SIDE)
        ag_walk(k, 0, nothing, gone)
        pl.loop(1, lines)(lambda s: ag_walk(k, s, nothing, gone))

    def gather_start(fulls, slot):
        for i, full in enumerate(fulls):
            rep_copy(full.at[me], full.at[me], slot + 3 * i, across).start()
            rep_copy(full.at[me], full.at[me], slot + 3 * i + 1, sibling).start()

    def gather_pass(fulls, slot):
        for i, full in enumerate(fulls):
            rep_copy(full.at[me], full.at[me], slot + 3 * i, across).wait_recv()
            rep_copy(full.at[across], full.at[across], slot + 3 * i + 2, sibling).start()

    def gather_end(fulls, slot):
        for i, full in enumerate(fulls):
            rep_copy(full.at[me], full.at[me], slot + 3 * i + 1, sibling).wait_recv()
            rep_copy(full.at[across], full.at[across], slot + 3 * i + 2, sibling).wait_recv()
        for i, full in enumerate(fulls):
            rep_copy(full.at[me], full.at[me], slot + 3 * i, across).wait_send()
            rep_copy(full.at[me], full.at[me], slot + 3 * i + 1, sibling).wait_send()
            rep_copy(full.at[across], full.at[across], slot + 3 * i + 2, sibling).wait_send()

    def pair_of(ref, a, b):
        return jnp.concatenate([ref[a], ref[b]], axis=0)

    def sum_copies(slot, send_buf, first_land, second_land):
        return (
            rep_copy(send_buf, first_land, slot, sibling),
            rep_copy(ysend, second_land, slot + 1, across),
        )

    def column_chunk(i):
        return pl.ds(pl.multiple_of(i * quarter, quarter), quarter)

    def sum_theirs(product, copies, send_buf):
        @pl.loop(0, 4)
        def _(i):
            value = product(1 - core, 2 + (1 - core), i)
            send_buf[0, :, column_chunk(i)] = value[:t].astype(BF)
            send_buf[1, :, column_chunk(i)] = value[t:].astype(BF)

        copies[0].start()

    def sum_ours(product, own_buf):
        @pl.loop(0, 4)
        def _(i):
            value = product(across, me, i)
            own_buf[0, :, column_chunk(i)] = value[:t]
            own_buf[1, :, column_chunk(i)] = value[t:]

    def sum_turn(copies, own_buf, first_land):
        copies[0].wait_recv()
        ysend[...] = (own_buf[0] + first_land[1 - plane].astype(F32)).astype(BF)
        copies[1].start()
        own_buf[1] = own_buf[1] + first_land[plane].astype(F32)

    def sum_end(copies, own_buf, second_land):
        copies[1].wait_recv()
        total = own_buf[1] + second_land[...].astype(F32)
        copies[0].wait_send()
        copies[1].wait_send()
        return total

    def rs(k, block, way):
        return pltpu.make_async_remote_copy(
            src_ref=weights[k].at[block], dst_ref=lands[k].at[way, block],
            send_sem=rs_send.at[k, way, block], recv_sem=rs_recv.at[k, way, block],
            device_id=(me, peer_of[way]), device_id_type=MESH,
        )

    def rs_add(k, block, way):
        grad = weights[k]
        high, wide_k = grad.shape[1:]
        rs(k, block, way).wait_recv()
        slot = stage.at[pl.ds(0, high), pl.ds(0, wide_k)]
        copy = pltpu.make_async_copy(lands[k].at[way, block], slot, local.at[0])
        copy.start()
        copy.wait()
        step = 16 if high % 16 == 0 else high

        @pl.loop(0, high // step)
        def _(i):
            at = pl.ds(pl.multiple_of(i * step, step), step)
            total = grad[block, at, :].astype(F32) + stage[at, 0:wide_k].astype(F32)
            grad[block, at, :] = total.astype(BF)

    def rs_turn(k, j):
        sides = (side, 1 - side) if k == DOWN else (side,)
        high_target, low_target = lines - 1 - j, j

        @pl.when(high_target > z)
        def _():
            for q in sides:
                block = 2 * high_target + q
                if k != DOWN:
                    rs_add(k, block, SIDE)

                @pl.when(z > 0)
                def _():
                    rs_add(k, block, UP)

                rs(k, block, UP).start()

        @pl.when(low_target < z)
        def _():
            for q in sides:
                block = 2 * low_target + q
                if k != DOWN:
                    rs_add(k, block, SIDE)

                @pl.when(z < lines - 1)
                def _():
                    rs_add(k, block, DN)

                rs(k, block, DN).start()

    def rs_close(k):
        sides = (1 - side, side) if k == DOWN else (side,)
        for q in sides:
            block = 2 * z + q
            if k != DOWN:
                rs_add(k, block, SIDE)

            @pl.when(z > 0)
            def _():
                rs_add(k, block, UP)

            @pl.when(z < lines - 1)
            def _():
                rs_add(k, block, DN)

            if k == DOWN and q is not side:
                rs(k, block, SIDE).start()
        if k == DOWN:
            rs_add(k, f, SIDE)

    def rs_drain(k):
        sides = (side, 1 - side) if k == DOWN else (side,)

        @pl.loop(0, lines)
        def _(zz):
            @pl.when(zz > z)
            def _():
                for q in sides:
                    rs(k, 2 * zz + q, UP).wait_send()

            @pl.when(zz < z)
            def _():
                for q in sides:
                    rs(k, 2 * zz + q, DN).wait_send()

            if k != DOWN:
                rs(k, 2 * zz + (1 - side), SIDE).wait_send()

        if k == DOWN:
            rs(k, partner, SIDE).wait_send()

    outs = (all_first, all_mlp, all_down)

    def final_copies(k, slot):
        own = weights[k].at[f]
        full = outs[k]
        return (
            rep_copy(own, full.at[me], slot, across),
            rep_copy(own, full.at[me], slot + 1, sibling),
            rep_copy(full.at[across], full.at[across], slot + 2, sibling),
            pltpu.make_async_copy(own, full.at[me], local.at[1 + k]),
        )

    def final_start(k, slot):
        a, b, _, here = final_copies(k, slot)
        a.start()
        b.start()
        here.start()

    def final_pass(k, slot):
        a, _, c, _ = final_copies(k, slot)
        a.wait_recv()
        c.start()

    def final_end(k, slot):
        a, b, c, here = final_copies(k, slot)
        b.wait_recv()
        c.wait_recv()
        a.wait_send()
        b.wait_send()
        c.wait_send()
        here.wait()

    owns = (own_first, own_mlp, own_down)
    loads = [pltpu.make_async_copy(owns[k], weights[k].at[f], local.at[4 + k]) for k in range(3)]
    for load in loads:
        load.start()
    wide[me] = x_ref[...]
    g_mlp[me] = g_ref[...]
    seg_all[me] = seg_ref[...]
    entering = (seg_all, wide, g_mlp)
    gather_start(entering, 0)
    loads[FIRST].wait()
    ag_steps(FIRST, 0, 1)

    diff = cols - rows + (span - 1) // 2

    @pl.loop(0, heads)
    def _(h):
        for a in range(taps):
            band = jnp.zeros((t, t), F32)
            for b in range(span):
                band = jnp.where(diff == b, score_ref[h, a * span + b], band)
            bands[h, a * t : (a + 1) * t, :] = band.astype(BF)

    gather_pass(entering, 0)
    ag_steps(FIRST, 1, 2)
    gather_end(entering, 0)

    @pl.loop(0, 4)
    def _(r):
        value = wide[r].astype(F32)
        scale = lax.rsqrt(mean_of(value * value) + 1e-06)
        attn_in[r] = (value * scale * gain_first[...]).astype(BF)
        valid = jnp.transpose(jnp.broadcast_to(seg_all[r][0:1, :], (t, t)))[:, 0:1] < float(docs)
        g_mlp[r] = jnp.where(valid, g_mlp[r].astype(F32), 0.0).astype(BF)

    ag_steps(FIRST, 2, 3)
    loads[MLP].wait()
    loads[DOWN].wait()
    ag_steps(MLP, 0, 1)
    ag_steps(FIRST, 3, lines)
    ag_done(FIRST)

    def w_out_copy(peer, slot):
        return rep_copy(
            w_first.at[pl.ds(peer * part, part), :, pl.ds(3 * quarter, quarter)],
            w_out.at[:, :, pl.ds(pl.multiple_of(me * quarter, quarter), quarter)],
            slot, peer,
        )

    for i, peer in enumerate((sibling, across, diagonal)):
        w_out_copy(peer, 9 + i).start()
    own_out = pltpu.make_async_copy(
        w_first.at[pl.ds(me * part, part), :, pl.ds(3 * quarter, quarter)],
        w_out.at[:, :, pl.ds(pl.multiple_of(me * quarter, quarter), quarter)],
        local.at[0],
    )
    own_out.start()

    for i in range(3):
        value = dot(attn_in[...].reshape(tokens, d), merge(w_first[:, :, i * quarter : (i + 1) * quarter]))
        qkv[:, :, i * quarter : (i + 1) * quarter] = value.astype(BF).reshape(4, t, quarter)
    ag_steps(MLP, 1, 2)

    def split(ref, row, kind, h):
        return ref[row, :, kind * width + h * hd : kind * width + (h + 1) * hd]

    @pl.loop(0, 4)
    def _(row):
        allowed = allowed_of(seg_all[row][0:1, :], rows, cols)
        for pair in range(heads // 2):
            both = []
            for c in range(2):
                h = 2 * pair + c
                scores = dot(split(qkv, row, 0, h), split(qkv, row, 1, h), NT) * hd**-0.5
                kept = jnp.where(allowed, scores, 0.0)
                masked[row, h] = kept.astype(BF)
                logits = jnp.where(allowed, dot(lagged(kept, taps, rows), bands[h]), -1e30)
                e = jnp.exp(logits - jnp.max(logits, axis=1, keepdims=True))
                p = e / jnp.sum(e, axis=1, keepdims=True)
                probs[row, h] = p
                both.append(p)
            for e in range(2):
                h = 2 * pair + e
                mixed = (mix_ref[h, 0] * both[0] + mix_ref[h, 1] * both[1]).astype(BF)
                out = dot(mixed, split(qkv, row, 2, h))
                centred = out - mean_of(out)
                scale = lax.rsqrt(mean_of(centred * centred) + 1e-05)
                hat[row, :, h * hd : (h + 1) * hd] = centred * scale
                inv[row, :, h * hd : (h + 1) * hd] = jnp.broadcast_to(scale, (t, hd))
        head_in[row] = (hat[row] * gain_head[...]).astype(BF)

    for i, peer in enumerate((sibling, across, diagonal)):
        w_out_copy(peer, 9 + i).wait_recv()
    own_out.wait()

    copies = sum_copies(12, psend, r1, r2)
    product = lambda a, b, i: dot(pair_of(head_in, a, b), merge(w_out[:, :, column_chunk(i)]))
    sum_theirs(product, copies, psend)
    sum_ours(product, pown)
    ag_steps(MLP, 2, 3)
    sum_turn(copies, pown, r1)
    ag(DOWN, f, SIDE).start()
    total = sum_end(copies, pown, r2)
    attn_part = valid_ref[...] * total
    value = x_ref[...].astype(F32) + attn_part
    middle[...] = value
    stat_attn = jnp.sum(row_sum(attn_part * attn_part), axis=1, keepdims=True)
    scale = lax.rsqrt(mean_of(value * value) + 1e-06)
    wide[me] = (value * scale * gain_second[...]).astype(BF)
    gather_start((wide,), 14)
    ag_steps(MLP, 3, lines)
    gather_pass((wide,), 14)
    ag_steps(DOWN, 0, 1)
    gather_end((wide,), 14)
    mlp_in = wide
    ag_steps(DOWN, 1, 2)
    ag_done(MLP)

    chunk = 256

    @pl.loop(0, units // chunk)
    def _(i):
        at = pl.ds(pl.multiple_of(i * chunk, chunk), chunk)
        after = pl.ds(pl.multiple_of(units + i * chunk, chunk), chunk)
        operand = mlp_in[...].reshape(tokens, d)
        gate = dot(operand, merge(w_mlp[:, :, at]))
        upper = dot(operand, merge(w_mlp[:, :, after]))
        sig = 1.0 / (1.0 + jnp.exp(-gate))
        act = gate * sig
        hidden[:, :, at] = (act * upper).astype(BF).reshape(4, t, chunk)
        silu[:, at] = act
        slope[:, at] = upper * sig * (1.0 + gate * (1.0 - sig))

    ag_steps(DOWN, 2, 3)
    ag_steps(DOWN, 3, lines)

    @pl.loop(0, 4)
    def _(i):
        span_units = units // 4
        at = pl.ds(pl.multiple_of(i * span_units, span_units), span_units)
        after = pl.ds(pl.multiple_of(units + i * span_units, span_units), span_units)
        g_hidden = dot(g_mlp[...].reshape(tokens, d), merge(w_down[pl.ds(i * part, part)]), NT)
        g_gu[:, :, at] = (g_hidden * slope[:, at]).astype(BF).reshape(4, t, span_units)
        g_gu[:, :, after] = (g_hidden * silu[:, at]).astype(BF).reshape(4, t, span_units)

    mlp_copies = sum_copies(17, psend, r1, r2)
    product = lambda a, b, i: dot(pair_of(g_gu, a, b), merge(w_mlp[pl.ds(i * part, part)]), NT)
    sum_theirs(product, mlp_copies, psend)
    sum_ours(product, pown)

    out_copies = (rep_copy(psend2, r1b, 19, sibling), rep_copy(ysend, r2b, 20, across))
    product = lambda a, b, i: dot(pair_of(hidden, a, b), merge(w_down[:, :, column_chunk(i)]))
    sum_theirs(product, out_copies, psend2)
    sum_ours(product, pown2)
    sum_turn(mlp_copies, pown, r1)

    ag_drain(DOWN)

    @pl.loop(0, 4)
    def _(i):
        span_units = units // 4
        at = pl.ds(pl.multiple_of(i * span_units, span_units), span_units)
        value = dot(hidden[:, :, at].reshape(tokens, span_units), g_mlp[...].reshape(tokens, d), TN)
        w_down[pl.ds(i * part, part)] = value.reshape(part, w_down.shape[1], d).astype(BF)

    def early(k):
        @pl.when(z == 0)
        def _():
            @pl.loop(0, lines - 1)
            def _(j):
                for q in (side, 1 - side):
                    rs(k, 2 * (lines - 1 - j) + q, UP).start()

        @pl.when(z == lines - 1)
        def _():
            @pl.loop(0, lines - 1)
            def _(j):
                for q in (side, 1 - side):
                    rs(k, 2 * j + q, DN).start()

    early(DOWN)
    inner = (z > 0) & (z < lines - 1)

    def down_turn(j):
        @pl.when(inner)
        def _():
            rs_turn(DOWN, j)

    total = sum_end(mlp_copies, pown, r2)
    value = middle[...]
    scale = lax.rsqrt(mean_of(value * value) + 1e-06)
    normed = value * scale
    prod = total * normed
    g_second = row_sum(prod)
    mean = mean_of(prod * gain_second[...])
    value = g_ref[...].astype(F32) + scale * (total * gain_second[...] - normed * mean)
    g_middle[...] = value
    g_attn[me] = (valid_ref[...] * value).astype(BF)
    gather_start((g_attn,), 21)
    ag_drain(MLP)

    def farthest(i):
        return (1 - i % 2) * (3 - i // 2) + (i % 2) * (i // 2)

    def send_side(k, p):
        @pl.loop(0, part // 2)
        def _(j):
            zz = p * (part // 2) + j
            rs(k, 2 * zz + (1 - side), SIDE).start()

    @pl.loop(0, 4)
    def _(i):
        p = farthest(i)
        at = pl.ds(pl.multiple_of(p * quarter, quarter), quarter)
        value = dot(mlp_in[:, :, at].reshape(tokens, quarter), g_gu[...].reshape(tokens, 2 * units), TN)
        w_mlp[pl.ds(p * part, part)] = value.reshape(part, w_mlp.shape[1], 2 * units).astype(BF)
        send_side(MLP, p)

    gather_pass((g_attn,), 21)
    gather_end((g_attn,), 21)

    value = dot(g_attn[...].reshape(tokens, d), merge(w_out[...]), NT)
    g_hin[...] = value.reshape(4, t, width)
    value = dot(head_in[...].reshape(tokens, width), g_attn[...].reshape(tokens, d), TN)
    d_out[...] = value.reshape(part, w_first.shape[1], d).astype(BF)

    def d_out_copy(peer, slot):
        return rep_copy(
            d_out.at[:, :, pl.ds(pl.multiple_of(peer * quarter, quarter), quarter)],
            d_out_in.at[pl.ds(me * part, part)],
            slot, peer,
        )

    for i, peer in enumerate((sibling, across, diagonal)):
        d_out_copy(peer, 24 + i).start()
    own_d_out = pltpu.make_async_copy(
        d_out.at[:, :, pl.ds(pl.multiple_of(me * quarter, quarter), quarter)],
        d_out_in.at[pl.ds(me * part, part)], local.at[7],
    )
    own_d_out.start()
    down_turn(0)

    corr[...] = jnp.zeros_like(corr)
    g_mix[...] = jnp.zeros_like(g_mix)
    lanes[...] = jnp.zeros_like(lanes)

    @pl.loop(0, 4)
    def _(row):
        allowed = allowed_of(seg_all[row][0:1, :], rows, cols)
        g_wide[...] = g_hin[row] * gain_head[...]
        for pair in range(heads // 2):
            g_heads, g_mixed = [], []
            both = [probs[row, 2 * pair + c] for c in range(2)]
            for e in range(2):
                h = 2 * pair + e
                scaled = g_wide[:, h * hd : (h + 1) * hd]
                own_hat = hat[row, :, h * hd : (h + 1) * hd]
                g = inv[row, :, h * hd : (h + 1) * hd] * (scaled - mean_of(scaled) - own_hat * mean_of(scaled * own_hat))
                g = g.astype(BF)
                g_heads.append(g)
                g_mixed.append(dot(g, split(qkv, row, 2, h), NT))
            for e in range(2):
                h = 2 * pair + e
                mixed = (mix_ref[h, 0] * both[0] + mix_ref[h, 1] * both[1]).astype(BF)
                g_v = dot(mixed, g_heads[e], TN)
                g_qkv[row, :, 2 * width + h * hd : 2 * width + (h + 1) * hd] = g_v.astype(BF)
                for c in range(2):
                    place = (2 * pair + e) * 2 + c
                    g_mix[place : place + 1, :] += row_sum(g_mixed[e] * both[c])
            for c in range(2):
                h = 2 * pair + c
                g_probs = mix_ref[2 * pair, c] * g_mixed[0] + mix_ref[2 * pair + 1, c] * g_mixed[1]
                weighted = both[c] * g_probs
                g_conv = weighted - both[c] * jnp.sum(weighted, axis=1, keepdims=True)
                corr[h] += dot(lagged(masked[row, h].astype(F32), taps, rows), g_conv.astype(BF), TN)
                g_kept = dot(g_conv.astype(BF), bands[h, 0:t, :], NT)
                for a in range(1, taps):
                    lead = jnp.where(rows < t - a, pltpu.roll(g_conv, t - a, 0), 0.0).astype(BF)
                    g_kept += dot(lead, bands[h, a * t : (a + 1) * t, :], NT)
                g_raw = jnp.where(allowed, g_kept, 0.0).astype(BF)
                g_q = dot(g_raw, split(qkv, row, 1, h)) * hd**-0.5
                g_k = dot(g_raw, split(qkv, row, 0, h), TN) * hd**-0.5
                g_qkv[row, :, h * hd : (h + 1) * hd] = g_q.astype(BF)
                g_qkv[row, :, width + h * hd : width + (h + 1) * hd] = g_k.astype(BF)

    down_turn(1)
    in_copies = sum_copies(27, psend, r1, r2)
    product = lambda a, b, i: dot(pair_of(g_qkv, a, b), merge(w_first[pl.ds(i * part, part), :, 0 : 3 * quarter]), NT)
    sum_theirs(product, in_copies, psend)
    sum_ours(product, pown)
    sum_turn(in_copies, pown, r1)

    ag_drain(FIRST)
    for i, peer in enumerate((sibling, across, diagonal)):
        w_out_copy(peer, 9 + i).wait_send()
        d_out_copy(peer, 24 + i).wait_recv()
    own_d_out.wait()

    @pl.loop(0, 4)
    def _(i):
        p = farthest(i)
        at = pl.ds(pl.multiple_of(p * quarter, quarter), quarter)
        value = dot(attn_in[:, :, at].reshape(tokens, quarter), g_qkv[...].reshape(tokens, 3 * quarter), TN)
        w_first[pl.ds(p * part, part), :, 0 : 3 * quarter] = value.reshape(part, w_first.shape[1], 3 * quarter).astype(BF)
        w_first[pl.ds(p * part, part), :, 3 * quarter :] = d_out_in[pl.ds(p * part, part)]
        send_side(FIRST, p)

    total = sum_end(in_copies, pown, r2)
    value = x_ref[...].astype(F32)
    scale = lax.rsqrt(mean_of(value * value) + 1e-06)
    normed = value * scale
    prod = total * normed
    g_first = row_sum(prod)
    mean = mean_of(prod * gain_first[...])
    grad_in_ref[...] = (g_middle[...] + scale * (total * gain_first[...] - normed * mean)).astype(BF)

    sum_turn(out_copies, pown2, r1b)
    pl.loop(2, lines - 1)(lambda j: down_turn(j))
    total = sum_end(out_copies, pown2, r2b)
    mlp_part = valid_ref[...] * total
    value = middle[...] + mlp_part
    out_ref[...] = value.astype(BF)
    stat_out = jnp.sum(row_sum(valid_ref[...] * value * value), axis=1, keepdims=True)
    stat_mlp = jnp.sum(row_sum(mlp_part * mlp_part), axis=1, keepdims=True)

    strips = d // 128
    small_ref[...] = jnp.zeros_like(small_ref)
    for i in range(strips):
        at = slice(128 * i, 128 * (i + 1))
        small_ref[i : i + 1, :] = g_first[:, at]
        small_ref[strips + i : strips + i + 1, :] = g_second[:, at]
    own_gain = row_sum((g_hin[...] * hat[...]).reshape(tokens, width))
    for i in range(width // 128):
        small_ref[pl.ds(2 * strips + me * (width // 128) + i, 1), :] = own_gain[:, 128 * i : 128 * (i + 1)]
    base = 3 * strips
    for h in range(heads):
        for a in range(taps):
            tile = corr[h, a * t : (a + 1) * t, :]
            for b in range(span):
                lanes[a * span + b : a * span + b + 1, :] = row_sum(jnp.where(diff == b, tile, 0.0))
        small_ref[pl.ds(base + me * heads + h, 1), :] = row_sum(jnp.transpose(lanes[...]))
    base += 4 * heads
    lanes[0 : 2 * heads, :] = g_mix[...]
    lanes[2 * heads :, :] = jnp.zeros((t - 2 * heads, t), F32)
    small_ref[pl.ds(base + me, 1), :] = row_sum(jnp.transpose(lanes[...]))
    base += 4
    lane = lax.broadcasted_iota(jnp.int32, (1, 128), 1)
    count = jnp.sum(row_sum(jnp.broadcast_to(valid_ref[...], (t, 128))), axis=1, keepdims=True) * (1.0 / 128.0)
    stats = jnp.zeros((1, 128), F32)
    for i, stat in enumerate((stat_out, stat_attn, stat_mlp, count)):
        stats = jnp.where(lane == i, stat, stats)
    small_ref[base : base + 1, :] = stats

    peers = [(sibling, f), (across, f)] + [(me, flip(bit)) for bit in bits]

    def small_copy(i):
        return pltpu.make_async_remote_copy(
            src_ref=small_send.at[i], dst_ref=small_recv.at[i],
            send_sem=rep_send.at[40 + i], recv_sem=rep_recv.at[40 + i],
            device_id=peers[i], device_id_type=MESH,
        )

    def small_step(i):
        small_send[i] = small_ref[...]
        small_copy(i).start()

    def small_take(i):
        small_copy(i).wait_recv()
        small_ref[...] = small_ref[...] + small_recv[i]

    small_step(0)
    rs_close(DOWN)
    final_start(DOWN, 30)
    small_take(0)
    small_step(1)
    rs_turn(MLP, 0)
    small_take(1)
    small_step(2)
    final_pass(DOWN, 30)
    pl.loop(1, lines - 1)(lambda j: rs_turn(MLP, j))
    for i in range(2, len(peers)):
        small_take(i)
        if i + 1 < len(peers):
            small_step(i + 1)
    rs_close(MLP)
    final_start(MLP, 33)
    rs_turn(FIRST, 0)
    final_pass(MLP, 33)
    pl.loop(1, lines - 1)(lambda j: rs_turn(FIRST, j))
    rs_close(FIRST)
    final_start(FIRST, 36)
    final_pass(FIRST, 36)
    for k in range(3):
        final_end(k, (36, 33, 30)[k])
    for k in range(3):
        rs_drain(k)
    for i in range(len(peers)):
        small_copy(i).wait_send()
    for i, peer in enumerate((sibling, across, diagonal)):
        d_out_copy(peer, 24 + i).wait_send()


def run_layer(cfg, x, g, seg, valid, gains, score, mix, shards_in):
    heads, hd, taps, span, docs, shards, units = cfg
    t, d = x.shape
    width = heads * hd
    first, mlp, down = shards_in
    bits = shards.bit_length() - 1
    tall = max(s.shape[0] for s in shards_in)
    broad = max(s.shape[1] for s in shards_in)

    def shape(dtype, *dims):
        return jax.ShapeDtypeStruct(dims, dtype)

    v = pltpu.VMEM
    dma = pltpu.SemaphoreType.DMA
    out_shape = (
        shape(BF, t, d), shape(BF, t, d), shape(F32, 64, 128),
        *(shape(BF, 4, *s.shape) for s in shards_in),
        *(shape(BF, 3, shards, *s.shape) for s in shards_in),
    )
    scratch = [
        *(v((shards, *s.shape), BF) for s in shards_in),
        v((4, t, d), BF), v((4, t, d), BF), v((4, 8, t), F32), v((4, t, d), BF), v((4, t, 3 * width), BF),
        v((4, t, width), F32), v((4, t, width), F32), v((4, heads, t, t), F32), v((4, heads, t, t), BF),
        v((4, t, width), BF), v((shards // 4, first.shape[0], d), BF),
        v((t, d), F32), v((4 * t, units), F32), v((4 * t, units), F32), v((4, t, units), BF), v((4, t, 2 * units), BF),
        v((4, t, d), BF), v((t, d), F32), v((4, t, 3 * width), BF), v((4, t, width), F32),
        v((shards // 4, first.shape[0], d), BF), v((shards, first.shape[0], width), BF),
        v((2, t, d), BF), v((2, t, d), F32), v((2, t, d), BF), v((t, d), BF), v((t, d), BF),
        v((2, t, d), BF), v((2, t, d), F32), v((2, t, d), BF), v((t, d), BF),
        v((heads, taps * t, t), BF), v((heads, taps * t, t), F32), v((t, width), F32), v((t, t), F32), v((2 * heads, t), F32),
        v((tall, broad), BF), v((2 + bits, 64, 128), F32), v((2 + bits, 64, 128), F32),
        dma((3, 3, shards)), dma((3, shards)), dma((3, 3, shards)), dma((3, 3, shards)), dma((48,)), dma((48,)), dma((8,)),
    ]
    return pl.pallas_call(
        functools.partial(layer_kernel, cfg),
        out_shape=out_shape,
        in_specs=[vmem_spec()] * 7 + [smem_spec()] * 2 + [hbm_spec()] * 3,
        out_specs=(vmem_spec(),) * 3 + (hbm_spec(),) * 6,
        scratch_shapes=scratch,
        compiler_params=pltpu.CompilerParams(
            collective_id=0, has_side_effects=True, vmem_limit_bytes=VMEM_LIMIT
        ),
    )(x, g, seg, valid, *gains, score, mix, *shards_in)


def widen_kernel(strip, count, first_ref, mlp_ref, down_ref, *outs):
    quarter = first_ref.shape[2] // 4
    for r in range(4):
        for k in range(4):
            outs[k][:, r * quarter : (r + 1) * quarter] = first_ref[r, :, k * quarter : (k + 1) * quarter].astype(F32)
        outs[6][r] = down_ref[r].astype(F32)
        for k in range(2):
            for i in range(count):
                at = (4 * i + r) * strip
                outs[4 + k][:, at : at + strip] = mlp_ref[r, :, (k * count + i) * strip : (k * count + i + 1) * strip].astype(F32)


def widen(first, mlp, down, strip, count):
    _, rows, d = first.shape
    steps = 4 if rows % 64 == 0 and down.shape[1] % 64 == 0 else 1
    hidden = 4 * strip * count
    rows_step, down_step = rows // steps, down.shape[1] // steps

    def taken(array, size):
        return pl.BlockSpec((4, size, array.shape[2]), lambda i: (0, i, 0))

    def given(size, width):
        return pl.BlockSpec((size, width), lambda i: (i, 0))

    return pl.pallas_call(
        functools.partial(widen_kernel, strip, count),
        grid=(steps,),
        out_shape=tuple(jax.ShapeDtypeStruct((rows, d), F32) for _ in range(4))
        + tuple(jax.ShapeDtypeStruct((rows, hidden), F32) for _ in range(2))
        + (jax.ShapeDtypeStruct(down.shape, F32),),
        in_specs=[taken(first, rows_step), taken(mlp, rows_step), taken(down, down_step)],
        out_specs=tuple(given(rows_step, d) for _ in range(4))
        + tuple(given(rows_step, hidden) for _ in range(2))
        + (taken(down, down_step),),
        compiler_params=pltpu.CompilerParams(vmem_limit_bytes=VMEM_LIMIT),
    )(first, mlp, down)


def per_device(
    hidden_in,
    doc_lengths,
    w_query,
    w_key,
    w_value,
    w_output,
    w_gate,
    w_up,
    w_down,
    attn_norm,
    mlp_norm,
    head_norm,
    score_kernel,
    head_mixing,
    grad_out,
):
    _, t, d = hidden_in.shape
    reps = lax.axis_size("rep")
    shards = lax.axis_size("fsdp")
    me = lax.axis_index("rep")
    hidden = w_gate.shape[1]
    heads = H // reps
    hd = d // H
    quarter = d // reps
    units = hidden // reps
    strip = units // shards
    taps, span = score_kernel.shape[1:]
    docs = doc_lengths.shape[1] - 1
    rows_here = w_gate.shape[0]

    def mine(array, size, axis):
        return lax.dynamic_slice_in_dim(array, me * size, size, axis)

    def strips(w):
        return mine(w.reshape(rows_here, shards, reps, strip), 1, 2).reshape(rows_here, units)

    first_shard = jnp.concatenate([mine(w, quarter, 1) for w in (w_query, w_key, w_value, w_output)], axis=1)
    mlp_shard = jnp.concatenate([strips(w_gate), strips(w_up)], axis=1)
    down_shard = mine(w_down, strip, 0)

    boundary = jnp.cumsum(doc_lengths[:, :-1], axis=1)
    places = jnp.arange(t, dtype=jnp.int32)
    seg_ids = jnp.sum((places[None, :, None] >= boundary[:, None, :]).astype(jnp.int32), axis=2)
    seg_own = jnp.broadcast_to(seg_ids.astype(F32), (8, t))
    valid = (seg_ids < docs).astype(F32).reshape(t, 1)
    gains = (attn_norm.reshape(1, d), mlp_norm.reshape(1, d), mine(head_norm, quarter, 0).reshape(1, quarter))
    score = mine(score_kernel.reshape(H, taps * span), heads, 0)
    mix = mine(head_mixing, heads, 0)
    cfg = (heads, hd, taps, span, docs, shards, units)
    block_out, grad_in, small, a_first, a_mlp, a_down = run_layer(
        cfg, hidden_in.reshape(t, d), grad_out.reshape(t, d), seg_own, valid, gains, score, mix,
        (first_shard, mlp_shard, down_shard),
    )[:6]

    lines = d // 128
    base = 3 * lines
    small_score = small[base : base + H, : taps * span]
    base += H
    small_mix = small[base : base + reps, : 2 * heads]
    stats = small[base + reps, :STATS]
    root_means = jnp.sqrt(stats[:3] / (stats[3] * d))

    if strip % 128 == 0:
        g_q, g_k, g_v, g_o, g_gate, g_up, g_down = widen(a_first, a_mlp, a_down, strip, shards)
    else:
        first = a_first.astype(F32).reshape(reps, rows_here, 4, quarter)
        first = jnp.moveaxis(first, 0, 2).reshape(rows_here, 4, d)
        g_q, g_k, g_v, g_o = (first[:, k] for k in range(4))
        mlp = a_mlp.astype(F32).reshape(reps, rows_here, 2, shards, strip)
        mlp = jnp.moveaxis(mlp, 0, 3).reshape(rows_here, 2, hidden)
        g_gate, g_up = mlp[:, 0], mlp[:, 1]
        g_down = a_down.astype(F32)
    return (
        block_out.reshape(hidden_in.shape),
        grad_in.reshape(hidden_in.shape),
        g_q,
        g_k,
        g_v,
        g_o,
        g_gate,
        g_up,
        g_down.reshape(w_down.shape),
        small[:lines].reshape(d),
        small[lines : 2 * lines].reshape(d),
        small[2 * lines : 3 * lines].reshape(d),
        small_score.reshape(score_kernel.shape),
        small_mix.reshape(head_mixing.shape),
        root_means,
    )


def solution(mesh):
    rows = P(("rep", "fsdp"), None, None)
    split = P("fsdp", None)
    placed = (rows, P(("rep", "fsdp"), None)) + (split,) * 7 + (P(),) * 5 + (rows,)
    return jax.shard_map(
        per_device,
        mesh=mesh,
        in_specs=placed,
        out_specs=(rows, rows) + (split,) * 7 + (P(),) * 6,
        check_vma=False,
    )
```

```python
import functools

import jax
import jax.numpy as jnp
from jax import lax
from jax.experimental import pallas as pl
from jax.experimental.pallas import tpu as pltpu
from jax.sharding import PartitionSpec as P

H = 16
BF = jnp.bfloat16
F32 = jnp.float32
MESH = pl.DeviceIdType.MESH
VMEM_LIMIT = 62 * 1024 * 1024
NN = (((1,), (0,)), ((), ()))
NT = (((1,), (1,)), ((), ()))
TN = (((0,), (0,)), ((), ()))
FIRST, MLP, DOWN = 0, 1, 2
UP, DN, SIDE = 0, 1, 2
STATS = 4


def dot(a, b, dims=NN):
    return lax.dot_general(a, b, dims, preferred_element_type=F32)


def merge(value):
    n, rows, width = value.shape
    if rows % 16 == 0:
        return value.reshape(n * rows, width)
    return value.astype(F32).reshape(n * rows, width).astype(value.dtype)


def vmem_spec():
    return pl.BlockSpec(memory_space=pltpu.VMEM)


def smem_spec():
    return pl.BlockSpec(memory_space=pltpu.SMEM)


def hbm_spec():
    return pl.BlockSpec(memory_space=pl.ANY)


def grids(t):
    rows = lax.broadcasted_iota(jnp.int32, (t, t), 0)
    cols = lax.broadcasted_iota(jnp.int32, (t, t), 1)
    return rows, cols


def allowed_of(seg_row, rows, cols):
    t = rows.shape[0]
    along = jnp.broadcast_to(seg_row, (t, t))
    return (along == jnp.transpose(along)) & (cols <= rows)


def lagged(masked, taps, rows):
    parts = [masked.astype(BF)]
    for a in range(1, taps):
        parts.append(jnp.where(rows >= a, pltpu.roll(masked, a, 0), 0.0).astype(BF))
    return jnp.concatenate(parts, axis=1)


def row_sum(value):
    return jnp.sum(value, axis=0, keepdims=True)


def mean_of(value):
    return jnp.mean(value, axis=1, keepdims=True)


def layer_kernel(cfg, *refs):
    heads, hd, taps, span, docs, shards, units = cfg
    (
        x_ref, g_ref, seg_ref, valid_ref, gain_first, gain_second, gain_head, score_ref, mix_ref,
        own_first, own_mlp, own_down,
        out_ref, grad_in_ref, small_ref, all_first, all_mlp, all_down,
        w_first, w_mlp, w_down, wide, g_mlp, seg_all, attn_in, qkv, hat, inv, probs, masked, head_in, w_out,
        middle, slope, silu, hidden, g_gu, g_attn, g_middle, g_qkv, g_hin, d_out_in,
        psend, pown, r1, ysend, r2, psend2, pown2, r1b, r2b, bands, corr, g_wide, lanes, g_mix,
        x_first, x_mlp, x_down, z_first, z_mlp, z_down, small_send, small_recv,
        ag_send, ag_recv, rs_send, rs_recv, rep_send, rep_recv, local, credit,
    ) = refs
    t, d = x_ref.shape
    width = heads * hd
    quarter = d // 4
    lines = shards // 2
    me = lax.axis_index("rep")
    f = lax.axis_index("fsdp")
    plane, core = me // 2, me % 2
    sibling, across = plane * 2 + (1 - core), (1 - plane) * 2 + core
    diagonal = (1 - plane) * 2 + (1 - core)
    z, side = f // 2, f % 2
    partner = 2 * z + (1 - side)
    weights = (w_first, w_mlp, w_down)
    x_lands, z_lands = (x_first, x_mlp, x_down), (z_first, z_mlp, z_down)
    peer_of = (f + 2, f - 2, partner)
    tokens = 4 * t
    part = shards // 4
    strip = units // shards
    rows, cols = grids(t)

    def flip(bit):
        return f + (1 - 2 * ((f // bit) % 2)) * bit

    bits = []
    bit = 1
    while bit < shards:
        bits.append(bit)
        bit *= 2

    barrier = pltpu.get_barrier_semaphore()

    def greet(r, s):
        pl.semaphore_signal(barrier, inc=1, device_id=(r, s), device_id_type=MESH)

    for r in (sibling, across, diagonal):
        greet(r, f)
    greet(me, partner)

    @pl.loop(1, lines)
    def _(s):
        greet(me, 2 * ((z + s) % lines) + side)

    pl.semaphore_wait(barrier, 3 + lines)

    def rep_copy(src, dst, slot, peer):
        return pltpu.make_async_remote_copy(
            src_ref=src, dst_ref=dst, send_sem=rep_send.at[slot], recv_sem=rep_recv.at[slot],
            device_id=(peer, f), device_id_type=MESH,
        )

    def ag(k, block, way):
        return pltpu.make_async_remote_copy(
            src_ref=weights[k].at[block], dst_ref=weights[k].at[block],
            send_sem=ag_send.at[k, way, block], recv_sem=ag_recv.at[k, block],
            device_id=(me, peer_of[way]), device_id_type=MESH,
        )

    def ag_walk(k, s, first, act):
        sides = (side, 1 - side) if k == DOWN else (side,)
        if isinstance(s, int) and s == 0:
            for q in sides:
                block = 2 * z + q
                if k == DOWN and q is not side:
                    first(k, block)

                @pl.when(z < lines - 1)
                def _():
                    act(k, block, UP)

                @pl.when(z > 0)
                def _():
                    act(k, block, DN)

                if k != DOWN:
                    act(k, block, SIDE)
            return

        @pl.when(z - s >= 0)
        def _():
            for q in sides:
                block = 2 * (z - s) + q
                first(k, block)

                @pl.when(z < lines - 1)
                def _():
                    act(k, block, UP)

                if k != DOWN:
                    act(k, block, SIDE)

        @pl.when(z + s < lines)
        def _():
            for q in sides:
                block = 2 * (z + s) + q
                first(k, block)

                @pl.when(z > 0)
                def _():
                    act(k, block, DN)

                if k != DOWN:
                    act(k, block, SIDE)

    def arrived(k, block):
        ag(k, block, SIDE).wait_recv()

    def go(k, block, way):
        ag(k, block, way).start()

    def gone(k, block, way):
        ag(k, block, way).wait_send()

    def ag_steps(k, low, high):
        if low == 0:
            ag_walk(k, 0, arrived, go)
        else:
            pl.loop(low, high)(lambda s: ag_walk(k, s, arrived, go))

    def ag_done(k):
        if k != DOWN:
            pl.loop(0, lines)(lambda zz: arrived(k, 2 * zz + (1 - side)))

    def ag_drain(k):
        nothing = lambda *_: None
        if k == DOWN:
            gone(k, f, SIDE)
        ag_walk(k, 0, nothing, gone)
        pl.loop(1, lines)(lambda s: ag_walk(k, s, nothing, gone))

    def gather_start(fulls, slot):
        for i, full in enumerate(fulls):
            rep_copy(full.at[me], full.at[me], slot + 3 * i, across).start()
            rep_copy(full.at[me], full.at[me], slot + 3 * i + 1, sibling).start()

    def gather_pass(fulls, slot):
        for i, full in enumerate(fulls):
            rep_copy(full.at[me], full.at[me], slot + 3 * i, across).wait_recv()
            rep_copy(full.at[across], full.at[across], slot + 3 * i + 2, sibling).start()

    def gather_end(fulls, slot):
        for i, full in enumerate(fulls):
            rep_copy(full.at[me], full.at[me], slot + 3 * i + 1, sibling).wait_recv()
            rep_copy(full.at[across], full.at[across], slot + 3 * i + 2, sibling).wait_recv()
        for i, full in enumerate(fulls):
            rep_copy(full.at[me], full.at[me], slot + 3 * i, across).wait_send()
            rep_copy(full.at[me], full.at[me], slot + 3 * i + 1, sibling).wait_send()
            rep_copy(full.at[across], full.at[across], slot + 3 * i + 2, sibling).wait_send()

    def pair_of(ref, a, b):
        return jnp.concatenate([ref[a], ref[b]], axis=0)

    def sum_copies(slot, send_buf, first_land, second_land):
        return (
            rep_copy(send_buf, first_land, slot, sibling),
            rep_copy(ysend, second_land, slot + 1, across),
        )

    def column_chunk(i):
        return pl.ds(pl.multiple_of(i * quarter, quarter), quarter)

    def sum_theirs(product, copies, send_buf):
        @pl.loop(0, 4)
        def _(i):
            value = product(1 - core, 2 + (1 - core), i)
            send_buf[0, :, column_chunk(i)] = value[:t].astype(BF)
            send_buf[1, :, column_chunk(i)] = value[t:].astype(BF)

        copies[0].start()

    def sum_ours(product, own_buf):
        @pl.loop(0, 4)
        def _(i):
            value = product(across, me, i)
            own_buf[0, :, column_chunk(i)] = value[:t].astype(own_buf.dtype)
            own_buf[1, :, column_chunk(i)] = value[t:].astype(own_buf.dtype)

    def sum_turn(copies, own_buf, first_land):
        copies[0].wait_recv()
        ysend[...] = (own_buf[0].astype(F32) + first_land[1 - plane].astype(F32)).astype(BF)
        copies[1].start()
        own_buf[1] = (own_buf[1].astype(F32) + first_land[plane].astype(F32)).astype(own_buf.dtype)

    def sum_end(copies, own_buf, second_land):
        copies[1].wait_recv()
        total = own_buf[1].astype(F32) + second_land[...].astype(F32)
        copies[0].wait_send()
        copies[1].wait_send()
        return total

    def rs_side(k, zz):
        source = weights[k].at[2 * zz + (1 - side)]
        if k == DOWN:
            source = x_mlp.at[zz, pl.ds(0, strip), pl.ds(0, d)]
        return pltpu.make_async_remote_copy(
            src_ref=source, dst_ref=x_lands[k].at[zz],
            send_sem=rs_send.at[k, 0, zz], recv_sem=rs_recv.at[k, 0, zz],
            device_id=(me, partner), device_id_type=MESH,
        )

    def rs_owner(k, zz):
        return pltpu.make_async_remote_copy(
            src_ref=weights[k].at[2 * zz + side], dst_ref=z_lands[k].at[z],
            send_sem=rs_send.at[k, 1, zz], recv_sem=rs_recv.at[k, 1, z],
            device_id=(me, 2 * zz + side), device_id_type=MESH,
        )

    def rs_from(k, zz):
        return pltpu.make_async_remote_copy(
            src_ref=weights[k].at[2 * zz + side], dst_ref=z_lands[k].at[zz],
            send_sem=rs_send.at[k, 1, zz], recv_sem=rs_recv.at[k, 1, zz],
            device_id=(me, 2 * zz + side), device_id_type=MESH,
        )

    def rs_add(k, block, landed):
        grad = weights[k]
        high = grad.shape[1]
        step = 16 if high % 16 == 0 else high

        @pl.loop(0, high // step)
        def _(i):
            at = pl.ds(pl.multiple_of(i * step, step), step)
            total = grad[block, at, :].astype(F32)
            for land, slot in landed:
                total = total + land[slot, at, :].astype(F32)
            grad[block, at, :] = total.astype(BF)

    def after(s):
        return (z + s) % lines

    def rs_turn(k, s):
        zz = after(s)
        rs_side(k, zz).wait_recv()
        rs_add(k, 2 * zz + side, [(x_lands[k], zz)])
        rs_owner(k, zz).start()

    def rs_close(k):
        rs_side(k, z).wait_recv()
        landed = [(x_lands[k], z)]
        for s in range(1, lines):
            rs_from(k, after(s)).wait_recv()
            landed.append((z_lands[k], after(s)))
        rs_add(k, f, landed)

    def rs_drain(k):
        if k != DOWN:
            pl.loop(0, lines)(lambda s: rs_side(k, after(s)).wait_send())

        @pl.loop(1, lines)
        def _(s):
            rs_owner(k, after(s)).wait_send()

    outs = (all_first, all_mlp, all_down)

    def final_copies(k, slot):
        own = weights[k].at[f]
        full = outs[k]
        return (
            rep_copy(own, full.at[me], slot, across),
            rep_copy(own, full.at[me], slot + 1, sibling),
            rep_copy(full.at[across], full.at[across], slot + 2, sibling),
            pltpu.make_async_copy(own, full.at[me], local.at[1 + k]),
        )

    def final_start(k, slot):
        a, b, _, here = final_copies(k, slot)
        a.start()
        b.start()
        here.start()

    def final_pass(k, slot):
        a, _, c, _ = final_copies(k, slot)
        a.wait_recv()
        c.start()

    def final_end(k, slot):
        a, b, c, here = final_copies(k, slot)
        b.wait_recv()
        c.wait_recv()
        a.wait_send()
        b.wait_send()
        c.wait_send()
        here.wait()

    owns = (own_first, own_mlp, own_down)
    loads = [pltpu.make_async_copy(owns[k], weights[k].at[f], local.at[4 + k]) for k in range(3)]
    for load in loads:
        load.start()
    wide[me] = x_ref[...]
    g_mlp[me] = g_ref[...]
    seg_all[me] = seg_ref[...]
    entering = (seg_all, wide, g_mlp)
    gather_start(entering, 0)
    loads[FIRST].wait()
    ag_steps(FIRST, 0, 1)

    diff = cols - rows + (span - 1) // 2

    @pl.loop(0, heads)
    def _(h):
        for a in range(taps):
            band = jnp.zeros((t, t), F32)
            for b in range(span):
                band = jnp.where(diff == b, score_ref[h, a * span + b], band)
            bands[h, a * t : (a + 1) * t, :] = band.astype(BF)

    gather_pass(entering, 0)
    ag_steps(FIRST, 1, 2)
    loads[DOWN].wait()
    ag(DOWN, f, SIDE).start()
    gather_end(entering, 0)

    @pl.loop(0, 4)
    def _(r):
        value = wide[r].astype(F32)
        scale = lax.rsqrt(mean_of(value * value) + 1e-06)
        attn_in[r] = (value * scale * gain_first[...]).astype(BF)
        valid = jnp.transpose(jnp.broadcast_to(seg_all[r][0:1, :], (t, t)))[:, 0:1] < float(docs)
        g_mlp[r] = jnp.where(valid, g_mlp[r].astype(F32), 0.0).astype(BF)

    ag_steps(FIRST, 2, 3)
    loads[MLP].wait()
    ag_steps(MLP, 0, 1)
    ag_steps(FIRST, 3, lines)
    ag_steps(MLP, 1, 2)
    ag_done(FIRST)

    def w_out_copy(peer, slot):
        return rep_copy(
            w_first.at[pl.ds(peer * part, part), :, pl.ds(3 * quarter, quarter)],
            w_out.at[:, :, pl.ds(pl.multiple_of(me * quarter, quarter), quarter)],
            slot, peer,
        )

    for i, peer in enumerate((sibling, across, diagonal)):
        w_out_copy(peer, 9 + i).start()
    own_out = pltpu.make_async_copy(
        w_first.at[pl.ds(me * part, part), :, pl.ds(3 * quarter, quarter)],
        w_out.at[:, :, pl.ds(pl.multiple_of(me * quarter, quarter), quarter)],
        local.at[0],
    )
    own_out.start()

    for i in range(3):
        value = dot(attn_in[...].reshape(tokens, d), merge(w_first[:, :, i * quarter : (i + 1) * quarter]))
        qkv[:, :, i * quarter : (i + 1) * quarter] = value.astype(BF).reshape(4, t, quarter)
    ag_steps(MLP, 2, 3)
    ag_steps(DOWN, 0, 1)

    def split(ref, row, kind, h):
        return ref[row, :, kind * width + h * hd : kind * width + (h + 1) * hd]

    @pl.loop(0, 4)
    def _(row):
        allowed = allowed_of(seg_all[row][0:1, :], rows, cols)
        for pair in range(heads // 2):
            both = []
            for c in range(2):
                h = 2 * pair + c
                scores = dot(split(qkv, row, 0, h), split(qkv, row, 1, h), NT) * hd**-0.5
                kept = jnp.where(allowed, scores, 0.0)
                masked[row, h] = kept.astype(BF)
                logits = jnp.where(allowed, dot(lagged(kept, taps, rows), bands[h]), -1e30)
                e = jnp.exp(logits - jnp.max(logits, axis=1, keepdims=True))
                p = e / jnp.sum(e, axis=1, keepdims=True)
                probs[row, h] = p
                both.append(p)
            for e in range(2):
                h = 2 * pair + e
                mixed = (mix_ref[h, 0] * both[0] + mix_ref[h, 1] * both[1]).astype(BF)
                out = dot(mixed, split(qkv, row, 2, h))
                centred = out - mean_of(out)
                scale = lax.rsqrt(mean_of(centred * centred) + 1e-05)
                hat[row, :, h * hd : (h + 1) * hd] = centred * scale
                inv[row, :, h : h + 1] = scale
        head_in[row] = (hat[row] * gain_head[...]).astype(BF)

    for i, peer in enumerate((sibling, across, diagonal)):
        w_out_copy(peer, 9 + i).wait_recv()
    own_out.wait()

    copies = sum_copies(12, psend, r1, r2)
    product = lambda a, b, i: dot(pair_of(head_in, a, b), merge(w_out[:, :, column_chunk(i)]))
    sum_theirs(product, copies, psend)
    sum_ours(product, pown)
    ag_steps(MLP, 3, lines)
    sum_turn(copies, pown, r1)
    total = sum_end(copies, pown, r2)
    attn_part = valid_ref[...] * total
    value = x_ref[...].astype(F32) + attn_part
    middle[...] = value
    stat_attn = jnp.sum(row_sum(attn_part * attn_part), axis=1, keepdims=True)
    scale = lax.rsqrt(mean_of(value * value) + 1e-06)
    wide[me] = (value * scale * gain_second[...]).astype(BF)
    gather_start((wide,), 14)
    ag_steps(DOWN, 1, 2)
    gather_pass((wide,), 14)
    gather_end((wide,), 14)
    mlp_in = wide
    ag_steps(DOWN, 2, 3)
    ag_done(MLP)

    chunk = 256

    @pl.loop(0, units // chunk)
    def _(i):
        at = pl.ds(pl.multiple_of(i * chunk, chunk), chunk)
        after = pl.ds(pl.multiple_of(units + i * chunk, chunk), chunk)
        operand = mlp_in[...].reshape(tokens, d)
        gate = dot(operand, merge(w_mlp[:, :, at]))
        upper = dot(operand, merge(w_mlp[:, :, after]))
        sig = 1.0 / (1.0 + jnp.exp(-gate))
        act = gate * sig
        hidden[:, :, at] = (act * upper).astype(BF).reshape(4, t, chunk)
        silu[:, at] = act.astype(BF)
        slope[:, at] = (upper * sig * (1.0 + gate * (1.0 - sig))).astype(BF)

    @pl.loop(0, 4)
    def _(i):
        span_units = units // 4
        at = pl.ds(pl.multiple_of(i * span_units, span_units), span_units)
        value = dot(hidden[:, :, at].reshape(tokens, span_units), g_mlp[...].reshape(tokens, d), TN)
        value = value.reshape(part, strip, d)
        for j in range(part // 2):
            half = jnp.where(side == 0, value[2 * j + 1], value[2 * j])
            x_mlp[i * (part // 2) + j, 0:strip, 0:d] = half.astype(BF)

    @pl.loop(1, lines + 1)
    def _(s):
        rs_side(DOWN, after(s)).start()

    ag_steps(DOWN, 3, lines)

    @pl.loop(0, 4)
    def _(i):
        span_units = units // 4
        at = pl.ds(pl.multiple_of(i * span_units, span_units), span_units)
        after = pl.ds(pl.multiple_of(units + i * span_units, span_units), span_units)
        g_hidden = dot(g_mlp[...].reshape(tokens, d), merge(w_down[pl.ds(i * part, part)]), NT)
        g_gu[:, :, at] = (g_hidden * slope[:, at].astype(F32)).astype(BF).reshape(4, t, span_units)
        g_gu[:, :, after] = (g_hidden * silu[:, at].astype(F32)).astype(BF).reshape(4, t, span_units)

    mlp_copies = sum_copies(17, psend, r1, r2)
    product = lambda a, b, i: dot(pair_of(g_gu, a, b), merge(w_mlp[pl.ds(i * part, part)]), NT)
    sum_theirs(product, mlp_copies, psend)
    sum_ours(product, pown)

    out_copies = (rep_copy(psend2, r1b, 19, sibling), rep_copy(ysend, r2b, 20, across))
    product = lambda a, b, i: dot(pair_of(hidden, a, b), merge(w_down[:, :, column_chunk(i)]))
    sum_theirs(product, out_copies, psend2)
    sum_ours(product, pown2)
    sum_turn(mlp_copies, pown, r1)

    ag_drain(DOWN)

    @pl.loop(0, 4)
    def _(i):
        span_units = units // 4
        at = pl.ds(pl.multiple_of(i * span_units, span_units), span_units)
        value = dot(hidden[:, :, at].reshape(tokens, span_units), g_mlp[...].reshape(tokens, d), TN)
        w_down[pl.ds(i * part, part)] = value.reshape(part, w_down.shape[1], d).astype(BF)

    total = sum_end(mlp_copies, pown, r2)
    value = middle[...]
    scale = lax.rsqrt(mean_of(value * value) + 1e-06)
    normed = value * scale
    prod = total * normed
    g_second = row_sum(prod)
    mean = mean_of(prod * gain_second[...])
    value = g_ref[...].astype(F32) + scale * (total * gain_second[...] - normed * mean)
    g_middle[...] = value
    g_attn[me] = (valid_ref[...] * value).astype(BF)
    gather_start((g_attn,), 21)
    ag_drain(MLP)
    pl.loop(0, lines)(lambda s: rs_side(DOWN, after(s)).wait_send())
    pl.semaphore_signal(credit, inc=1, device_id=(me, partner), device_id_type=MESH)

    def in_turn(i):
        return (z // (part // 2) + 1 + i) % 4

    def send_side(k, p):
        @pl.loop(0, part // 2)
        def _(j):
            zz = p * (part // 2) + j
            rs_side(k, zz).start()

    @pl.loop(0, 4)
    def _(i):
        p = in_turn(i)
        at = pl.ds(pl.multiple_of(p * quarter, quarter), quarter)
        size = units // 2

        @pl.loop(0, 4)
        def _(j):
            to = pl.ds(pl.multiple_of(j * size, size), size)
            value = dot(mlp_in[:, :, at].reshape(tokens, quarter), g_gu[:, :, to].reshape(tokens, size), TN)
            w_mlp[pl.ds(p * part, part), :, to] = value.reshape(part, w_mlp.shape[1], size).astype(BF)


        @pl.when(i == 0)
        def _():
            pl.semaphore_wait(credit, 1)

        send_side(MLP, p)

    gather_pass((g_attn,), 21)
    gather_end((g_attn,), 21)

    value = dot(g_attn[...].reshape(tokens, d), merge(w_out[...]), NT)
    g_hin[...] = value.reshape(4, t, width)
    d_out = w_out

    @pl.loop(0, 4)
    def _(i):
        value = dot(head_in[...].reshape(tokens, width), g_attn[:, :, column_chunk(i)].reshape(tokens, quarter), TN)
        d_out[:, :, column_chunk(i)] = value.reshape(part, w_first.shape[1], quarter).astype(BF)


    def d_out_copy(peer, slot):
        return rep_copy(
            d_out.at[:, :, pl.ds(pl.multiple_of(peer * quarter, quarter), quarter)],
            d_out_in.at[pl.ds(me * part, part)],
            slot, peer,
        )

    for i, peer in enumerate((sibling, across, diagonal)):
        d_out_copy(peer, 24 + i).start()
    own_d_out = pltpu.make_async_copy(
        d_out.at[:, :, pl.ds(pl.multiple_of(me * quarter, quarter), quarter)],
        d_out_in.at[pl.ds(me * part, part)], local.at[7],
    )
    own_d_out.start()
    pl.loop(1, lines)(lambda s: rs_turn(DOWN, s))

    corr[...] = jnp.zeros_like(corr)
    g_mix[...] = jnp.zeros_like(g_mix)
    lanes[...] = jnp.zeros_like(lanes)

    @pl.loop(0, 4)
    def _(row):
        allowed = allowed_of(seg_all[row][0:1, :], rows, cols)
        g_wide[...] = g_hin[row] * gain_head[...]
        for pair in range(heads // 2):
            g_heads, g_mixed = [], []
            both = [probs[row, 2 * pair + c] for c in range(2)]
            for e in range(2):
                h = 2 * pair + e
                scaled = g_wide[:, h * hd : (h + 1) * hd]
                own_hat = hat[row, :, h * hd : (h + 1) * hd]
                g = inv[row, :, h : h + 1] * (scaled - mean_of(scaled) - own_hat * mean_of(scaled * own_hat))
                g = g.astype(BF)
                g_heads.append(g)
                g_mixed.append(dot(g, split(qkv, row, 2, h), NT))
            for e in range(2):
                h = 2 * pair + e
                mixed = (mix_ref[h, 0] * both[0] + mix_ref[h, 1] * both[1]).astype(BF)
                g_v = dot(mixed, g_heads[e], TN)
                g_qkv[row, :, 2 * width + h * hd : 2 * width + (h + 1) * hd] = g_v.astype(BF)
                for c in range(2):
                    place = (2 * pair + e) * 2 + c
                    g_mix[place : place + 1, :] += row_sum(g_mixed[e] * both[c])
            for c in range(2):
                h = 2 * pair + c
                g_probs = mix_ref[2 * pair, c] * g_mixed[0] + mix_ref[2 * pair + 1, c] * g_mixed[1]
                weighted = both[c] * g_probs
                g_conv = weighted - both[c] * jnp.sum(weighted, axis=1, keepdims=True)
                corr[h] += dot(lagged(masked[row, h].astype(F32), taps, rows), g_conv.astype(BF), TN)
                g_kept = dot(g_conv.astype(BF), bands[h, 0:t, :], NT)
                for a in range(1, taps):
                    lead = jnp.where(rows < t - a, pltpu.roll(g_conv, t - a, 0), 0.0).astype(BF)
                    g_kept += dot(lead, bands[h, a * t : (a + 1) * t, :], NT)
                g_raw = jnp.where(allowed, g_kept, 0.0).astype(BF)
                g_q = dot(g_raw, split(qkv, row, 1, h)) * hd**-0.5
                g_k = dot(g_raw, split(qkv, row, 0, h), TN) * hd**-0.5
                g_qkv[row, :, h * hd : (h + 1) * hd] = g_q.astype(BF)
                g_qkv[row, :, width + h * hd : width + (h + 1) * hd] = g_k.astype(BF)

    in_copies = sum_copies(27, psend, r1, r2)
    product = lambda a, b, i: dot(pair_of(g_qkv, a, b), merge(w_first[pl.ds(i * part, part), :, 0 : 3 * quarter]), NT)
    sum_theirs(product, in_copies, psend)
    sum_ours(product, pown)
    sum_turn(in_copies, pown, r1)

    ag_drain(FIRST)
    for i, peer in enumerate((sibling, across, diagonal)):
        w_out_copy(peer, 9 + i).wait_send()
        d_out_copy(peer, 24 + i).wait_recv()
    own_d_out.wait()

    @pl.loop(0, 4)
    def _(i):
        p = in_turn(i)
        at = pl.ds(pl.multiple_of(p * quarter, quarter), quarter)
        value = dot(attn_in[:, :, at].reshape(tokens, quarter), g_qkv[...].reshape(tokens, 3 * quarter), TN)
        w_first[pl.ds(p * part, part), :, 0 : 3 * quarter] = value.reshape(part, w_first.shape[1], 3 * quarter).astype(BF)
        w_first[pl.ds(p * part, part), :, 3 * quarter :] = d_out_in[pl.ds(p * part, part)]
        send_side(FIRST, p)

    total = sum_end(in_copies, pown, r2)
    value = x_ref[...].astype(F32)
    scale = lax.rsqrt(mean_of(value * value) + 1e-06)
    normed = value * scale
    prod = total * normed
    g_first = row_sum(prod)
    mean = mean_of(prod * gain_first[...])
    grad_in_ref[...] = (g_middle[...] + scale * (total * gain_first[...] - normed * mean)).astype(BF)

    sum_turn(out_copies, pown2, r1b)
    total = sum_end(out_copies, pown2, r2b)
    mlp_part = valid_ref[...] * total
    value = middle[...] + mlp_part
    out_ref[...] = value.astype(BF)
    stat_out = jnp.sum(row_sum(valid_ref[...] * value * value), axis=1, keepdims=True)
    stat_mlp = jnp.sum(row_sum(mlp_part * mlp_part), axis=1, keepdims=True)

    strips = d // 128
    small_ref[...] = jnp.zeros_like(small_ref)
    for i in range(strips):
        at = slice(128 * i, 128 * (i + 1))
        small_ref[i : i + 1, :] = g_first[:, at]
        small_ref[strips + i : strips + i + 1, :] = g_second[:, at]
    own_gain = row_sum((g_hin[...] * hat[...]).reshape(tokens, width))
    for i in range(width // 128):
        small_ref[pl.ds(2 * strips + me * (width // 128) + i, 1), :] = own_gain[:, 128 * i : 128 * (i + 1)]
    base = 3 * strips
    for h in range(heads):
        for a in range(taps):
            tile = corr[h, a * t : (a + 1) * t, :]
            for b in range(span):
                lanes[a * span + b : a * span + b + 1, :] = row_sum(jnp.where(diff == b, tile, 0.0))
        small_ref[pl.ds(base + me * heads + h, 1), :] = row_sum(jnp.transpose(lanes[...]))
    base += 4 * heads
    lanes[0 : 2 * heads, :] = g_mix[...]
    lanes[2 * heads :, :] = jnp.zeros((t - 2 * heads, t), F32)
    small_ref[pl.ds(base + me, 1), :] = row_sum(jnp.transpose(lanes[...]))
    base += 4
    lane = lax.broadcasted_iota(jnp.int32, (1, 128), 1)
    count = jnp.sum(row_sum(jnp.broadcast_to(valid_ref[...], (t, 128))), axis=1, keepdims=True) * (1.0 / 128.0)
    stats = jnp.zeros((1, 128), F32)
    for i, stat in enumerate((stat_out, stat_attn, stat_mlp, count)):
        stats = jnp.where(lane == i, stat, stats)
    small_ref[base : base + 1, :] = stats

    peers = [(sibling, f), (across, f)] + [(me, flip(bit)) for bit in bits]

    def small_copy(i):
        return pltpu.make_async_remote_copy(
            src_ref=small_send.at[i], dst_ref=small_recv.at[i],
            send_sem=rep_send.at[40 + i], recv_sem=rep_recv.at[40 + i],
            device_id=peers[i], device_id_type=MESH,
        )

    def small_step(i):
        small_send[i] = small_ref[...]
        small_copy(i).start()

    def small_take(i):
        small_copy(i).wait_recv()
        small_ref[...] = small_ref[...] + small_recv[i]

    rs_close(DOWN)
    final_start(DOWN, 30)
    pl.loop(1, lines)(lambda s: rs_turn(MLP, s))
    final_pass(DOWN, 30)
    small_step(0)
    for i in range(len(peers)):
        small_take(i)
        if i + 1 < len(peers):
            small_step(i + 1)
    rs_turn(FIRST, 1)
    rs_close(MLP)
    final_start(MLP, 33)
    pl.loop(2, lines)(lambda s: rs_turn(FIRST, s))
    final_pass(MLP, 33)
    rs_close(FIRST)
    final_start(FIRST, 36)
    final_pass(FIRST, 36)
    for k in range(3):
        final_end(k, (36, 33, 30)[k])
    for k in range(3):
        rs_drain(k)
    for i in range(len(peers)):
        small_copy(i).wait_send()
    for i, peer in enumerate((sibling, across, diagonal)):
        d_out_copy(peer, 24 + i).wait_send()


def run_layer(cfg, x, g, seg, valid, gains, score, mix, shards_in):
    heads, hd, taps, span, docs, shards, units = cfg
    t, d = x.shape
    width = heads * hd
    first, mlp, down = shards_in
    bits = shards.bit_length() - 1

    def shape(dtype, *dims):
        return jax.ShapeDtypeStruct(dims, dtype)

    v = pltpu.VMEM
    dma = pltpu.SemaphoreType.DMA
    out_shape = (
        shape(BF, t, d), shape(BF, t, d), shape(F32, 64, 128),
        *(shape(BF, 4, *s.shape) for s in shards_in),
    )
    scratch = [
        *(v((shards, *s.shape), BF) for s in shards_in),
        v((4, t, d), BF), v((4, t, d), BF), v((4, 8, t), F32), v((4, t, d), BF), v((4, t, 3 * width), BF),
        v((4, t, width), F32), v((4, t, 128), F32), v((4, heads, t, t), F32), v((4, heads, t, t), BF),
        v((4, t, width), BF), v((shards // 4, first.shape[0], d), BF),
        v((t, d), F32), v((4 * t, units), BF), v((4 * t, units), BF), v((4, t, units), BF), v((4, t, 2 * units), BF),
        v((4, t, d), BF), v((t, d), F32), v((4, t, 3 * width), BF), v((4, t, width), F32),
        v((shards, first.shape[0], width), BF),
        v((2, t, d), BF), v((2, t, d), BF), v((2, t, d), BF), v((t, d), BF), v((t, d), BF),
        v((2, t, d), BF), v((2, t, d), BF), v((2, t, d), BF), v((t, d), BF),
        v((heads, taps * t, t), BF), v((heads, taps * t, t), F32), v((t, width), F32), v((t, t), F32), v((2 * heads, t), F32),
        *(v((shards // 2, *s.shape), BF) for s in shards_in + shards_in), v((2 + bits, 64, 128), F32), v((2 + bits, 64, 128), F32),
        dma((3, 3, shards)), dma((3, shards)), dma((3, 2, shards // 2)), dma((3, 2, shards // 2)), dma((48,)), dma((48,)), dma((8,)), pltpu.SemaphoreType.REGULAR,
    ]
    return pl.pallas_call(
        functools.partial(layer_kernel, cfg),
        out_shape=out_shape,
        in_specs=[vmem_spec()] * 7 + [smem_spec()] * 2 + [hbm_spec()] * 3,
        out_specs=(vmem_spec(),) * 3 + (hbm_spec(),) * 3,
        scratch_shapes=scratch,
        compiler_params=pltpu.CompilerParams(
            collective_id=0, has_side_effects=True, vmem_limit_bytes=VMEM_LIMIT
        ),
    )(x, g, seg, valid, *gains, score, mix, *shards_in)


def widen_kernel(strip, count, first_ref, mlp_ref, down_ref, *outs):
    quarter = first_ref.shape[2] // 4
    for r in range(4):
        for k in range(4):
            outs[k][:, r * quarter : (r + 1) * quarter] = first_ref[r, :, k * quarter : (k + 1) * quarter].astype(F32)
        outs[6][r] = down_ref[r].astype(F32)
        for k in range(2):
            for i in range(count):
                at = (4 * i + r) * strip
                outs[4 + k][:, at : at + strip] = mlp_ref[r, :, (k * count + i) * strip : (k * count + i + 1) * strip].astype(F32)


def widen(first, mlp, down, strip, count):
    _, rows, d = first.shape
    steps = 4 if rows % 64 == 0 and down.shape[1] % 64 == 0 else 1
    hidden = 4 * strip * count
    rows_step, down_step = rows // steps, down.shape[1] // steps

    def taken(array, size):
        return pl.BlockSpec((4, size, array.shape[2]), lambda i: (0, i, 0))

    def given(size, width):
        return pl.BlockSpec((size, width), lambda i: (i, 0))

    return pl.pallas_call(
        functools.partial(widen_kernel, strip, count),
        grid=(steps,),
        out_shape=tuple(jax.ShapeDtypeStruct((rows, d), F32) for _ in range(4))
        + tuple(jax.ShapeDtypeStruct((rows, hidden), F32) for _ in range(2))
        + (jax.ShapeDtypeStruct(down.shape, F32),),
        in_specs=[taken(first, rows_step), taken(mlp, rows_step), taken(down, down_step)],
        out_specs=tuple(given(rows_step, d) for _ in range(4))
        + tuple(given(rows_step, hidden) for _ in range(2))
        + (taken(down, down_step),),
        compiler_params=pltpu.CompilerParams(vmem_limit_bytes=VMEM_LIMIT),
    )(first, mlp, down)


def per_device(
    hidden_in,
    doc_lengths,
    w_query,
    w_key,
    w_value,
    w_output,
    w_gate,
    w_up,
    w_down,
    attn_norm,
    mlp_norm,
    head_norm,
    score_kernel,
    head_mixing,
    grad_out,
):
    _, t, d = hidden_in.shape
    reps = lax.axis_size("rep")
    shards = lax.axis_size("fsdp")
    me = lax.axis_index("rep")
    hidden = w_gate.shape[1]
    heads = H // reps
    hd = d // H
    quarter = d // reps
    units = hidden // reps
    strip = units // shards
    taps, span = score_kernel.shape[1:]
    docs = doc_lengths.shape[1] - 1
    rows_here = w_gate.shape[0]

    def mine(array, size, axis):
        return lax.dynamic_slice_in_dim(array, me * size, size, axis)

    def strips(w):
        return mine(w.reshape(rows_here, shards, reps, strip), 1, 2).reshape(rows_here, units)

    first_shard = jnp.concatenate([mine(w, quarter, 1) for w in (w_query, w_key, w_value, w_output)], axis=1)
    mlp_shard = jnp.concatenate([strips(w_gate), strips(w_up)], axis=1)
    down_shard = mine(w_down, strip, 0)

    boundary = jnp.cumsum(doc_lengths[:, :-1], axis=1)
    places = jnp.arange(t, dtype=jnp.int32)
    seg_ids = jnp.sum((places[None, :, None] >= boundary[:, None, :]).astype(jnp.int32), axis=2)
    seg_own = jnp.broadcast_to(seg_ids.astype(F32), (8, t))
    valid = (seg_ids < docs).astype(F32).reshape(t, 1)
    gains = (attn_norm.reshape(1, d), mlp_norm.reshape(1, d), mine(head_norm, quarter, 0).reshape(1, quarter))
    score = mine(score_kernel.reshape(H, taps * span), heads, 0)
    mix = mine(head_mixing, heads, 0)
    cfg = (heads, hd, taps, span, docs, shards, units)
    block_out, grad_in, small, a_first, a_mlp, a_down = run_layer(
        cfg, hidden_in.reshape(t, d), grad_out.reshape(t, d), seg_own, valid, gains, score, mix,
        (first_shard, mlp_shard, down_shard),
    )

    lines = d // 128
    base = 3 * lines
    small_score = small[base : base + H, : taps * span]
    base += H
    small_mix = small[base : base + reps, : 2 * heads]
    stats = small[base + reps, :STATS]
    root_means = jnp.sqrt(stats[:3] / (stats[3] * d))

    if strip % 128 == 0:
        g_q, g_k, g_v, g_o, g_gate, g_up, g_down = widen(a_first, a_mlp, a_down, strip, shards)
    else:
        first = a_first.astype(F32).reshape(reps, rows_here, 4, quarter)
        first = jnp.moveaxis(first, 0, 2).reshape(rows_here, 4, d)
        g_q, g_k, g_v, g_o = (first[:, k] for k in range(4))
        mlp = a_mlp.astype(F32).reshape(reps, rows_here, 2, shards, strip)
        mlp = jnp.moveaxis(mlp, 0, 3).reshape(rows_here, 2, hidden)
        g_gate, g_up = mlp[:, 0], mlp[:, 1]
        g_down = a_down.astype(F32)
    return (
        block_out.reshape(hidden_in.shape),
        grad_in.reshape(hidden_in.shape),
        g_q,
        g_k,
        g_v,
        g_o,
        g_gate,
        g_up,
        g_down.reshape(w_down.shape),
        small[:lines].reshape(d),
        small[lines : 2 * lines].reshape(d),
        small[2 * lines : 3 * lines].reshape(d),
        small_score.reshape(score_kernel.shape),
        small_mix.reshape(head_mixing.shape),
        root_means,
    )


def solution(mesh):
    rows = P(("rep", "fsdp"), None, None)
    split = P("fsdp", None)
    placed = (rows, P(("rep", "fsdp"), None)) + (split,) * 7 + (P(),) * 5 + (rows,)
    return jax.shard_map(
        per_device,
        mesh=mesh,
        in_specs=placed,
        out_specs=(rows, rows) + (split,) * 7 + (P(),) * 6,
        check_vma=False,
    )
```

```python
import functools

import jax
import jax.numpy as jnp
from jax import lax
from jax.experimental import pallas as pl
from jax.experimental.pallas import tpu as pltpu
from jax.sharding import PartitionSpec as P

H = 16
BF = jnp.bfloat16
F32 = jnp.float32
MESH = pl.DeviceIdType.MESH
VMEM_LIMIT = 62 * 1024 * 1024
NN = (((1,), (0,)), ((), ()))
NT = (((1,), (1,)), ((), ()))
TN = (((0,), (0,)), ((), ()))
FIRST, MLP, DOWN = 0, 1, 2
UP, DN, SIDE = 0, 1, 2
STATS = 4


def dot(a, b, dims=NN):
    return lax.dot_general(a, b, dims, preferred_element_type=F32)


def merge(value):
    n, rows, width = value.shape
    if rows % 16 == 0:
        return value.reshape(n * rows, width)
    return value.astype(F32).reshape(n * rows, width).astype(value.dtype)


def vmem_spec():
    return pl.BlockSpec(memory_space=pltpu.VMEM)


def smem_spec():
    return pl.BlockSpec(memory_space=pltpu.SMEM)


def hbm_spec():
    return pl.BlockSpec(memory_space=pl.ANY)


def grids(t):
    rows = lax.broadcasted_iota(jnp.int32, (t, t), 0)
    cols = lax.broadcasted_iota(jnp.int32, (t, t), 1)
    return rows, cols


def allowed_of(seg_row, rows, cols):
    t = rows.shape[0]
    along = jnp.broadcast_to(seg_row, (t, t))
    return (along == jnp.transpose(along)) & (cols <= rows)


def lagged(masked, taps, rows):
    parts = [masked.astype(BF)]
    for a in range(1, taps):
        parts.append(jnp.where(rows >= a, pltpu.roll(masked, a, 0), 0.0).astype(BF))
    return jnp.concatenate(parts, axis=1)


def row_sum(value):
    return jnp.sum(value, axis=0, keepdims=True)


def mean_of(value):
    return jnp.mean(value, axis=1, keepdims=True)


def layer_kernel(cfg, *refs):
    heads, hd, taps, span, docs, shards, units = cfg
    strip = units // shards
    mlp_parts = 2 if strip % 128 == 0 else 1
    given, refs = refs[: 13 + mlp_parts], refs[13 + mlp_parts :]
    x_ref, g_ref, first_norm, second_norm, head_norm, docs_ref, score_ref, mix_ref = given[:8]
    own_first, own_down, own_mlp = given[8:12], given[12], given[13:]
    (
        out_ref, grad_in_ref, grad_first_norm, grad_second_norm, grad_head_norm, grad_score, grad_mix, means,
        all_first, all_mlp, all_down,
        w_first, w_mlp, w_down, wide, g_mlp, seg_all, attn_in, qkv, hat, inv, probs, masked, head_in, w_out,
        middle, slope, silu, hidden, g_gu, g_attn, g_middle, g_qkv, g_hin, d_out_in,
        psend, pown, r1, ysend, r2, psend2, pown2, r1b, r2b, bands, corr, g_wide, lanes, g_mix,
        x_first, x_mlp, x_down, z_first, z_mlp, z_down, small_send, small_recv, small_ref, valid_ref, gain_first, gain_second, gain_all, gain_head,
        ag_send, ag_recv, rs_send, rs_recv, rep_send, rep_recv, local, credit,
    ) = refs
    t, d = x_ref.shape
    width = heads * hd
    quarter = d // 4
    lines = shards // 2
    me = lax.axis_index("rep")
    f = lax.axis_index("fsdp")
    plane, core = me // 2, me % 2
    sibling, across = plane * 2 + (1 - core), (1 - plane) * 2 + core
    diagonal = (1 - plane) * 2 + (1 - core)
    z, side = f // 2, f % 2
    partner = 2 * z + (1 - side)
    weights = (w_first, w_mlp, w_down)
    x_lands, z_lands = (x_first, x_mlp, x_down), (z_first, z_mlp, z_down)
    peer_of = (f + 2, f - 2, partner)
    tokens = 4 * t
    part = shards // 4
    rows, cols = grids(t)

    def flip(bit):
        return f + (1 - 2 * ((f // bit) % 2)) * bit

    bits = []
    bit = 1
    while bit < shards:
        bits.append(bit)
        bit *= 2

    barrier = pltpu.get_barrier_semaphore()

    def greet(r, s):
        pl.semaphore_signal(barrier, inc=1, device_id=(r, s), device_id_type=MESH)

    for r in (sibling, across, diagonal):
        greet(r, f)
    greet(me, partner)

    @pl.loop(1, lines)
    def _(s):
        greet(me, 2 * ((z + s) % lines) + side)

    pl.semaphore_wait(barrier, 3 + lines)

    def rep_copy(src, dst, slot, peer):
        return pltpu.make_async_remote_copy(
            src_ref=src, dst_ref=dst, send_sem=rep_send.at[slot], recv_sem=rep_recv.at[slot],
            device_id=(peer, f), device_id_type=MESH,
        )

    def ag(k, block, way):
        return pltpu.make_async_remote_copy(
            src_ref=weights[k].at[block], dst_ref=weights[k].at[block],
            send_sem=ag_send.at[k, way, block], recv_sem=ag_recv.at[k, block],
            device_id=(me, peer_of[way]), device_id_type=MESH,
        )

    def ag_walk(k, s, first, act):
        sides = (side, 1 - side) if k == DOWN else (side,)
        if isinstance(s, int) and s == 0:
            for q in sides:
                block = 2 * z + q
                if k == DOWN and q is not side:
                    first(k, block)

                @pl.when(z < lines - 1)
                def _():
                    act(k, block, UP)

                @pl.when(z > 0)
                def _():
                    act(k, block, DN)

                if k != DOWN:
                    act(k, block, SIDE)
            return

        @pl.when(z - s >= 0)
        def _():
            for q in sides:
                block = 2 * (z - s) + q
                first(k, block)

                @pl.when(z < lines - 1)
                def _():
                    act(k, block, UP)

                if k != DOWN:
                    act(k, block, SIDE)

        @pl.when(z + s < lines)
        def _():
            for q in sides:
                block = 2 * (z + s) + q
                first(k, block)

                @pl.when(z > 0)
                def _():
                    act(k, block, DN)

                if k != DOWN:
                    act(k, block, SIDE)

    def arrived(k, block):
        ag(k, block, SIDE).wait_recv()

    def go(k, block, way):
        ag(k, block, way).start()

    def gone(k, block, way):
        ag(k, block, way).wait_send()

    def ag_steps(k, low, high):
        if low == 0:
            ag_walk(k, 0, arrived, go)
        else:
            pl.loop(low, high)(lambda s: ag_walk(k, s, arrived, go))

    def ag_done(k):
        if k != DOWN:
            pl.loop(0, lines)(lambda zz: arrived(k, 2 * zz + (1 - side)))

    def ag_drain(k):
        nothing = lambda *_: None
        if k == DOWN:
            gone(k, f, SIDE)
        ag_walk(k, 0, nothing, gone)
        pl.loop(1, lines)(lambda s: ag_walk(k, s, nothing, gone))

    def gather_start(fulls, slot):
        for i, full in enumerate(fulls):
            rep_copy(full.at[me], full.at[me], slot + 3 * i, across).start()
            rep_copy(full.at[me], full.at[me], slot + 3 * i + 1, sibling).start()

    def gather_pass(fulls, slot):
        for i, full in enumerate(fulls):
            rep_copy(full.at[me], full.at[me], slot + 3 * i, across).wait_recv()
            rep_copy(full.at[across], full.at[across], slot + 3 * i + 2, sibling).start()

    def gather_end(fulls, slot):
        for i, full in enumerate(fulls):
            rep_copy(full.at[me], full.at[me], slot + 3 * i + 1, sibling).wait_recv()
            rep_copy(full.at[across], full.at[across], slot + 3 * i + 2, sibling).wait_recv()
        for i, full in enumerate(fulls):
            rep_copy(full.at[me], full.at[me], slot + 3 * i, across).wait_send()
            rep_copy(full.at[me], full.at[me], slot + 3 * i + 1, sibling).wait_send()
            rep_copy(full.at[across], full.at[across], slot + 3 * i + 2, sibling).wait_send()

    def pair_of(ref, a, b):
        return jnp.concatenate([ref[a], ref[b]], axis=0)

    def sum_copies(slot, send_buf, first_land, second_land):
        return (
            rep_copy(send_buf, first_land, slot, sibling),
            rep_copy(ysend, second_land, slot + 1, across),
        )

    def column_chunk(i):
        return pl.ds(pl.multiple_of(i * quarter, quarter), quarter)

    def sum_theirs(product, copies, send_buf):
        @pl.loop(0, 4)
        def _(i):
            value = product(1 - core, 2 + (1 - core), i)
            send_buf[0, :, column_chunk(i)] = value[:t].astype(BF)
            send_buf[1, :, column_chunk(i)] = value[t:].astype(BF)

        copies[0].start()

    def sum_ours(product, own_buf):
        @pl.loop(0, 4)
        def _(i):
            value = product(across, me, i)
            own_buf[0, :, column_chunk(i)] = value[:t].astype(own_buf.dtype)
            own_buf[1, :, column_chunk(i)] = value[t:].astype(own_buf.dtype)

    def sum_turn(copies, own_buf, first_land):
        copies[0].wait_recv()
        ysend[...] = (own_buf[0].astype(F32) + first_land[1 - plane].astype(F32)).astype(BF)
        copies[1].start()
        own_buf[1] = (own_buf[1].astype(F32) + first_land[plane].astype(F32)).astype(own_buf.dtype)

    def sum_end(copies, own_buf, second_land):
        copies[1].wait_recv()
        total = own_buf[1].astype(F32) + second_land[...].astype(F32)
        copies[0].wait_send()
        copies[1].wait_send()
        return total

    def rs_side(k, zz):
        source = weights[k].at[2 * zz + (1 - side)]
        if k == DOWN:
            source = x_mlp.at[zz, pl.ds(0, strip), pl.ds(0, d)]
        return pltpu.make_async_remote_copy(
            src_ref=source, dst_ref=x_lands[k].at[zz],
            send_sem=rs_send.at[k, 0, zz], recv_sem=rs_recv.at[k, 0, zz],
            device_id=(me, partner), device_id_type=MESH,
        )

    def rs_owner(k, zz):
        return pltpu.make_async_remote_copy(
            src_ref=weights[k].at[2 * zz + side], dst_ref=z_lands[k].at[z],
            send_sem=rs_send.at[k, 1, zz], recv_sem=rs_recv.at[k, 1, z],
            device_id=(me, 2 * zz + side), device_id_type=MESH,
        )

    def rs_from(k, zz):
        return pltpu.make_async_remote_copy(
            src_ref=weights[k].at[2 * zz + side], dst_ref=z_lands[k].at[zz],
            send_sem=rs_send.at[k, 1, zz], recv_sem=rs_recv.at[k, 1, zz],
            device_id=(me, 2 * zz + side), device_id_type=MESH,
        )

    def rs_add(k, block, landed):
        grad = weights[k]
        high = grad.shape[1]
        step = 16 if high % 16 == 0 else high

        @pl.loop(0, high // step)
        def _(i):
            at = pl.ds(pl.multiple_of(i * step, step), step)
            total = grad[block, at, :].astype(F32)
            for land, slot in landed:
                total = total + land[slot, at, :].astype(F32)
            grad[block, at, :] = total.astype(BF)

    def after(s):
        return (z + s) % lines

    def rs_turn(k, s):
        zz = after(s)
        rs_side(k, zz).wait_recv()
        rs_add(k, 2 * zz + side, [(x_lands[k], zz)])
        rs_owner(k, zz).start()

    def rs_close(k):
        rs_side(k, z).wait_recv()
        landed = [(x_lands[k], z)]
        for s in range(1, lines):
            rs_from(k, after(s)).wait_recv()
            landed.append((z_lands[k], after(s)))
        rs_add(k, f, landed)

    def rs_drain(k):
        if k != DOWN:
            pl.loop(0, lines)(lambda s: rs_side(k, after(s)).wait_send())

        @pl.loop(1, lines)
        def _(s):
            rs_owner(k, after(s)).wait_send()

    outs = (all_first, all_mlp, all_down)

    def final_copies(k, slot):
        own = weights[k].at[f]
        full = outs[k]
        return (
            rep_copy(own, full.at[me], slot, across),
            rep_copy(own, full.at[me], slot + 1, sibling),
            rep_copy(full.at[across], full.at[across], slot + 2, sibling),
            pltpu.make_async_copy(own, full.at[me], local.at[1 + k]),
        )

    def final_start(k, slot):
        a, b, _, here = final_copies(k, slot)
        a.start()
        b.start()
        here.start()

    def final_pass(k, slot):
        a, _, c, _ = final_copies(k, slot)
        a.wait_recv()
        c.start()

    def final_end(k, slot):
        a, b, c, here = final_copies(k, slot)
        b.wait_recv()
        c.wait_recv()
        a.wait_send()
        b.wait_send()
        c.wait_send()
        here.wait()

    def cut(ref, at, size):
        return ref.at[:, pl.ds(pl.multiple_of(at, size), size)]

    sources = [
        [(cut(own_first[i], me * quarter, quarter), w_first.at[f, :, pl.ds(i * quarter, quarter)]) for i in range(4)],
        [(own_mlp[0], w_mlp.at[f])],
        [(own_down.at[pl.ds(pl.multiple_of(me * strip, strip), strip), :], w_down.at[f])],
    ]
    if mlp_parts == 2:
        sources[MLP] = [
            (cut(own_mlp[i // shards], (4 * (i % shards) + me) * strip, strip), w_mlp.at[f, :, pl.ds(i * strip, strip)])
            for i in range(2 * shards)
        ]
    loads, used = [], 4
    for pairs in sources:
        loads.append([pltpu.make_async_copy(a, b, local.at[used + i]) for i, (a, b) in enumerate(pairs)])
        used += len(pairs)
    for k in range(3):
        for load in loads[k]:
            load.start()

    def load_wait(k):
        for load in loads[k]:
            load.wait()

    lane = lax.broadcasted_iota(jnp.int32, (1, t), 1)
    seg = jnp.zeros((1, t), F32)
    edge = 0
    for i in range(docs):
        edge = edge + docs_ref[0, i]
        seg = seg + jnp.where(lane >= edge, 1.0, 0.0)
    valid = jnp.where(jnp.transpose(jnp.broadcast_to(seg, (t, t))) < float(docs), 1.0, 0.0)
    valid_ref[...] = valid[:, 0:1]

    def as_row(ref):
        return jnp.concatenate([ref[i : i + 1, :] for i in range(ref.shape[0])], axis=1)

    gain_first[...] = as_row(first_norm)
    gain_second[...] = as_row(second_norm)
    gain_all[...] = as_row(head_norm)
    gain_head[...] = gain_all[:, pl.ds(pl.multiple_of(me * quarter, quarter), quarter)]
    wide[me] = x_ref[...]
    g_mlp[me] = g_ref[...]
    seg_all[me] = jnp.broadcast_to(seg, (8, t))
    entering = (seg_all, wide, g_mlp)
    gather_start(entering, 0)
    load_wait(FIRST)
    ag_steps(FIRST, 0, 1)

    diff = cols - rows + (span - 1) // 2

    @pl.loop(0, heads)
    def _(h):
        for a in range(taps):
            band = jnp.zeros((t, t), F32)
            for b in range(span):
                band = jnp.where(diff == b, score_ref[me * heads + h, a, b], band)
            bands[h, a * t : (a + 1) * t, :] = band.astype(BF)

    gather_pass(entering, 0)
    ag_steps(FIRST, 1, 2)
    load_wait(DOWN)
    ag(DOWN, f, SIDE).start()
    gather_end(entering, 0)

    @pl.loop(0, 4)
    def _(r):
        value = wide[r].astype(F32)
        scale = lax.rsqrt(mean_of(value * value) + 1e-06)
        attn_in[r] = (value * scale * gain_first[...]).astype(BF)
        valid = jnp.transpose(jnp.broadcast_to(seg_all[r][0:1, :], (t, t)))[:, 0:1] < float(docs)
        g_mlp[r] = jnp.where(valid, g_mlp[r].astype(F32), 0.0).astype(BF)

    ag_steps(FIRST, 2, 3)
    load_wait(MLP)
    ag_steps(MLP, 0, 1)
    ag_steps(FIRST, 3, lines)
    ag_steps(MLP, 1, 2)
    ag_done(FIRST)

    def w_out_copy(peer, slot):
        return rep_copy(
            w_first.at[pl.ds(peer * part, part), :, pl.ds(3 * quarter, quarter)],
            w_out.at[:, :, pl.ds(pl.multiple_of(me * quarter, quarter), quarter)],
            slot, peer,
        )

    for i, peer in enumerate((sibling, across, diagonal)):
        w_out_copy(peer, 9 + i).start()
    own_out = pltpu.make_async_copy(
        w_first.at[pl.ds(me * part, part), :, pl.ds(3 * quarter, quarter)],
        w_out.at[:, :, pl.ds(pl.multiple_of(me * quarter, quarter), quarter)],
        local.at[0],
    )
    own_out.start()

    for i in range(3):
        value = dot(attn_in[...].reshape(tokens, d), merge(w_first[:, :, i * quarter : (i + 1) * quarter]))
        qkv[:, :, i * quarter : (i + 1) * quarter] = value.astype(BF).reshape(4, t, quarter)
    ag_steps(MLP, 2, 3)
    ag_steps(DOWN, 0, 1)

    def split(ref, row, kind, h):
        return ref[row, :, kind * width + h * hd : kind * width + (h + 1) * hd]

    @pl.loop(0, 4)
    def _(row):
        allowed = allowed_of(seg_all[row][0:1, :], rows, cols)
        for pair in range(heads // 2):
            both = []
            for c in range(2):
                h = 2 * pair + c
                scores = dot(split(qkv, row, 0, h), split(qkv, row, 1, h), NT) * hd**-0.5
                kept = jnp.where(allowed, scores, 0.0)
                masked[row, h] = kept.astype(BF)
                logits = jnp.where(allowed, dot(lagged(kept, taps, rows), bands[h]), -1e30)
                e = jnp.exp(logits - jnp.max(logits, axis=1, keepdims=True))
                p = e / jnp.sum(e, axis=1, keepdims=True)
                probs[row, h] = p
                both.append(p)
            for e in range(2):
                h = 2 * pair + e
                mixed = (mix_ref[me * heads + h, 0] * both[0] + mix_ref[me * heads + h, 1] * both[1]).astype(BF)
                out = dot(mixed, split(qkv, row, 2, h))
                centred = out - mean_of(out)
                scale = lax.rsqrt(mean_of(centred * centred) + 1e-05)
                hat[row, :, h * hd : (h + 1) * hd] = centred * scale
                inv[row, :, h : h + 1] = scale
        head_in[row] = (hat[row] * gain_head[...]).astype(BF)

    for i, peer in enumerate((sibling, across, diagonal)):
        w_out_copy(peer, 9 + i).wait_recv()
    own_out.wait()

    copies = sum_copies(12, psend, r1, r2)
    product = lambda a, b, i: dot(pair_of(head_in, a, b), merge(w_out[:, :, column_chunk(i)]))
    sum_theirs(product, copies, psend)
    sum_ours(product, pown)
    ag_steps(MLP, 3, lines)
    sum_turn(copies, pown, r1)
    total = sum_end(copies, pown, r2)
    attn_part = valid_ref[...] * total
    value = x_ref[...].astype(F32) + attn_part
    middle[...] = value
    stat_attn = jnp.sum(row_sum(attn_part * attn_part), axis=1, keepdims=True)
    scale = lax.rsqrt(mean_of(value * value) + 1e-06)
    wide[me] = (value * scale * gain_second[...]).astype(BF)
    gather_start((wide,), 14)
    ag_steps(DOWN, 1, 2)
    gather_pass((wide,), 14)
    gather_end((wide,), 14)
    mlp_in = wide
    ag_steps(DOWN, 2, 3)
    ag_done(MLP)

    chunk = 256

    @pl.loop(0, units // chunk)
    def _(i):
        at = pl.ds(pl.multiple_of(i * chunk, chunk), chunk)
        after = pl.ds(pl.multiple_of(units + i * chunk, chunk), chunk)
        operand = mlp_in[...].reshape(tokens, d)
        gate = dot(operand, merge(w_mlp[:, :, at]))
        upper = dot(operand, merge(w_mlp[:, :, after]))
        sig = 1.0 / (1.0 + jnp.exp(-gate))
        act = gate * sig
        hidden[:, :, at] = (act * upper).astype(BF).reshape(4, t, chunk)
        silu[:, at] = act.astype(BF)
        slope[:, at] = (upper * sig * (1.0 + gate * (1.0 - sig))).astype(BF)

    @pl.loop(0, 4)
    def _(i):
        span_units = units // 4
        at = pl.ds(pl.multiple_of(i * span_units, span_units), span_units)
        value = dot(hidden[:, :, at].reshape(tokens, span_units), g_mlp[...].reshape(tokens, d), TN)
        value = value.reshape(part, strip, d)
        for j in range(part // 2):
            half = jnp.where(side == 0, value[2 * j + 1], value[2 * j])
            x_mlp[i * (part // 2) + j, 0:strip, 0:d] = half.astype(BF)

    @pl.loop(1, lines + 1)
    def _(s):
        rs_side(DOWN, after(s)).start()

    ag_steps(DOWN, 3, lines)

    @pl.loop(0, 4)
    def _(i):
        span_units = units // 4
        at = pl.ds(pl.multiple_of(i * span_units, span_units), span_units)
        after = pl.ds(pl.multiple_of(units + i * span_units, span_units), span_units)
        g_hidden = dot(g_mlp[...].reshape(tokens, d), merge(w_down[pl.ds(i * part, part)]), NT)
        g_gu[:, :, at] = (g_hidden * slope[:, at].astype(F32)).astype(BF).reshape(4, t, span_units)
        g_gu[:, :, after] = (g_hidden * silu[:, at].astype(F32)).astype(BF).reshape(4, t, span_units)

    mlp_copies = sum_copies(17, psend, r1, r2)
    product = lambda a, b, i: dot(pair_of(g_gu, a, b), merge(w_mlp[pl.ds(i * part, part)]), NT)
    sum_theirs(product, mlp_copies, psend)
    sum_ours(product, pown)

    out_copies = (rep_copy(psend2, r1b, 19, sibling), rep_copy(ysend, r2b, 20, across))
    product = lambda a, b, i: dot(pair_of(hidden, a, b), merge(w_down[:, :, column_chunk(i)]))
    sum_theirs(product, out_copies, psend2)
    sum_ours(product, pown2)
    sum_turn(mlp_copies, pown, r1)

    ag_drain(DOWN)

    @pl.loop(0, 4)
    def _(i):
        span_units = units // 4
        at = pl.ds(pl.multiple_of(i * span_units, span_units), span_units)
        value = dot(hidden[:, :, at].reshape(tokens, span_units), g_mlp[...].reshape(tokens, d), TN)
        w_down[pl.ds(i * part, part)] = value.reshape(part, w_down.shape[1], d).astype(BF)

    total = sum_end(mlp_copies, pown, r2)
    value = middle[...]
    scale = lax.rsqrt(mean_of(value * value) + 1e-06)
    normed = value * scale
    prod = total * normed
    g_second = row_sum(prod)
    mean = mean_of(prod * gain_second[...])
    value = g_ref[...].astype(F32) + scale * (total * gain_second[...] - normed * mean)
    g_middle[...] = value
    g_attn[me] = (valid_ref[...] * value).astype(BF)
    gather_start((g_attn,), 21)
    ag_drain(MLP)
    pl.loop(0, lines)(lambda s: rs_side(DOWN, after(s)).wait_send())
    pl.semaphore_signal(credit, inc=1, device_id=(me, partner), device_id_type=MESH)

    def in_turn(i):
        return (z // (part // 2) + 1 + i) % 4

    def send_side(k, p):
        @pl.loop(0, part // 2)
        def _(j):
            zz = p * (part // 2) + j
            rs_side(k, zz).start()

    @pl.loop(0, 4)
    def _(i):
        p = in_turn(i)
        at = pl.ds(pl.multiple_of(p * quarter, quarter), quarter)
        size = units // 2

        @pl.loop(0, 4)
        def _(j):
            to = pl.ds(pl.multiple_of(j * size, size), size)
            value = dot(mlp_in[:, :, at].reshape(tokens, quarter), g_gu[:, :, to].reshape(tokens, size), TN)
            w_mlp[pl.ds(p * part, part), :, to] = value.reshape(part, w_mlp.shape[1], size).astype(BF)


        @pl.when(i == 0)
        def _():
            pl.semaphore_wait(credit, 1)

        send_side(MLP, p)

    gather_pass((g_attn,), 21)
    gather_end((g_attn,), 21)

    value = dot(g_attn[...].reshape(tokens, d), merge(w_out[...]), NT)
    g_hin[...] = value.reshape(4, t, width)
    d_out = w_out

    @pl.loop(0, 4)
    def _(i):
        value = dot(head_in[...].reshape(tokens, width), g_attn[:, :, column_chunk(i)].reshape(tokens, quarter), TN)
        d_out[:, :, column_chunk(i)] = value.reshape(part, w_first.shape[1], quarter).astype(BF)


    def d_out_copy(peer, slot):
        return rep_copy(
            d_out.at[:, :, pl.ds(pl.multiple_of(peer * quarter, quarter), quarter)],
            d_out_in.at[pl.ds(me * part, part)],
            slot, peer,
        )

    for i, peer in enumerate((sibling, across, diagonal)):
        d_out_copy(peer, 24 + i).start()
    own_d_out = pltpu.make_async_copy(
        d_out.at[:, :, pl.ds(pl.multiple_of(me * quarter, quarter), quarter)],
        d_out_in.at[pl.ds(me * part, part)], local.at[4],
    )
    own_d_out.start()
    pl.loop(1, lines)(lambda s: rs_turn(DOWN, s))

    corr[...] = jnp.zeros_like(corr)
    g_mix[...] = jnp.zeros_like(g_mix)
    lanes[...] = jnp.zeros_like(lanes)

    @pl.loop(0, 4)
    def _(row):
        allowed = allowed_of(seg_all[row][0:1, :], rows, cols)
        g_wide[...] = g_hin[row] * gain_head[...]
        for pair in range(heads // 2):
            g_heads, g_mixed = [], []
            both = [probs[row, 2 * pair + c] for c in range(2)]
            for e in range(2):
                h = 2 * pair + e
                scaled = g_wide[:, h * hd : (h + 1) * hd]
                own_hat = hat[row, :, h * hd : (h + 1) * hd]
                g = inv[row, :, h : h + 1] * (scaled - mean_of(scaled) - own_hat * mean_of(scaled * own_hat))
                g = g.astype(BF)
                g_heads.append(g)
                g_mixed.append(dot(g, split(qkv, row, 2, h), NT))
            for e in range(2):
                h = 2 * pair + e
                mixed = (mix_ref[me * heads + h, 0] * both[0] + mix_ref[me * heads + h, 1] * both[1]).astype(BF)
                g_v = dot(mixed, g_heads[e], TN)
                g_qkv[row, :, 2 * width + h * hd : 2 * width + (h + 1) * hd] = g_v.astype(BF)
                for c in range(2):
                    place = (2 * pair + e) * 2 + c
                    g_mix[place : place + 1, :] += row_sum(g_mixed[e] * both[c])
            for c in range(2):
                h = 2 * pair + c
                g_probs = mix_ref[me * heads + 2 * pair, c] * g_mixed[0] + mix_ref[me * heads + 2 * pair + 1, c] * g_mixed[1]
                weighted = both[c] * g_probs
                g_conv = weighted - both[c] * jnp.sum(weighted, axis=1, keepdims=True)
                corr[h] += dot(lagged(masked[row, h].astype(F32), taps, rows), g_conv.astype(BF), TN)
                g_kept = dot(g_conv.astype(BF), bands[h, 0:t, :], NT)
                for a in range(1, taps):
                    lead = jnp.where(rows < t - a, pltpu.roll(g_conv, t - a, 0), 0.0).astype(BF)
                    g_kept += dot(lead, bands[h, a * t : (a + 1) * t, :], NT)
                g_raw = jnp.where(allowed, g_kept, 0.0).astype(BF)
                g_q = dot(g_raw, split(qkv, row, 1, h)) * hd**-0.5
                g_k = dot(g_raw, split(qkv, row, 0, h), TN) * hd**-0.5
                g_qkv[row, :, h * hd : (h + 1) * hd] = g_q.astype(BF)
                g_qkv[row, :, width + h * hd : width + (h + 1) * hd] = g_k.astype(BF)

    in_copies = sum_copies(27, psend, r1, r2)
    product = lambda a, b, i: dot(pair_of(g_qkv, a, b), merge(w_first[pl.ds(i * part, part), :, 0 : 3 * quarter]), NT)
    sum_theirs(product, in_copies, psend)
    sum_ours(product, pown)
    sum_turn(in_copies, pown, r1)

    ag_drain(FIRST)
    for i, peer in enumerate((sibling, across, diagonal)):
        w_out_copy(peer, 9 + i).wait_send()
        d_out_copy(peer, 24 + i).wait_recv()
    own_d_out.wait()

    @pl.loop(0, 4)
    def _(i):
        p = in_turn(i)
        at = pl.ds(pl.multiple_of(p * quarter, quarter), quarter)
        value = dot(attn_in[:, :, at].reshape(tokens, quarter), g_qkv[...].reshape(tokens, 3 * quarter), TN)
        w_first[pl.ds(p * part, part), :, 0 : 3 * quarter] = value.reshape(part, w_first.shape[1], 3 * quarter).astype(BF)
        w_first[pl.ds(p * part, part), :, 3 * quarter :] = d_out_in[pl.ds(p * part, part)]
        send_side(FIRST, p)

    total = sum_end(in_copies, pown, r2)
    value = x_ref[...].astype(F32)
    scale = lax.rsqrt(mean_of(value * value) + 1e-06)
    normed = value * scale
    prod = total * normed
    g_first = row_sum(prod)
    mean = mean_of(prod * gain_first[...])
    grad_in_ref[...] = (g_middle[...] + scale * (total * gain_first[...] - normed * mean)).astype(BF)

    sum_turn(out_copies, pown2, r1b)
    total = sum_end(out_copies, pown2, r2b)
    mlp_part = valid_ref[...] * total
    value = middle[...] + mlp_part
    out_ref[...] = value.astype(BF)
    stat_out = jnp.sum(row_sum(valid_ref[...] * value * value), axis=1, keepdims=True)
    stat_mlp = jnp.sum(row_sum(mlp_part * mlp_part), axis=1, keepdims=True)

    strips = d // 128
    small_ref[...] = jnp.zeros_like(small_ref)
    for i in range(strips):
        at = slice(128 * i, 128 * (i + 1))
        small_ref[i : i + 1, :] = g_first[:, at]
        small_ref[strips + i : strips + i + 1, :] = g_second[:, at]
    own_gain = row_sum((g_hin[...] * hat[...]).reshape(tokens, width))
    for i in range(width // 128):
        small_ref[pl.ds(2 * strips + me * (width // 128) + i, 1), :] = own_gain[:, 128 * i : 128 * (i + 1)]
    base = 3 * strips
    for h in range(heads):
        for a in range(taps):
            tile = corr[h, a * t : (a + 1) * t, :]
            for b in range(span):
                lanes[a * span + b : a * span + b + 1, :] = row_sum(jnp.where(diff == b, tile, 0.0))
        small_ref[pl.ds(base + me * heads + h, 1), :] = row_sum(jnp.transpose(lanes[...]))
    base += 4 * heads
    lanes[0 : 2 * heads, :] = g_mix[...]
    lanes[2 * heads :, :] = jnp.zeros((t - 2 * heads, t), F32)
    small_ref[pl.ds(base + me, 1), :] = row_sum(jnp.transpose(lanes[...]))
    base += 4
    lane = lax.broadcasted_iota(jnp.int32, (1, 128), 1)
    count = jnp.sum(row_sum(jnp.broadcast_to(valid_ref[...], (t, 128))), axis=1, keepdims=True) * (1.0 / 128.0)
    stats = jnp.zeros((1, 128), F32)
    for i, stat in enumerate((stat_out, stat_attn, stat_mlp, count)):
        stats = jnp.where(lane == i, stat, stats)
    small_ref[base : base + 1, :] = stats

    peers = [(sibling, f), (across, f)] + [(me, flip(bit)) for bit in bits]

    def small_copy(i):
        return pltpu.make_async_remote_copy(
            src_ref=small_send.at[i], dst_ref=small_recv.at[i],
            send_sem=rep_send.at[40 + i], recv_sem=rep_recv.at[40 + i],
            device_id=peers[i], device_id_type=MESH,
        )

    def small_step(i):
        small_send[i] = small_ref[...]
        small_copy(i).start()

    def small_take(i):
        small_copy(i).wait_recv()
        small_ref[...] = small_ref[...] + small_recv[i]

    rs_close(DOWN)
    final_start(DOWN, 30)
    pl.loop(1, lines)(lambda s: rs_turn(MLP, s))
    final_pass(DOWN, 30)
    small_step(0)
    for i in range(len(peers)):
        small_take(i)
        if i + 1 < len(peers):
            small_step(i + 1)
    grad_first_norm[...] = small_ref[0:strips, :]
    grad_second_norm[...] = small_ref[strips : 2 * strips, :]
    grad_head_norm[...] = small_ref[2 * strips : 3 * strips, :]
    at = 3 * strips
    grad_score[...] = small_ref[at : at + 4 * heads, :]
    grad_mix[...] = small_ref[at + 4 * heads : at + 4 * heads + 4, :]
    sums = small_ref[at + 4 * heads + 4 : at + 4 * heads + 5, :]
    means[...] = jnp.sqrt(sums / (sums[:, 3:4] * float(d)))
    rs_turn(FIRST, 1)
    rs_close(MLP)
    final_start(MLP, 33)
    pl.loop(2, lines)(lambda s: rs_turn(FIRST, s))
    final_pass(MLP, 33)
    rs_close(FIRST)
    final_start(FIRST, 36)
    final_pass(FIRST, 36)
    for k in range(3):
        final_end(k, (36, 33, 30)[k])
    for k in range(3):
        rs_drain(k)
    for i in range(len(peers)):
        small_copy(i).wait_send()
    for i, peer in enumerate((sibling, across, diagonal)):
        d_out_copy(peer, 24 + i).wait_send()


def run_layer(cfg, vectors, scalars, first_in, down_in, mlp_in, sizes):
    heads, hd, taps, span, docs, shards, units = cfg
    t, d = vectors[0].shape
    width = heads * hd
    first, mlp, down = shards_in = sizes
    bits = shards.bit_length() - 1

    def shape(dtype, *dims):
        return jax.ShapeDtypeStruct(dims, dtype)

    v = pltpu.VMEM
    dma = pltpu.SemaphoreType.DMA
    out_shape = (
        shape(BF, t, d), shape(BF, t, d), *(shape(F32, d // 128, 128) for _ in range(3)),
        shape(F32, 4 * heads, 128), shape(F32, 4, 128), shape(F32, 1, 128),
        *(shape(BF, 4, *s.shape) for s in shards_in),
    )
    scratch = [
        *(v((shards, *s.shape), BF) for s in shards_in),
        v((4, t, d), BF), v((4, t, d), BF), v((4, 8, t), F32), v((4, t, d), BF), v((4, t, 3 * width), BF),
        v((4, t, width), F32), v((4, t, 128), F32), v((4, heads, t, t), F32), v((4, heads, t, t), BF),
        v((4, t, width), BF), v((shards // 4, first.shape[0], d), BF),
        v((t, d), F32), v((4 * t, units), BF), v((4 * t, units), BF), v((4, t, units), BF), v((4, t, 2 * units), BF),
        v((4, t, d), BF), v((t, d), F32), v((4, t, 3 * width), BF), v((4, t, width), F32),
        v((shards, first.shape[0], width), BF),
        v((2, t, d), BF), v((2, t, d), BF), v((2, t, d), BF), v((t, d), BF), v((t, d), BF),
        v((2, t, d), BF), v((2, t, d), BF), v((2, t, d), BF), v((t, d), BF),
        v((heads, taps * t, t), BF), v((heads, taps * t, t), F32), v((t, width), F32), v((t, t), F32), v((2 * heads, t), F32),
        *(v((shards // 2, *s.shape), BF) for s in shards_in + shards_in), v((2 + bits, 64, 128), F32), v((2 + bits, 64, 128), F32),
        v((64, 128), F32), v((t, 1), F32), v((1, d), F32), v((1, d), F32), v((1, d), F32), v((1, width), F32),
        dma((3, 3, shards)), dma((3, shards)), dma((3, 2, shards // 2)), dma((3, 2, shards // 2)), dma((48,)), dma((48,)), dma((10 + 2 * shards,)), pltpu.SemaphoreType.REGULAR,
    ]
    return pl.pallas_call(
        functools.partial(layer_kernel, cfg),
        out_shape=out_shape,
        in_specs=[vmem_spec()] * 5 + [smem_spec()] * 3 + [hbm_spec()] * (5 + len(mlp_in)),
        out_specs=(vmem_spec(),) * 8 + (hbm_spec(),) * 3,
        scratch_shapes=scratch,
        compiler_params=pltpu.CompilerParams(
            collective_id=0, has_side_effects=True, vmem_limit_bytes=VMEM_LIMIT
        ),
    )(*vectors, *scalars, *first_in, down_in, *mlp_in)


def widen_kernel(strip, count, first_ref, mlp_ref, down_ref, *outs):
    quarter = first_ref.shape[2] // 4
    for r in range(4):
        for k in range(4):
            outs[k][:, r * quarter : (r + 1) * quarter] = first_ref[r, :, k * quarter : (k + 1) * quarter].astype(F32)
        outs[6][r] = down_ref[r].astype(F32)
        for k in range(2):
            for i in range(count):
                at = (4 * i + r) * strip
                outs[4 + k][:, at : at + strip] = mlp_ref[r, :, (k * count + i) * strip : (k * count + i + 1) * strip].astype(F32)


def widen(first, mlp, down, strip, count):
    _, rows, d = first.shape
    steps = 4 if rows % 64 == 0 and down.shape[1] % 64 == 0 else 1
    hidden = 4 * strip * count
    rows_step, down_step = rows // steps, down.shape[1] // steps

    def taken(array, size):
        return pl.BlockSpec((4, size, array.shape[2]), lambda i: (0, i, 0))

    def given(size, width):
        return pl.BlockSpec((size, width), lambda i: (i, 0))

    return pl.pallas_call(
        functools.partial(widen_kernel, strip, count),
        grid=(steps,),
        out_shape=tuple(jax.ShapeDtypeStruct((rows, d), F32) for _ in range(4))
        + tuple(jax.ShapeDtypeStruct((rows, hidden), F32) for _ in range(2))
        + (jax.ShapeDtypeStruct(down.shape, F32),),
        in_specs=[taken(first, rows_step), taken(mlp, rows_step), taken(down, down_step)],
        out_specs=tuple(given(rows_step, d) for _ in range(4))
        + tuple(given(rows_step, hidden) for _ in range(2))
        + (taken(down, down_step),),
        compiler_params=pltpu.CompilerParams(vmem_limit_bytes=VMEM_LIMIT),
    )(first, mlp, down)


def per_device(
    hidden_in,
    doc_lengths,
    w_query,
    w_key,
    w_value,
    w_output,
    w_gate,
    w_up,
    w_down,
    attn_norm,
    mlp_norm,
    head_norm,
    score_kernel,
    head_mixing,
    grad_out,
):
    _, t, d = hidden_in.shape
    reps = lax.axis_size("rep")
    shards = lax.axis_size("fsdp")
    me = lax.axis_index("rep")
    hidden = w_gate.shape[1]
    heads = H // reps
    hd = d // H
    quarter = d // reps
    units = hidden // reps
    strip = units // shards
    taps, span = score_kernel.shape[1:]
    docs = doc_lengths.shape[1] - 1
    rows_here = w_gate.shape[0]

    def mine(array, size, axis):
        return lax.dynamic_slice_in_dim(array, me * size, size, axis)

    def strips(w):
        return mine(w.reshape(rows_here, shards, reps, strip), 1, 2).reshape(rows_here, units)

    if strip % 128 == 0:
        mlp_in = (w_gate, w_up)
    else:
        mlp_in = (jnp.concatenate([strips(w_gate), strips(w_up)], axis=1),)
    lines = d // 128
    cfg = (heads, hd, taps, span, docs, shards, units)
    shape_of = jax.ShapeDtypeStruct
    block_out, grad_in, n_first, n_second, n_head, g_score, g_mix, means, a_first, a_mlp, a_down = run_layer(
        cfg,
        (hidden_in.reshape(t, d), grad_out.reshape(t, d), *(n.reshape(lines, 128) for n in (attn_norm, mlp_norm, head_norm))),
        (doc_lengths, score_kernel, head_mixing),
        (w_query, w_key, w_value, w_output),
        w_down,
        mlp_in,
        (shape_of((rows_here, d), BF), shape_of((rows_here, 2 * units), BF), shape_of((strip, d), BF)),
    )
    if strip % 128 == 0:
        g_q, g_k, g_v, g_o, g_gate, g_up, g_down = widen(a_first, a_mlp, a_down, strip, shards)
    else:
        first = a_first.astype(F32).reshape(reps, rows_here, 4, quarter)
        first = jnp.moveaxis(first, 0, 2).reshape(rows_here, 4, d)
        g_q, g_k, g_v, g_o = (first[:, k] for k in range(4))
        mlp = a_mlp.astype(F32).reshape(reps, rows_here, 2, shards, strip)
        mlp = jnp.moveaxis(mlp, 0, 3).reshape(rows_here, 2, hidden)
        g_gate, g_up = mlp[:, 0], mlp[:, 1]
        g_down = a_down.astype(F32)
    return (
        block_out.reshape(hidden_in.shape),
        grad_in.reshape(hidden_in.shape),
        g_q,
        g_k,
        g_v,
        g_o,
        g_gate,
        g_up,
        g_down.reshape(w_down.shape),
        n_first.reshape(d),
        n_second.reshape(d),
        n_head.reshape(d),
        g_score[:, : taps * span].reshape(score_kernel.shape),
        g_mix[:, : 2 * heads].reshape(head_mixing.shape),
        means[0, :3],
    )


def solution(mesh):
    rows = P(("rep", "fsdp"), None, None)
    split = P("fsdp", None)
    placed = (rows, P(("rep", "fsdp"), None)) + (split,) * 7 + (P(),) * 5 + (rows,)
    return jax.shard_map(
        per_device,
        mesh=mesh,
        in_specs=placed,
        out_specs=(rows, rows) + (split,) * 7 + (P(),) * 6,
        check_vma=False,
    )
```

```python
import functools

import jax
import jax.numpy as jnp
from jax import lax
from jax.experimental import pallas as pl
from jax.experimental.pallas import tpu as pltpu
from jax.sharding import PartitionSpec as P

H = 16
BF = jnp.bfloat16
F32 = jnp.float32
MESH = pl.DeviceIdType.MESH
VMEM_LIMIT = 62 * 1024 * 1024
NN = (((1,), (0,)), ((), ()))
NT = (((1,), (1,)), ((), ()))
TN = (((0,), (0,)), ((), ()))
FIRST, MLP, DOWN = 0, 1, 2
UP, DN, SIDE = 0, 1, 2
STATS = 4


def dot(a, b, dims=NN):
    return lax.dot_general(a, b, dims, preferred_element_type=F32)


def merge(value):
    n, rows, width = value.shape
    if rows % 16 == 0:
        return value.reshape(n * rows, width)
    return value.astype(F32).reshape(n * rows, width).astype(value.dtype)


def vmem_spec():
    return pl.BlockSpec(memory_space=pltpu.VMEM)


def smem_spec():
    return pl.BlockSpec(memory_space=pltpu.SMEM)


def hbm_spec():
    return pl.BlockSpec(memory_space=pl.ANY)


def grids(t):
    rows = lax.broadcasted_iota(jnp.int32, (t, t), 0)
    cols = lax.broadcasted_iota(jnp.int32, (t, t), 1)
    return rows, cols


def allowed_of(seg_row, rows, cols):
    t = rows.shape[0]
    along = jnp.broadcast_to(seg_row, (t, t))
    return (along == jnp.transpose(along)) & (cols <= rows)


def lagged(masked, taps, rows):
    parts = [masked.astype(BF)]
    for a in range(1, taps):
        parts.append(jnp.where(rows >= a, pltpu.roll(masked, a, 0), 0.0).astype(BF))
    return jnp.concatenate(parts, axis=1)


def row_sum(value):
    return jnp.sum(value, axis=0, keepdims=True)


def mean_of(value):
    return jnp.mean(value, axis=1, keepdims=True)


def layer_kernel(cfg, *refs):
    heads, hd, taps, span, docs, shards, units = cfg
    strip = units // shards
    mlp_parts = 2 if strip % 128 == 0 else 1
    given, refs = refs[: 13 + mlp_parts], refs[13 + mlp_parts :]
    x_ref, g_ref, first_norm, second_norm, head_norm, docs_ref, score_ref, mix_ref = given[:8]
    own_first, own_down, own_mlp = given[8:12], given[12], given[13:]
    (
        out_ref, grad_in_ref, grad_first_norm, grad_second_norm, grad_head_norm, grad_score, grad_mix, means,
        all_first, all_mlp, all_down,
        w_first, w_mlp, w_down, wide, g_mlp, seg_all, attn_in, qkv, hat, inv, probs, masked, head_in, w_out,
        middle, slope, silu, hidden, g_gu, g_attn, g_middle, g_qkv, g_hin, d_out_in,
        psend, pown, r1, ysend, r2, psend2, pown2, r1b, r2b, bands, corr, g_wide, lanes, g_mix,
        x_first, x_mlp, x_down, z_first, z_mlp, z_down, small_send, small_recv, small_ref, valid_ref, gain_first, gain_second, gain_all, gain_head,
        ag_send, ag_recv, rs_send, rs_recv, rs_side_recv, rep_send, rep_recv, local, credit,
    ) = refs
    t, d = x_ref.shape
    width = heads * hd
    quarter = d // 4
    lines = shards // 2
    me = lax.axis_index("rep")
    f = lax.axis_index("fsdp")
    plane, core = me // 2, me % 2
    sibling, across = plane * 2 + (1 - core), (1 - plane) * 2 + core
    diagonal = (1 - plane) * 2 + (1 - core)
    z, side = f // 2, f % 2
    partner = 2 * z + (1 - side)
    weights = (w_first, w_mlp, w_down)
    x_lands, z_lands = (x_first, x_mlp, x_down), (z_first, z_mlp, z_down)
    peer_of = (f + 2, f - 2, partner)
    tokens = 4 * t
    part = shards // 4
    rows, cols = grids(t)

    def flip(bit):
        return f + (1 - 2 * ((f // bit) % 2)) * bit

    bits = []
    bit = 1
    while bit < shards:
        bits.append(bit)
        bit *= 2

    barrier = pltpu.get_barrier_semaphore()

    def greet(r, s):
        pl.semaphore_signal(barrier, inc=1, device_id=(r, s), device_id_type=MESH)

    for r in (sibling, across, diagonal):
        greet(r, f)
    greet(me, partner)

    @pl.loop(1, lines)
    def _(s):
        greet(me, 2 * ((z + s) % lines) + side)

    pl.semaphore_wait(barrier, 3 + lines)

    def rep_copy(src, dst, slot, peer):
        return pltpu.make_async_remote_copy(
            src_ref=src, dst_ref=dst, send_sem=rep_send.at[slot], recv_sem=rep_recv.at[slot],
            device_id=(peer, f), device_id_type=MESH,
        )

    def ag(k, block, way):
        return pltpu.make_async_remote_copy(
            src_ref=weights[k].at[block], dst_ref=weights[k].at[block],
            send_sem=ag_send.at[k, way, block], recv_sem=ag_recv.at[k, block],
            device_id=(me, peer_of[way]), device_id_type=MESH,
        )

    def ag_walk(k, s, first, act):
        sides = (side, 1 - side) if k == DOWN else (side,)
        if isinstance(s, int) and s == 0:
            for q in sides:
                block = 2 * z + q
                if k == DOWN and q is not side:
                    first(k, block)

                @pl.when(z < lines - 1)
                def _():
                    act(k, block, UP)

                @pl.when(z > 0)
                def _():
                    act(k, block, DN)

                if k != DOWN:
                    act(k, block, SIDE)
            return

        @pl.when(z - s >= 0)
        def _():
            for q in sides:
                block = 2 * (z - s) + q
                first(k, block)

                @pl.when(z < lines - 1)
                def _():
                    act(k, block, UP)

                if k != DOWN:
                    act(k, block, SIDE)

        @pl.when(z + s < lines)
        def _():
            for q in sides:
                block = 2 * (z + s) + q
                first(k, block)

                @pl.when(z > 0)
                def _():
                    act(k, block, DN)

                if k != DOWN:
                    act(k, block, SIDE)

    def arrived(k, block):
        ag(k, block, SIDE).wait_recv()

    def go(k, block, way):
        ag(k, block, way).start()

    def gone(k, block, way):
        ag(k, block, way).wait_send()

    def ag_steps(k, low, high):
        if low == 0:
            ag_walk(k, 0, arrived, go)
        else:
            pl.loop(low, high)(lambda s: ag_walk(k, s, arrived, go))

    def ag_done(k):
        if k != DOWN:
            pl.loop(0, lines)(lambda zz: arrived(k, 2 * zz + (1 - side)))

    def ag_drain(k):
        nothing = lambda *_: None
        if k == DOWN:
            gone(k, f, SIDE)
        ag_walk(k, 0, nothing, gone)
        pl.loop(1, lines)(lambda s: ag_walk(k, s, nothing, gone))

    def gather_start(fulls, slot):
        for i, full in enumerate(fulls):
            rep_copy(full.at[me], full.at[me], slot + 3 * i, across).start()
            rep_copy(full.at[me], full.at[me], slot + 3 * i + 1, sibling).start()

    def gather_pass(fulls, slot):
        for i, full in enumerate(fulls):
            rep_copy(full.at[me], full.at[me], slot + 3 * i, across).wait_recv()
            rep_copy(full.at[across], full.at[across], slot + 3 * i + 2, sibling).start()

    def gather_end(fulls, slot):
        for i, full in enumerate(fulls):
            rep_copy(full.at[me], full.at[me], slot + 3 * i + 1, sibling).wait_recv()
            rep_copy(full.at[across], full.at[across], slot + 3 * i + 2, sibling).wait_recv()
        for i, full in enumerate(fulls):
            rep_copy(full.at[me], full.at[me], slot + 3 * i, across).wait_send()
            rep_copy(full.at[me], full.at[me], slot + 3 * i + 1, sibling).wait_send()
            rep_copy(full.at[across], full.at[across], slot + 3 * i + 2, sibling).wait_send()

    def pair_of(ref, a, b):
        return jnp.concatenate([ref[a], ref[b]], axis=0)

    def sum_copies(slot, send_buf, first_land, second_land):
        return (
            rep_copy(send_buf, first_land, slot, sibling),
            rep_copy(ysend, second_land, slot + 1, across),
        )

    def column_chunk(i):
        return pl.ds(pl.multiple_of(i * quarter, quarter), quarter)

    def sum_theirs(product, copies, send_buf):
        @pl.loop(0, 4)
        def _(i):
            value = product(1 - core, 2 + (1 - core), i)
            send_buf[0, :, column_chunk(i)] = value[:t].astype(BF)
            send_buf[1, :, column_chunk(i)] = value[t:].astype(BF)

        copies[0].start()

    def sum_ours(product, own_buf):
        @pl.loop(0, 4)
        def _(i):
            value = product(across, me, i)
            own_buf[0, :, column_chunk(i)] = value[:t].astype(own_buf.dtype)
            own_buf[1, :, column_chunk(i)] = value[t:].astype(own_buf.dtype)

    def sum_turn(copies, own_buf, first_land):
        copies[0].wait_recv()
        ysend[...] = (own_buf[0].astype(F32) + first_land[1 - plane].astype(F32)).astype(BF)
        copies[1].start()
        own_buf[1] = (own_buf[1].astype(F32) + first_land[plane].astype(F32)).astype(own_buf.dtype)

    def sum_end(copies, own_buf, second_land):
        copies[1].wait_recv()
        total = own_buf[1].astype(F32) + second_land[...].astype(F32)
        copies[0].wait_send()
        copies[1].wait_send()
        return total

    def yes(condition):
        return int(condition) if isinstance(condition, bool) else condition.astype(jnp.int32)

    def far_slot(at, target):
        return at if lines == 4 else target

    def near_slot(source, target):
        return source if lines == 4 else lines + source - target + 2 - yes(source > target)

    def target_of(s):
        ahead = lines - 1 - z
        first_end, last_end = yes(z == 0), yes(z == lines - 1)
        inner = 1 - first_end - last_end
        if lines == 4:
            near = yes(s == 1) * (z + 1) + yes(s == 2) * (z - 1) + yes(s == 3) * (3 * (2 - z))
        else:
            near = yes(s <= ahead) * (z + s) + yes(s > ahead) * (z - (s - ahead))
        return first_end * (lines - s) + last_end * (s - 1) + inner * near

    def rs_side(k, zz):
        source = weights[k].at[2 * zz + (1 - side)]
        if k == DOWN:
            source = x_mlp.at[zz, pl.ds(0, strip), pl.ds(0, d)]
        return pltpu.make_async_remote_copy(
            src_ref=source, dst_ref=x_lands[k].at[zz],
            send_sem=rs_send.at[k, 0, zz], recv_sem=rs_side_recv.at[k, zz],
            device_id=(me, partner), device_id_type=MESH,
        )

    def rs_hop(k, target):
        up = yes(target > z)
        toward = z + 2 * up - 1
        distance = up * (target - z) + (1 - up) * (z - target)
        far = yes(distance >= 3)
        to = far * toward + (1 - far) * target
        slot = far * far_slot(toward, target) + (1 - far) * near_slot(z, target)
        at = slot
        return pltpu.make_async_remote_copy(
            src_ref=weights[k].at[2 * target + side], dst_ref=z_lands[k].at[at],
            send_sem=rs_send.at[k, 1, 2 * target], recv_sem=rs_recv.at[k, at],
            device_id=(me, 2 * to + side), device_id_type=MESH,
        )

    def rs_landed(k, slot):
        at = slot
        pltpu.make_async_remote_copy(
            src_ref=weights[k].at[f], dst_ref=z_lands[k].at[at],
            send_sem=rs_send.at[k, 1, f], recv_sem=rs_recv.at[k, at],
            device_id=(me, partner), device_id_type=MESH,
        ).wait_recv()
        return z_lands[k], at

    def rs_add(k, block, landed):
        grad = weights[k]
        high = grad.shape[1]
        step = 16 if high % 16 == 0 else high

        @pl.loop(0, high // step)
        def _(i):
            at = pl.ds(pl.multiple_of(i * step, step), step)
            total = grad[block, at, :].astype(F32)
            for land, slot in landed:
                total = total + land[slot, at, :].astype(F32)
            grad[block, at, :] = total.astype(BF)

    def rs_turn(k, s):
        target = target_of(s)
        up = yes(target > z)
        distance = up * (target - z) + (1 - up) * (z - target)
        behind = up * yes(z > 0) + (1 - up) * yes(z < lines - 1)
        rs_side(k, target).wait_recv()
        handed = (distance >= 2) & (behind == 1)

        @pl.when(handed)
        def _():
            land = rs_landed(k, far_slot(z, target))
            rs_add(k, 2 * target + side, [(x_lands[k], target), land])

        @pl.when(jnp.logical_not(handed))
        def _():
            rs_add(k, 2 * target + side, [(x_lands[k], target)])

        rs_hop(k, target).start()

    def rs_close(k):
        first_end, last_end = yes(z == 0), yes(z == lines - 1)
        inner = 1 - first_end - last_end
        one = first_end * 1 + (1 - first_end) * (z - 1)
        two = first_end * 2 + last_end * (lines - 3) + inner * (z + 1)
        rs_side(k, z).wait_recv()
        rs_add(k, f, [(x_lands[k], z), rs_landed(k, near_slot(one, z)), rs_landed(k, near_slot(two, z))])

        @pl.when((z > 0) & (z + 2 < lines))
        def _():
            rs_add(k, f, [rs_landed(k, near_slot(z + 2, z))])

        @pl.when((z < lines - 1) & (z >= 2))
        def _():
            rs_add(k, f, [rs_landed(k, near_slot(z - 2, z))])

    def rs_drain(k):
        if k != DOWN:
            pl.loop(0, lines)(lambda zz: rs_side(k, zz).wait_send())
        pl.loop(1, lines)(lambda s: rs_hop(k, target_of(s)).wait_send())

    outs = (all_first, all_mlp, all_down)

    def final_copies(k, slot):
        own = weights[k].at[f]
        full = outs[k]
        return (
            rep_copy(own, full.at[me], slot, across),
            rep_copy(own, full.at[me], slot + 1, sibling),
            rep_copy(full.at[across], full.at[across], slot + 2, sibling),
            pltpu.make_async_copy(own, full.at[me], local.at[1 + k]),
        )

    def final_start(k, slot):
        a, b, _, here = final_copies(k, slot)
        a.start()
        b.start()
        here.start()

    def final_pass(k, slot):
        a, _, c, _ = final_copies(k, slot)
        a.wait_recv()
        c.start()

    def final_end(k, slot):
        a, b, c, here = final_copies(k, slot)
        b.wait_recv()
        c.wait_recv()
        a.wait_send()
        b.wait_send()
        c.wait_send()
        here.wait()

    def cut(ref, at, size):
        return ref.at[:, pl.ds(pl.multiple_of(at, size), size)]

    sources = [
        [(cut(own_first[i], me * quarter, quarter), w_first.at[f, :, pl.ds(i * quarter, quarter)]) for i in range(4)],
        [(own_mlp[0], w_mlp.at[f])],
        [(own_down.at[pl.ds(pl.multiple_of(me * strip, strip), strip), :], w_down.at[f])],
    ]
    if mlp_parts == 2:
        sources[MLP] = [
            (cut(own_mlp[i // shards], (4 * (i % shards) + me) * strip, strip), w_mlp.at[f, :, pl.ds(i * strip, strip)])
            for i in range(2 * shards)
        ]
    loads, used = [], 4
    for pairs in sources:
        loads.append([pltpu.make_async_copy(a, b, local.at[used + i]) for i, (a, b) in enumerate(pairs)])
        used += len(pairs)
    for k in range(3):
        for load in loads[k]:
            load.start()

    def load_wait(k):
        for load in loads[k]:
            load.wait()

    lane = lax.broadcasted_iota(jnp.int32, (1, t), 1)
    seg = jnp.zeros((1, t), F32)
    edge = 0
    for i in range(docs):
        edge = edge + docs_ref[0, i]
        seg = seg + jnp.where(lane >= edge, 1.0, 0.0)
    valid = jnp.where(jnp.transpose(jnp.broadcast_to(seg, (t, t))) < float(docs), 1.0, 0.0)
    valid_ref[...] = valid[:, 0:1]

    def as_row(ref):
        return jnp.concatenate([ref[i : i + 1, :] for i in range(ref.shape[0])], axis=1)

    gain_first[...] = as_row(first_norm)
    gain_second[...] = as_row(second_norm)
    gain_all[...] = as_row(head_norm)
    gain_head[...] = gain_all[:, pl.ds(pl.multiple_of(me * quarter, quarter), quarter)]
    wide[me] = x_ref[...]
    g_mlp[me] = g_ref[...]
    seg_all[me] = jnp.broadcast_to(seg, (8, t))
    entering = (seg_all, wide, g_mlp)
    gather_start(entering, 0)
    load_wait(FIRST)
    ag_steps(FIRST, 0, 1)

    diff = cols - rows + (span - 1) // 2

    @pl.loop(0, heads)
    def _(h):
        for a in range(taps):
            band = jnp.zeros((t, t), F32)
            for b in range(span):
                band = jnp.where(diff == b, score_ref[me * heads + h, a, b], band)
            bands[h, a * t : (a + 1) * t, :] = band.astype(BF)

    gather_pass(entering, 0)
    ag_steps(FIRST, 1, 2)
    load_wait(DOWN)
    ag(DOWN, f, SIDE).start()
    gather_end(entering, 0)

    @pl.loop(0, 4)
    def _(r):
        value = wide[r].astype(F32)
        scale = lax.rsqrt(mean_of(value * value) + 1e-06)
        attn_in[r] = (value * scale * gain_first[...]).astype(BF)
        valid = jnp.transpose(jnp.broadcast_to(seg_all[r][0:1, :], (t, t)))[:, 0:1] < float(docs)
        g_mlp[r] = jnp.where(valid, g_mlp[r].astype(F32), 0.0).astype(BF)

    ag_steps(FIRST, 2, 3)
    load_wait(MLP)
    ag_steps(MLP, 0, 1)
    ag_steps(FIRST, 3, lines)
    ag_steps(MLP, 1, 2)
    ag_done(FIRST)

    def w_out_copy(peer, slot):
        return rep_copy(
            w_first.at[pl.ds(peer * part, part), :, pl.ds(3 * quarter, quarter)],
            w_out.at[:, :, pl.ds(pl.multiple_of(me * quarter, quarter), quarter)],
            slot, peer,
        )

    for i, peer in enumerate((sibling, across, diagonal)):
        w_out_copy(peer, 9 + i).start()
    own_out = pltpu.make_async_copy(
        w_first.at[pl.ds(me * part, part), :, pl.ds(3 * quarter, quarter)],
        w_out.at[:, :, pl.ds(pl.multiple_of(me * quarter, quarter), quarter)],
        local.at[0],
    )
    own_out.start()

    for i in range(3):
        value = dot(attn_in[...].reshape(tokens, d), merge(w_first[:, :, i * quarter : (i + 1) * quarter]))
        qkv[:, :, i * quarter : (i + 1) * quarter] = value.astype(BF).reshape(4, t, quarter)
    ag_steps(MLP, 2, 3)
    ag_steps(DOWN, 0, 1)

    def split(ref, row, kind, h):
        return ref[row, :, kind * width + h * hd : kind * width + (h + 1) * hd]

    @pl.loop(0, 4)
    def _(row):
        allowed = allowed_of(seg_all[row][0:1, :], rows, cols)
        for pair in range(heads // 2):
            both = []
            for c in range(2):
                h = 2 * pair + c
                scores = dot(split(qkv, row, 0, h), split(qkv, row, 1, h), NT) * hd**-0.5
                kept = jnp.where(allowed, scores, 0.0)
                masked[row, h] = kept.astype(BF)
                logits = jnp.where(allowed, dot(lagged(kept, taps, rows), bands[h]), -1e30)
                e = jnp.exp(logits - jnp.max(logits, axis=1, keepdims=True))
                p = e / jnp.sum(e, axis=1, keepdims=True)
                probs[row, h] = p
                both.append(p)
            for e in range(2):
                h = 2 * pair + e
                mixed = (mix_ref[me * heads + h, 0] * both[0] + mix_ref[me * heads + h, 1] * both[1]).astype(BF)
                out = dot(mixed, split(qkv, row, 2, h))
                centred = out - mean_of(out)
                scale = lax.rsqrt(mean_of(centred * centred) + 1e-05)
                hat[row, :, h * hd : (h + 1) * hd] = centred * scale
                inv[row, :, h : h + 1] = scale
        head_in[row] = (hat[row] * gain_head[...]).astype(BF)

    for i, peer in enumerate((sibling, across, diagonal)):
        w_out_copy(peer, 9 + i).wait_recv()
    own_out.wait()

    copies = sum_copies(12, psend, r1, r2)
    product = lambda a, b, i: dot(pair_of(head_in, a, b), merge(w_out[:, :, column_chunk(i)]))
    sum_theirs(product, copies, psend)
    sum_ours(product, pown)
    ag_steps(MLP, 3, lines)
    sum_turn(copies, pown, r1)
    total = sum_end(copies, pown, r2)
    attn_part = valid_ref[...] * total
    value = x_ref[...].astype(F32) + attn_part
    middle[...] = value
    stat_attn = jnp.sum(row_sum(attn_part * attn_part), axis=1, keepdims=True)
    scale = lax.rsqrt(mean_of(value * value) + 1e-06)
    wide[me] = (value * scale * gain_second[...]).astype(BF)
    gather_start((wide,), 14)
    ag_steps(DOWN, 1, 2)
    gather_pass((wide,), 14)
    gather_end((wide,), 14)
    mlp_in = wide
    ag_steps(DOWN, 2, 3)
    ag_done(MLP)

    chunk = 256

    @pl.loop(0, units // chunk)
    def _(i):
        at = pl.ds(pl.multiple_of(i * chunk, chunk), chunk)
        after = pl.ds(pl.multiple_of(units + i * chunk, chunk), chunk)
        operand = mlp_in[...].reshape(tokens, d)
        gate = dot(operand, merge(w_mlp[:, :, at]))
        upper = dot(operand, merge(w_mlp[:, :, after]))
        sig = 1.0 / (1.0 + jnp.exp(-gate))
        act = gate * sig
        hidden[:, :, at] = (act * upper).astype(BF).reshape(4, t, chunk)
        silu[:, at] = act.astype(BF)
        slope[:, at] = (upper * sig * (1.0 + gate * (1.0 - sig))).astype(BF)

    @pl.loop(0, 4)
    def _(i):
        span_units = units // 4
        at = pl.ds(pl.multiple_of(i * span_units, span_units), span_units)
        value = dot(hidden[:, :, at].reshape(tokens, span_units), g_mlp[...].reshape(tokens, d), TN)
        value = value.reshape(part, strip, d)
        for j in range(part // 2):
            half = jnp.where(side == 0, value[2 * j + 1], value[2 * j])
            x_mlp[i * (part // 2) + j, 0:strip, 0:d] = half.astype(BF)

    pl.loop(1, lines)(lambda s: rs_side(DOWN, target_of(s)).start())
    rs_side(DOWN, z).start()

    ag_steps(DOWN, 3, lines)

    @pl.loop(0, 4)
    def _(i):
        span_units = units // 4
        at = pl.ds(pl.multiple_of(i * span_units, span_units), span_units)
        after = pl.ds(pl.multiple_of(units + i * span_units, span_units), span_units)
        g_hidden = dot(g_mlp[...].reshape(tokens, d), merge(w_down[pl.ds(i * part, part)]), NT)
        g_gu[:, :, at] = (g_hidden * slope[:, at].astype(F32)).astype(BF).reshape(4, t, span_units)
        g_gu[:, :, after] = (g_hidden * silu[:, at].astype(F32)).astype(BF).reshape(4, t, span_units)

    mlp_copies = sum_copies(17, psend, r1, r2)
    product = lambda a, b, i: dot(pair_of(g_gu, a, b), merge(w_mlp[pl.ds(i * part, part)]), NT)
    sum_theirs(product, mlp_copies, psend)
    sum_ours(product, pown)

    out_copies = (rep_copy(psend2, r1b, 19, sibling), rep_copy(ysend, r2b, 20, across))
    product = lambda a, b, i: dot(pair_of(hidden, a, b), merge(w_down[:, :, column_chunk(i)]))
    sum_theirs(product, out_copies, psend2)
    sum_ours(product, pown2)
    sum_turn(mlp_copies, pown, r1)

    ag_drain(DOWN)

    @pl.loop(0, 4)
    def _(i):
        span_units = units // 4
        at = pl.ds(pl.multiple_of(i * span_units, span_units), span_units)
        value = dot(hidden[:, :, at].reshape(tokens, span_units), g_mlp[...].reshape(tokens, d), TN)
        w_down[pl.ds(i * part, part)] = value.reshape(part, w_down.shape[1], d).astype(BF)

    total = sum_end(mlp_copies, pown, r2)
    value = middle[...]
    scale = lax.rsqrt(mean_of(value * value) + 1e-06)
    normed = value * scale
    prod = total * normed
    g_second = row_sum(prod)
    mean = mean_of(prod * gain_second[...])
    value = g_ref[...].astype(F32) + scale * (total * gain_second[...] - normed * mean)
    g_middle[...] = value
    g_attn[me] = (valid_ref[...] * value).astype(BF)
    gather_start((g_attn,), 21)
    ag_drain(MLP)
    pl.loop(0, lines)(lambda zz: rs_side(DOWN, zz).wait_send())
    pl.semaphore_signal(credit, inc=1, device_id=(me, partner), device_id_type=MESH)

    def in_turn(i):
        if lines != 4:
            return i
        return yes(i < 3) * target_of(i + 1) + yes(i == 3) * z

    def send_side(k, p):
        @pl.loop(0, part // 2)
        def _(j):
            zz = p * (part // 2) + j
            rs_side(k, zz).start()

    @pl.loop(0, 4)
    def _(i):
        p = in_turn(i)
        at = pl.ds(pl.multiple_of(p * quarter, quarter), quarter)
        size = units // 2

        @pl.loop(0, 4)
        def _(j):
            to = pl.ds(pl.multiple_of(j * size, size), size)
            value = dot(mlp_in[:, :, at].reshape(tokens, quarter), g_gu[:, :, to].reshape(tokens, size), TN)
            w_mlp[pl.ds(p * part, part), :, to] = value.reshape(part, w_mlp.shape[1], size).astype(BF)


        @pl.when(i == 0)
        def _():
            pl.semaphore_wait(credit, 1)

        send_side(MLP, p)

    gather_pass((g_attn,), 21)
    gather_end((g_attn,), 21)

    value = dot(g_attn[...].reshape(tokens, d), merge(w_out[...]), NT)
    g_hin[...] = value.reshape(4, t, width)
    d_out = w_out

    @pl.loop(0, 4)
    def _(i):
        value = dot(head_in[...].reshape(tokens, width), g_attn[:, :, column_chunk(i)].reshape(tokens, quarter), TN)
        d_out[:, :, column_chunk(i)] = value.reshape(part, w_first.shape[1], quarter).astype(BF)


    def d_out_copy(peer, slot):
        return rep_copy(
            d_out.at[:, :, pl.ds(pl.multiple_of(peer * quarter, quarter), quarter)],
            d_out_in.at[pl.ds(me * part, part)],
            slot, peer,
        )

    for i, peer in enumerate((sibling, across, diagonal)):
        d_out_copy(peer, 24 + i).start()
    own_d_out = pltpu.make_async_copy(
        d_out.at[:, :, pl.ds(pl.multiple_of(me * quarter, quarter), quarter)],
        d_out_in.at[pl.ds(me * part, part)], local.at[4],
    )
    own_d_out.start()
    pl.loop(1, lines)(lambda s: rs_turn(DOWN, s))

    corr[...] = jnp.zeros_like(corr)
    g_mix[...] = jnp.zeros_like(g_mix)
    lanes[...] = jnp.zeros_like(lanes)

    @pl.loop(0, 4)
    def _(row):
        allowed = allowed_of(seg_all[row][0:1, :], rows, cols)
        g_wide[...] = g_hin[row] * gain_head[...]
        for pair in range(heads // 2):
            g_heads, g_mixed = [], []
            both = [probs[row, 2 * pair + c] for c in range(2)]
            for e in range(2):
                h = 2 * pair + e
                scaled = g_wide[:, h * hd : (h + 1) * hd]
                own_hat = hat[row, :, h * hd : (h + 1) * hd]
                g = inv[row, :, h : h + 1] * (scaled - mean_of(scaled) - own_hat * mean_of(scaled * own_hat))
                g = g.astype(BF)
                g_heads.append(g)
                g_mixed.append(dot(g, split(qkv, row, 2, h), NT))
            for e in range(2):
                h = 2 * pair + e
                mixed = (mix_ref[me * heads + h, 0] * both[0] + mix_ref[me * heads + h, 1] * both[1]).astype(BF)
                g_v = dot(mixed, g_heads[e], TN)
                g_qkv[row, :, 2 * width + h * hd : 2 * width + (h + 1) * hd] = g_v.astype(BF)
                for c in range(2):
                    place = (2 * pair + e) * 2 + c
                    g_mix[place : place + 1, :] += row_sum(g_mixed[e] * both[c])
            for c in range(2):
                h = 2 * pair + c
                g_probs = mix_ref[me * heads + 2 * pair, c] * g_mixed[0] + mix_ref[me * heads + 2 * pair + 1, c] * g_mixed[1]
                weighted = both[c] * g_probs
                g_conv = weighted - both[c] * jnp.sum(weighted, axis=1, keepdims=True)
                corr[h] += dot(lagged(masked[row, h].astype(F32), taps, rows), g_conv.astype(BF), TN)
                g_kept = dot(g_conv.astype(BF), bands[h, 0:t, :], NT)
                for a in range(1, taps):
                    lead = jnp.where(rows < t - a, pltpu.roll(g_conv, t - a, 0), 0.0).astype(BF)
                    g_kept += dot(lead, bands[h, a * t : (a + 1) * t, :], NT)
                g_raw = jnp.where(allowed, g_kept, 0.0).astype(BF)
                g_q = dot(g_raw, split(qkv, row, 1, h)) * hd**-0.5
                g_k = dot(g_raw, split(qkv, row, 0, h), TN) * hd**-0.5
                g_qkv[row, :, h * hd : (h + 1) * hd] = g_q.astype(BF)
                g_qkv[row, :, width + h * hd : width + (h + 1) * hd] = g_k.astype(BF)

    rs_turn(MLP, 1)
    in_copies = sum_copies(27, psend, r1, r2)
    product = lambda a, b, i: dot(pair_of(g_qkv, a, b), merge(w_first[pl.ds(i * part, part), :, 0 : 3 * quarter]), NT)
    sum_theirs(product, in_copies, psend)
    sum_ours(product, pown)
    sum_turn(in_copies, pown, r1)

    ag_drain(FIRST)
    for i, peer in enumerate((sibling, across, diagonal)):
        w_out_copy(peer, 9 + i).wait_send()
        d_out_copy(peer, 24 + i).wait_recv()
    own_d_out.wait()

    @pl.loop(0, 4)
    def _(i):
        p = in_turn(i)
        at = pl.ds(pl.multiple_of(p * quarter, quarter), quarter)
        value = dot(attn_in[:, :, at].reshape(tokens, quarter), g_qkv[...].reshape(tokens, 3 * quarter), TN)
        w_first[pl.ds(p * part, part), :, 0 : 3 * quarter] = value.reshape(part, w_first.shape[1], 3 * quarter).astype(BF)
        w_first[pl.ds(p * part, part), :, 3 * quarter :] = d_out_in[pl.ds(p * part, part)]
        send_side(FIRST, p)

    rs_turn(MLP, 2)
    total = sum_end(in_copies, pown, r2)
    value = x_ref[...].astype(F32)
    scale = lax.rsqrt(mean_of(value * value) + 1e-06)
    normed = value * scale
    prod = total * normed
    g_first = row_sum(prod)
    mean = mean_of(prod * gain_first[...])
    grad_in_ref[...] = (g_middle[...] + scale * (total * gain_first[...] - normed * mean)).astype(BF)

    sum_turn(out_copies, pown2, r1b)
    total = sum_end(out_copies, pown2, r2b)
    mlp_part = valid_ref[...] * total
    value = middle[...] + mlp_part
    out_ref[...] = value.astype(BF)
    stat_out = jnp.sum(row_sum(valid_ref[...] * value * value), axis=1, keepdims=True)
    stat_mlp = jnp.sum(row_sum(mlp_part * mlp_part), axis=1, keepdims=True)

    strips = d // 128
    small_ref[...] = jnp.zeros_like(small_ref)
    for i in range(strips):
        at = slice(128 * i, 128 * (i + 1))
        small_ref[i : i + 1, :] = g_first[:, at]
        small_ref[strips + i : strips + i + 1, :] = g_second[:, at]
    own_gain = row_sum((g_hin[...] * hat[...]).reshape(tokens, width))
    for i in range(width // 128):
        small_ref[pl.ds(2 * strips + me * (width // 128) + i, 1), :] = own_gain[:, 128 * i : 128 * (i + 1)]
    base = 3 * strips
    for h in range(heads):
        for a in range(taps):
            tile = corr[h, a * t : (a + 1) * t, :]
            for b in range(span):
                lanes[a * span + b : a * span + b + 1, :] = row_sum(jnp.where(diff == b, tile, 0.0))
        small_ref[pl.ds(base + me * heads + h, 1), :] = row_sum(jnp.transpose(lanes[...]))
    base += 4 * heads
    lanes[0 : 2 * heads, :] = g_mix[...]
    lanes[2 * heads :, :] = jnp.zeros((t - 2 * heads, t), F32)
    small_ref[pl.ds(base + me, 1), :] = row_sum(jnp.transpose(lanes[...]))
    base += 4
    lane = lax.broadcasted_iota(jnp.int32, (1, 128), 1)
    count = jnp.sum(row_sum(jnp.broadcast_to(valid_ref[...], (t, 128))), axis=1, keepdims=True) * (1.0 / 128.0)
    stats = jnp.zeros((1, 128), F32)
    for i, stat in enumerate((stat_out, stat_attn, stat_mlp, count)):
        stats = jnp.where(lane == i, stat, stats)
    small_ref[base : base + 1, :] = stats

    peers = [(sibling, f), (across, f)] + [(me, flip(bit)) for bit in bits]

    def small_copy(i):
        return pltpu.make_async_remote_copy(
            src_ref=small_send.at[i], dst_ref=small_recv.at[i],
            send_sem=rep_send.at[40 + i], recv_sem=rep_recv.at[40 + i],
            device_id=peers[i], device_id_type=MESH,
        )

    def small_step(i):
        small_send[i] = small_ref[...]
        small_copy(i).start()

    def small_take(i):
        small_copy(i).wait_recv()
        small_ref[...] = small_ref[...] + small_recv[i]

    rs_close(DOWN)
    final_start(DOWN, 30)
    pl.loop(3, lines)(lambda s: rs_turn(MLP, s))
    final_pass(DOWN, 30)
    small_step(0)
    small_take(0)
    small_step(1)
    rs_turn(FIRST, 1)
    rs_close(MLP)
    final_start(MLP, 33)
    small_take(1)
    small_step(2)
    pl.loop(2, lines)(lambda s: rs_turn(FIRST, s))
    final_pass(MLP, 33)
    rs_close(FIRST)
    final_start(FIRST, 36)
    for i in range(2, len(peers)):
        small_take(i)
        if i + 1 < len(peers):
            small_step(i + 1)
    final_pass(FIRST, 36)
    grad_first_norm[...] = small_ref[0:strips, :]
    grad_second_norm[...] = small_ref[strips : 2 * strips, :]
    grad_head_norm[...] = small_ref[2 * strips : 3 * strips, :]
    at = 3 * strips
    grad_score[...] = small_ref[at : at + 4 * heads, :]
    grad_mix[...] = small_ref[at + 4 * heads : at + 4 * heads + 4, :]
    sums = small_ref[at + 4 * heads + 4 : at + 4 * heads + 5, :]
    means[...] = jnp.sqrt(sums / (sums[:, 3:4] * float(d)))
    for k in range(3):
        final_end(k, (36, 33, 30)[k])
    for k in range(3):
        rs_drain(k)
    for i in range(len(peers)):
        small_copy(i).wait_send()
    for i, peer in enumerate((sibling, across, diagonal)):
        d_out_copy(peer, 24 + i).wait_send()


def run_layer(cfg, vectors, scalars, first_in, down_in, mlp_in, sizes):
    heads, hd, taps, span, docs, shards, units = cfg
    t, d = vectors[0].shape
    width = heads * hd
    first, mlp, down = shards_in = sizes
    bits = shards.bit_length() - 1
    lines = shards // 2
    slots = lines if lines == 4 else lines + 4

    def shape(dtype, *dims):
        return jax.ShapeDtypeStruct(dims, dtype)

    v = pltpu.VMEM
    dma = pltpu.SemaphoreType.DMA
    out_shape = (
        shape(BF, t, d), shape(BF, t, d), *(shape(F32, d // 128, 128) for _ in range(3)),
        shape(F32, 4 * heads, 128), shape(F32, 4, 128), shape(F32, 1, 128),
        *(shape(BF, 4, *s.shape) for s in shards_in),
    )
    scratch = [
        *(v((shards, *s.shape), BF) for s in shards_in),
        v((4, t, d), BF), v((4, t, d), BF), v((4, 8, t), F32), v((4, t, d), BF), v((4, t, 3 * width), BF),
        v((4, t, width), F32), v((4, t, 128), F32), v((4, heads, t, t), F32), v((4, heads, t, t), BF),
        v((4, t, width), BF), v((shards // 4, first.shape[0], d), BF),
        v((t, d), F32), v((4 * t, units), BF), v((4 * t, units), BF), v((4, t, units), BF), v((4, t, 2 * units), BF),
        v((4, t, d), BF), v((t, d), F32), v((4, t, 3 * width), BF), v((4, t, width), F32),
        v((shards, first.shape[0], width), BF),
        v((2, t, d), BF), v((2, t, d), BF), v((2, t, d), BF), v((t, d), BF), v((t, d), BF),
        v((2, t, d), BF), v((2, t, d), BF), v((2, t, d), BF), v((t, d), BF),
        v((heads, taps * t, t), BF), v((heads, taps * t, t), F32), v((t, width), F32), v((t, t), F32), v((2 * heads, t), F32),
        *(v((lines, *s.shape), BF) for s in shards_in), *(v((slots, *s.shape), BF) for s in shards_in), v((2 + bits, 64, 128), F32), v((2 + bits, 64, 128), F32),
        v((64, 128), F32), v((t, 1), F32), v((1, d), F32), v((1, d), F32), v((1, d), F32), v((1, width), F32),
        dma((3, 3, shards)), dma((3, shards)), dma((3, 2, shards)), dma((3, slots)), dma((3, lines)), dma((48,)), dma((48,)), dma((10 + 2 * shards,)), pltpu.SemaphoreType.REGULAR,
    ]
    return pl.pallas_call(
        functools.partial(layer_kernel, cfg),
        out_shape=out_shape,
        in_specs=[vmem_spec()] * 5 + [smem_spec()] * 3 + [hbm_spec()] * (5 + len(mlp_in)),
        out_specs=(vmem_spec(),) * 8 + (hbm_spec(),) * 3,
        scratch_shapes=scratch,
        compiler_params=pltpu.CompilerParams(
            collective_id=0, has_side_effects=True, vmem_limit_bytes=VMEM_LIMIT
        ),
    )(*vectors, *scalars, *first_in, down_in, *mlp_in)


def widen_kernel(strip, count, first_ref, mlp_ref, down_ref, *outs):
    quarter = first_ref.shape[2] // 4
    for r in range(4):
        for k in range(4):
            outs[k][:, r * quarter : (r + 1) * quarter] = first_ref[r, :, k * quarter : (k + 1) * quarter].astype(F32)
        outs[6][r] = down_ref[r].astype(F32)
        for k in range(2):
            for i in range(count):
                at = (4 * i + r) * strip
                outs[4 + k][:, at : at + strip] = mlp_ref[r, :, (k * count + i) * strip : (k * count + i + 1) * strip].astype(F32)


def widen(first, mlp, down, strip, count):
    _, rows, d = first.shape
    steps = 4 if rows % 64 == 0 and down.shape[1] % 64 == 0 else 1
    hidden = 4 * strip * count
    rows_step, down_step = rows // steps, down.shape[1] // steps

    def taken(array, size):
        return pl.BlockSpec((4, size, array.shape[2]), lambda i: (0, i, 0))

    def given(size, width):
        return pl.BlockSpec((size, width), lambda i: (i, 0))

    return pl.pallas_call(
        functools.partial(widen_kernel, strip, count),
        grid=(steps,),
        out_shape=tuple(jax.ShapeDtypeStruct((rows, d), F32) for _ in range(4))
        + tuple(jax.ShapeDtypeStruct((rows, hidden), F32) for _ in range(2))
        + (jax.ShapeDtypeStruct(down.shape, F32),),
        in_specs=[taken(first, rows_step), taken(mlp, rows_step), taken(down, down_step)],
        out_specs=tuple(given(rows_step, d) for _ in range(4))
        + tuple(given(rows_step, hidden) for _ in range(2))
        + (taken(down, down_step),),
        compiler_params=pltpu.CompilerParams(vmem_limit_bytes=VMEM_LIMIT),
    )(first, mlp, down)


def per_device(
    hidden_in,
    doc_lengths,
    w_query,
    w_key,
    w_value,
    w_output,
    w_gate,
    w_up,
    w_down,
    attn_norm,
    mlp_norm,
    head_norm,
    score_kernel,
    head_mixing,
    grad_out,
):
    _, t, d = hidden_in.shape
    reps = lax.axis_size("rep")
    shards = lax.axis_size("fsdp")
    me = lax.axis_index("rep")
    hidden = w_gate.shape[1]
    heads = H // reps
    hd = d // H
    quarter = d // reps
    units = hidden // reps
    strip = units // shards
    taps, span = score_kernel.shape[1:]
    docs = doc_lengths.shape[1] - 1
    rows_here = w_gate.shape[0]

    def mine(array, size, axis):
        return lax.dynamic_slice_in_dim(array, me * size, size, axis)

    def strips(w):
        return mine(w.reshape(rows_here, shards, reps, strip), 1, 2).reshape(rows_here, units)

    if strip % 128 == 0:
        mlp_in = (w_gate, w_up)
    else:
        mlp_in = (jnp.concatenate([strips(w_gate), strips(w_up)], axis=1),)
    lines = d // 128
    cfg = (heads, hd, taps, span, docs, shards, units)
    shape_of = jax.ShapeDtypeStruct
    block_out, grad_in, n_first, n_second, n_head, g_score, g_mix, means, a_first, a_mlp, a_down = run_layer(
        cfg,
        (hidden_in.reshape(t, d), grad_out.reshape(t, d), *(n.reshape(lines, 128) for n in (attn_norm, mlp_norm, head_norm))),
        (doc_lengths, score_kernel, head_mixing),
        (w_query, w_key, w_value, w_output),
        w_down,
        mlp_in,
        (shape_of((rows_here, d), BF), shape_of((rows_here, 2 * units), BF), shape_of((strip, d), BF)),
    )
    if strip % 128 == 0:
        g_q, g_k, g_v, g_o, g_gate, g_up, g_down = widen(a_first, a_mlp, a_down, strip, shards)
    else:
        first = a_first.astype(F32).reshape(reps, rows_here, 4, quarter)
        first = jnp.moveaxis(first, 0, 2).reshape(rows_here, 4, d)
        g_q, g_k, g_v, g_o = (first[:, k] for k in range(4))
        mlp = a_mlp.astype(F32).reshape(reps, rows_here, 2, shards, strip)
        mlp = jnp.moveaxis(mlp, 0, 3).reshape(rows_here, 2, hidden)
        g_gate, g_up = mlp[:, 0], mlp[:, 1]
        g_down = a_down.astype(F32)
    return (
        block_out.reshape(hidden_in.shape),
        grad_in.reshape(hidden_in.shape),
        g_q,
        g_k,
        g_v,
        g_o,
        g_gate,
        g_up,
        g_down.reshape(w_down.shape),
        n_first.reshape(d),
        n_second.reshape(d),
        n_head.reshape(d),
        g_score[:, : taps * span].reshape(score_kernel.shape),
        g_mix[:, : 2 * heads].reshape(head_mixing.shape),
        means[0, :3],
    )


def solution(mesh):
    rows = P(("rep", "fsdp"), None, None)
    split = P("fsdp", None)
    placed = (rows, P(("rep", "fsdp"), None)) + (split,) * 7 + (P(),) * 5 + (rows,)
    return jax.shard_map(
        per_device,
        mesh=mesh,
        in_specs=placed,
        out_specs=(rows, rows) + (split,) * 7 + (P(),) * 6,
        check_vma=False,
    )
```

```python
import functools

import jax
import jax.numpy as jnp
from jax import lax
from jax.experimental import pallas as pl
from jax.experimental.pallas import tpu as pltpu
from jax.sharding import PartitionSpec as P

H = 16
BF = jnp.bfloat16
F32 = jnp.float32
MESH = pl.DeviceIdType.MESH
VMEM_LIMIT = 63 * 1024 * 1024
NN = (((1,), (0,)), ((), ()))
NT = (((1,), (1,)), ((), ()))
TN = (((0,), (0,)), ((), ()))
FIRST, MLP, DOWN = 0, 1, 2
UP, DN, SIDE = 0, 1, 2
STATS = 4


def dot(a, b, dims=NN):
    return lax.dot_general(a, b, dims, preferred_element_type=F32)


def merge(value):
    n, rows, width = value.shape
    if rows % 16 == 0:
        return value.reshape(n * rows, width)
    return value.astype(F32).reshape(n * rows, width).astype(value.dtype)


def vmem_spec():
    return pl.BlockSpec(memory_space=pltpu.VMEM)


def smem_spec():
    return pl.BlockSpec(memory_space=pltpu.SMEM)


def hbm_spec():
    return pl.BlockSpec(memory_space=pl.ANY)


def grids(t):
    rows = lax.broadcasted_iota(jnp.int32, (t, t), 0)
    cols = lax.broadcasted_iota(jnp.int32, (t, t), 1)
    return rows, cols


def allowed_of(seg_row, rows, cols):
    t = rows.shape[0]
    along = jnp.broadcast_to(seg_row, (t, t))
    return (along == jnp.transpose(along)) & (cols <= rows)


def lagged(masked, taps, rows):
    parts = [masked.astype(BF)]
    for a in range(1, taps):
        parts.append(jnp.where(rows >= a, pltpu.roll(masked, a, 0), 0.0).astype(BF))
    return jnp.concatenate(parts, axis=1)


def row_sum(value):
    return jnp.sum(value, axis=0, keepdims=True)


def mean_of(value):
    return jnp.mean(value, axis=1, keepdims=True)


def layer_kernel(cfg, *refs):
    heads, hd, taps, span, docs, shards, units = cfg
    strip = units // shards
    mlp_parts = 2 if strip % 128 == 0 else 1
    given, refs = refs[: 13 + mlp_parts], refs[13 + mlp_parts :]
    x_ref, g_ref, first_norm, second_norm, head_norm, docs_ref, score_ref, mix_ref = given[:8]
    own_first, own_down, own_mlp = given[8:12], given[12], given[13:]
    (
        out_ref, grad_in_ref, grad_first_norm, grad_second_norm, grad_head_norm, grad_score, grad_mix, means,
        all_first, all_mlp, all_down,
        w_first, w_mlp, w_down, wide, g_mlp, seg_all, attn_in, qkv, hat, inv, probs, masked, head_in, w_out,
        middle, slope, silu, hidden, g_gu, g_attn, g_middle, g_qkv, g_hin, d_out_in,
        psend, pown, r1, ysend, r2, psend2, pown2, r1b, r2b, bands, corr, g_wide, lanes, g_mix,
        x_first, x_mlp, x_down, z_first, z_mlp, z_down, small_send, small_recv, small_ref, valid_ref, gain_first, gain_second, gain_all, gain_head,
        ag_send, ag_recv, rs_send, rs_recv, rs_side_recv, rep_send, rep_recv, local, credit,
    ) = refs
    t, d = x_ref.shape
    width = heads * hd
    quarter = d // 4
    lines = shards // 2
    me = lax.axis_index("rep")
    f = lax.axis_index("fsdp")
    plane, core = me // 2, me % 2
    sibling, across = plane * 2 + (1 - core), (1 - plane) * 2 + core
    diagonal = (1 - plane) * 2 + (1 - core)
    z, side = f // 2, f % 2
    partner = 2 * z + (1 - side)
    weights = (w_first, w_mlp, w_down)
    x_lands, z_lands = (x_first, x_mlp, x_down), (z_first, z_mlp, z_down)
    peer_of = (f + 2, f - 2, partner)
    tokens = 4 * t
    part = shards // 4
    rows, cols = grids(t)

    def flip(bit):
        return f + (1 - 2 * ((f // bit) % 2)) * bit

    bits = []
    bit = 1
    while bit < shards:
        bits.append(bit)
        bit *= 2

    barrier = pltpu.get_barrier_semaphore()

    def greet(r, s):
        pl.semaphore_signal(barrier, inc=1, device_id=(r, s), device_id_type=MESH)

    for r in (sibling, across, diagonal):
        greet(r, f)
    greet(me, partner)

    @pl.loop(1, lines)
    def _(s):
        greet(me, 2 * ((z + s) % lines) + side)

    pl.semaphore_wait(barrier, 3 + lines)

    def rep_copy(src, dst, slot, peer):
        return pltpu.make_async_remote_copy(
            src_ref=src, dst_ref=dst, send_sem=rep_send.at[slot], recv_sem=rep_recv.at[slot],
            device_id=(peer, f), device_id_type=MESH,
        )

    def ag(k, block, way):
        return pltpu.make_async_remote_copy(
            src_ref=weights[k].at[block], dst_ref=weights[k].at[block],
            send_sem=ag_send.at[k, way, block], recv_sem=ag_recv.at[k, block],
            device_id=(me, peer_of[way]), device_id_type=MESH,
        )

    def ag_walk(k, s, first, act):
        sides = (side, 1 - side) if k == DOWN else (side,)
        if isinstance(s, int) and s == 0:
            for q in sides:
                block = 2 * z + q
                if k == DOWN and q is not side:
                    first(k, block)

                @pl.when(z < lines - 1)
                def _():
                    act(k, block, UP)

                @pl.when(z > 0)
                def _():
                    act(k, block, DN)

                if k != DOWN:
                    act(k, block, SIDE)
            return

        @pl.when(z - s >= 0)
        def _():
            for q in sides:
                block = 2 * (z - s) + q
                first(k, block)

                @pl.when(z < lines - 1)
                def _():
                    act(k, block, UP)

                if k != DOWN:
                    act(k, block, SIDE)

        @pl.when(z + s < lines)
        def _():
            for q in sides:
                block = 2 * (z + s) + q
                first(k, block)

                @pl.when(z > 0)
                def _():
                    act(k, block, DN)

                if k != DOWN:
                    act(k, block, SIDE)

    def arrived(k, block):
        ag(k, block, SIDE).wait_recv()

    def go(k, block, way):
        ag(k, block, way).start()

    def gone(k, block, way):
        ag(k, block, way).wait_send()

    def ag_steps(k, low, high):
        if low == 0:
            ag_walk(k, 0, arrived, go)
        else:
            pl.loop(low, high)(lambda s: ag_walk(k, s, arrived, go))

    def ag_done(k):
        if k != DOWN:
            pl.loop(0, lines)(lambda zz: arrived(k, 2 * zz + (1 - side)))

    def ag_drain(k):
        nothing = lambda *_: None
        if k == DOWN:
            gone(k, f, SIDE)
        ag_walk(k, 0, nothing, gone)
        pl.loop(1, lines)(lambda s: ag_walk(k, s, nothing, gone))

    def gather_start(fulls, slot):
        for i, full in enumerate(fulls):
            rep_copy(full.at[me], full.at[me], slot + 3 * i, across).start()
            rep_copy(full.at[me], full.at[me], slot + 3 * i + 1, sibling).start()

    def gather_pass(fulls, slot):
        for i, full in enumerate(fulls):
            rep_copy(full.at[me], full.at[me], slot + 3 * i, across).wait_recv()
            rep_copy(full.at[across], full.at[across], slot + 3 * i + 2, sibling).start()

    def gather_end(fulls, slot):
        for i, full in enumerate(fulls):
            rep_copy(full.at[me], full.at[me], slot + 3 * i + 1, sibling).wait_recv()
            rep_copy(full.at[across], full.at[across], slot + 3 * i + 2, sibling).wait_recv()
        for i, full in enumerate(fulls):
            rep_copy(full.at[me], full.at[me], slot + 3 * i, across).wait_send()
            rep_copy(full.at[me], full.at[me], slot + 3 * i + 1, sibling).wait_send()
            rep_copy(full.at[across], full.at[across], slot + 3 * i + 2, sibling).wait_send()

    def pair_of(ref, a, b):
        return jnp.concatenate([ref[a], ref[b]], axis=0)

    def sum_copies(slot, send_buf, first_land, second_land):
        return (
            rep_copy(send_buf, first_land, slot, sibling),
            rep_copy(ysend, second_land, slot + 1, across),
        )

    def column_chunk(i):
        return pl.ds(pl.multiple_of(i * quarter, quarter), quarter)

    def sum_theirs(product, copies, send_buf):
        @pl.loop(0, 4)
        def _(i):
            value = product(1 - core, 2 + (1 - core), i)
            send_buf[0, :, column_chunk(i)] = value[:t].astype(BF)
            send_buf[1, :, column_chunk(i)] = value[t:].astype(BF)

        copies[0].start()

    def sum_ours(product, own_buf):
        @pl.loop(0, 4)
        def _(i):
            value = product(across, me, i)
            own_buf[0, :, column_chunk(i)] = value[:t].astype(own_buf.dtype)
            own_buf[1, :, column_chunk(i)] = value[t:].astype(own_buf.dtype)

    def sum_turn(copies, own_buf, first_land):
        copies[0].wait_recv()
        ysend[...] = (own_buf[0].astype(F32) + first_land[1 - plane].astype(F32)).astype(BF)
        copies[1].start()
        own_buf[1] = (own_buf[1].astype(F32) + first_land[plane].astype(F32)).astype(own_buf.dtype)

    def sum_end(copies, own_buf, second_land):
        copies[1].wait_recv()
        total = own_buf[1].astype(F32) + second_land[...].astype(F32)
        copies[0].wait_send()
        copies[1].wait_send()
        return total

    def yes(condition):
        return int(condition) if isinstance(condition, bool) else condition.astype(jnp.int32)

    def far_slot(at, target):
        return at if lines == 4 else target

    def near_slot(source, target):
        return source if lines == 4 else lines + source - target + 2 - yes(source > target)

    def target_of(s):
        ahead = lines - 1 - z
        first_end, last_end = yes(z == 0), yes(z == lines - 1)
        inner = 1 - first_end - last_end
        if lines == 4:
            near = yes(s == 1) * (z + 1) + yes(s == 2) * (z - 1) + yes(s == 3) * (3 * (2 - z))
        else:
            near = yes(s <= ahead) * (z + s) + yes(s > ahead) * (z - (s - ahead))
        return first_end * (lines - s) + last_end * (s - 1) + inner * near

    def rs_side(k, zz):
        source = weights[k].at[2 * zz + (1 - side)]
        if k == DOWN:
            source = x_mlp.at[zz, pl.ds(0, strip), pl.ds(0, d)]
        return pltpu.make_async_remote_copy(
            src_ref=source, dst_ref=x_lands[k].at[zz],
            send_sem=rs_send.at[k, 0, zz], recv_sem=rs_side_recv.at[k, zz],
            device_id=(me, partner), device_id_type=MESH,
        )

    def rs_hop(k, target):
        up = yes(target > z)
        toward = z + 2 * up - 1
        distance = up * (target - z) + (1 - up) * (z - target)
        far = yes(distance >= 3)
        to = far * toward + (1 - far) * target
        slot = far * far_slot(toward, target) + (1 - far) * near_slot(z, target)
        at = slot
        return pltpu.make_async_remote_copy(
            src_ref=weights[k].at[2 * target + side], dst_ref=z_lands[k].at[at],
            send_sem=rs_send.at[k, 1, 2 * target], recv_sem=rs_recv.at[k, at],
            device_id=(me, 2 * to + side), device_id_type=MESH,
        )

    def rs_landed(k, slot):
        at = slot
        pltpu.make_async_remote_copy(
            src_ref=weights[k].at[f], dst_ref=z_lands[k].at[at],
            send_sem=rs_send.at[k, 1, f], recv_sem=rs_recv.at[k, at],
            device_id=(me, partner), device_id_type=MESH,
        ).wait_recv()
        return z_lands[k], at

    def rs_add(k, block, landed):
        grad = weights[k]
        high = grad.shape[1]
        step = 16 if high % 16 == 0 else high

        @pl.loop(0, high // step)
        def _(i):
            at = pl.ds(pl.multiple_of(i * step, step), step)
            total = grad[block, at, :].astype(F32)
            for land, slot in landed:
                total = total + land[slot, at, :].astype(F32)
            grad[block, at, :] = total.astype(BF)

    def rs_turn(k, s):
        target = target_of(s)
        up = yes(target > z)
        distance = up * (target - z) + (1 - up) * (z - target)
        behind = up * yes(z > 0) + (1 - up) * yes(z < lines - 1)
        rs_side(k, target).wait_recv()
        handed = (distance >= 2) & (behind == 1)

        @pl.when(handed)
        def _():
            land = rs_landed(k, far_slot(z, target))
            rs_add(k, 2 * target + side, [(x_lands[k], target), land])

        @pl.when(jnp.logical_not(handed))
        def _():
            rs_add(k, 2 * target + side, [(x_lands[k], target)])

        rs_hop(k, target).start()

    def rs_close(k):
        first_end, last_end = yes(z == 0), yes(z == lines - 1)
        inner = 1 - first_end - last_end
        one = first_end * 1 + (1 - first_end) * (z - 1)
        two = first_end * 2 + last_end * (lines - 3) + inner * (z + 1)
        rs_side(k, z).wait_recv()
        rs_add(k, f, [(x_lands[k], z), rs_landed(k, near_slot(one, z)), rs_landed(k, near_slot(two, z))])

        @pl.when((z > 0) & (z + 2 < lines))
        def _():
            rs_add(k, f, [rs_landed(k, near_slot(z + 2, z))])

        @pl.when((z < lines - 1) & (z >= 2))
        def _():
            rs_add(k, f, [rs_landed(k, near_slot(z - 2, z))])

    def rs_drain(k):
        if k != DOWN:
            pl.loop(0, lines)(lambda zz: rs_side(k, zz).wait_send())
        pl.loop(1, lines)(lambda s: rs_hop(k, target_of(s)).wait_send())

    outs = (all_first, all_mlp, all_down)

    def final_copies(k, slot):
        own = weights[k].at[f]
        full = outs[k]
        return (
            rep_copy(own, full.at[me], slot, across),
            rep_copy(own, full.at[me], slot + 1, sibling),
            rep_copy(full.at[across], full.at[across], slot + 2, sibling),
            pltpu.make_async_copy(own, full.at[me], local.at[1 + k]),
        )

    def final_start(k, slot):
        a, b, _, here = final_copies(k, slot)
        a.start()
        b.start()
        here.start()

    def final_pass(k, slot):
        a, _, c, _ = final_copies(k, slot)
        a.wait_recv()
        c.start()

    def final_end(k, slot):
        a, b, c, here = final_copies(k, slot)
        b.wait_recv()
        c.wait_recv()
        a.wait_send()
        b.wait_send()
        c.wait_send()
        here.wait()

    def cut(ref, at, size):
        return ref.at[:, pl.ds(pl.multiple_of(at, size), size)]

    sources = [
        [(cut(own_first[i], me * quarter, quarter), w_first.at[f, :, pl.ds(i * quarter, quarter)]) for i in range(4)],
        [(own_mlp[0], w_mlp.at[f])],
        [(own_down.at[pl.ds(pl.multiple_of(me * strip, strip), strip), :], w_down.at[f])],
    ]
    if mlp_parts == 2:
        sources[MLP] = [
            (cut(own_mlp[i // shards], (4 * (i % shards) + me) * strip, strip), w_mlp.at[f, :, pl.ds(i * strip, strip)])
            for i in range(2 * shards)
        ]
    loads, used = [], 4
    for pairs in sources:
        loads.append([pltpu.make_async_copy(a, b, local.at[used + i]) for i, (a, b) in enumerate(pairs)])
        used += len(pairs)
    for k in range(3):
        for load in loads[k]:
            load.start()

    def load_wait(k):
        for load in loads[k]:
            load.wait()

    load_wait(FIRST)
    ag_steps(FIRST, 0, 1)
    load_wait(DOWN)
    ag(DOWN, f, SIDE).start()

    lane = lax.broadcasted_iota(jnp.int32, (1, t), 1)
    seg = jnp.zeros((1, t), F32)
    edge = 0
    for i in range(docs):
        edge = edge + docs_ref[0, i]
        seg = seg + jnp.where(lane >= edge, 1.0, 0.0)
    valid = jnp.where(jnp.transpose(jnp.broadcast_to(seg, (t, t))) < float(docs), 1.0, 0.0)
    valid_ref[...] = valid[:, 0:1]

    def as_row(ref):
        return jnp.concatenate([ref[i : i + 1, :] for i in range(ref.shape[0])], axis=1)

    gain_first[...] = as_row(first_norm)
    gain_second[...] = as_row(second_norm)
    gain_all[...] = as_row(head_norm)
    gain_head[...] = gain_all[:, pl.ds(pl.multiple_of(me * quarter, quarter), quarter)]
    wide[me] = x_ref[...]
    g_mlp[me] = g_ref[...]
    seg_all[me] = jnp.broadcast_to(seg, (8, t))
    entering = (seg_all, wide)
    gather_start(entering, 0)

    diff = cols - rows + (span - 1) // 2

    @pl.loop(0, heads)
    def _(h):
        for a in range(taps):
            band = jnp.zeros((t, t), F32)
            for b in range(span):
                band = jnp.where(diff == b, score_ref[me * heads + h, a, b], band)
            bands[h, a * t : (a + 1) * t, :] = band.astype(BF)

    gather_pass(entering, 0)
    gather_start((g_mlp,), 6)
    ag_steps(FIRST, 1, 2)
    gather_end(entering, 0)

    @pl.loop(0, 4)
    def _(r):
        value = wide[r].astype(F32)
        scale = lax.rsqrt(mean_of(value * value) + 1e-06)
        attn_in[r] = (value * scale * gain_first[...]).astype(BF)

    ag_steps(FIRST, 2, 3)
    load_wait(MLP)
    ag_steps(MLP, 0, 1)
    gather_pass((g_mlp,), 6)
    gather_end((g_mlp,), 6)

    @pl.loop(0, 4)
    def _(r):
        valid = jnp.transpose(jnp.broadcast_to(seg_all[r][0:1, :], (t, t)))[:, 0:1] < float(docs)
        g_mlp[r] = jnp.where(valid, g_mlp[r].astype(F32), 0.0).astype(BF)

    ag_steps(FIRST, 3, lines)
    ag_steps(MLP, 1, 2)
    ag_done(FIRST)

    def w_out_copy(peer, slot):
        return rep_copy(
            w_first.at[pl.ds(peer * part, part), :, pl.ds(3 * quarter, quarter)],
            w_out.at[:, :, pl.ds(pl.multiple_of(me * quarter, quarter), quarter)],
            slot, peer,
        )

    for i, peer in enumerate((sibling, across, diagonal)):
        w_out_copy(peer, 9 + i).start()
    own_out = pltpu.make_async_copy(
        w_first.at[pl.ds(me * part, part), :, pl.ds(3 * quarter, quarter)],
        w_out.at[:, :, pl.ds(pl.multiple_of(me * quarter, quarter), quarter)],
        local.at[0],
    )
    own_out.start()

    for i in range(3):
        value = dot(attn_in[...].reshape(tokens, d), merge(w_first[:, :, i * quarter : (i + 1) * quarter]))
        qkv[:, :, i * quarter : (i + 1) * quarter] = value.astype(BF).reshape(4, t, quarter)
    ag_steps(MLP, 2, 3)
    ag_steps(DOWN, 0, 1)

    def split(ref, row, kind, h):
        return ref[row, :, kind * width + h * hd : kind * width + (h + 1) * hd]

    @pl.loop(0, 4)
    def _(row):
        allowed = allowed_of(seg_all[row][0:1, :], rows, cols)
        for pair in range(heads // 2):
            both = []
            for c in range(2):
                h = 2 * pair + c
                scores = dot(split(qkv, row, 0, h), split(qkv, row, 1, h), NT) * hd**-0.5
                kept = jnp.where(allowed, scores, 0.0)
                masked[row, h] = kept.astype(BF)
                logits = jnp.where(allowed, dot(lagged(kept, taps, rows), bands[h]), -1e30)
                e = jnp.exp(logits - jnp.max(logits, axis=1, keepdims=True))
                p = e / jnp.sum(e, axis=1, keepdims=True)
                probs[row, h] = p
                both.append(p)
            for e in range(2):
                h = 2 * pair + e
                mixed = (mix_ref[me * heads + h, 0] * both[0] + mix_ref[me * heads + h, 1] * both[1]).astype(BF)
                out = dot(mixed, split(qkv, row, 2, h))
                centred = out - mean_of(out)
                scale = lax.rsqrt(mean_of(centred * centred) + 1e-05)
                hat[row, :, h * hd : (h + 1) * hd] = centred * scale
                inv[row, :, h : h + 1] = scale
        head_in[row] = (hat[row] * gain_head[...]).astype(BF)

    for i, peer in enumerate((sibling, across, diagonal)):
        w_out_copy(peer, 9 + i).wait_recv()
    own_out.wait()

    copies = sum_copies(12, psend, r1, r2)
    product = lambda a, b, i: dot(pair_of(head_in, a, b), merge(w_out[:, :, column_chunk(i)]))
    sum_theirs(product, copies, psend)
    sum_ours(product, pown)
    ag_steps(MLP, 3, lines)
    sum_turn(copies, pown, r1)
    total = sum_end(copies, pown, r2)
    attn_part = valid_ref[...] * total
    value = x_ref[...].astype(F32) + attn_part
    middle[...] = value
    stat_attn = jnp.sum(row_sum(attn_part * attn_part), axis=1, keepdims=True)
    scale = lax.rsqrt(mean_of(value * value) + 1e-06)
    wide[me] = (value * scale * gain_second[...]).astype(BF)
    gather_start((wide,), 14)
    ag_steps(DOWN, 1, 2)
    gather_pass((wide,), 14)
    gather_end((wide,), 14)
    mlp_in = wide
    ag_steps(DOWN, 2, 3)
    ag_done(MLP)

    chunk = units // 4

    def in_turn(i):
        if lines != 4:
            return i
        return yes(i < 3) * target_of(i + 1) + yes(i == 3) * z


    @pl.loop(0, 4)
    def _(i):
        p = in_turn(i)
        at = pl.ds(pl.multiple_of(p * chunk, chunk), chunk)
        after = pl.ds(pl.multiple_of(units + p * chunk, chunk), chunk)
        operand = mlp_in[...].reshape(tokens, d)
        gate = dot(operand, merge(w_mlp[:, :, at]))
        upper = dot(operand, merge(w_mlp[:, :, after]))
        sig = 1.0 / (1.0 + jnp.exp(-gate))
        act = gate * sig
        product = (act * upper).astype(BF)
        hidden[:, :, at] = product.reshape(4, t, chunk)
        silu[:, at] = act.astype(BF)
        slope[:, at] = (upper * sig * (1.0 + gate * (1.0 - sig))).astype(BF)
        value = dot(product, g_mlp[...].reshape(tokens, d), TN).reshape(part, strip, d)
        for j in range(part // 2):
            half = jnp.where(side == 0, value[2 * j + 1], value[2 * j])
            x_mlp[p * (part // 2) + j, 0:strip, 0:d] = half.astype(BF)
        pl.loop(0, part // 2)(lambda j: rs_side(DOWN, p * (part // 2) + j).start())

    ag_steps(DOWN, 3, lines)

    @pl.loop(0, 4)
    def _(i):
        span_units = units // 4
        at = pl.ds(pl.multiple_of(i * span_units, span_units), span_units)
        after = pl.ds(pl.multiple_of(units + i * span_units, span_units), span_units)
        g_hidden = dot(g_mlp[...].reshape(tokens, d), merge(w_down[pl.ds(i * part, part)]), NT)
        g_gu[:, :, at] = (g_hidden * slope[:, at].astype(F32)).astype(BF).reshape(4, t, span_units)
        g_gu[:, :, after] = (g_hidden * silu[:, at].astype(F32)).astype(BF).reshape(4, t, span_units)

    mlp_copies = sum_copies(17, psend, r1, r2)
    product = lambda a, b, i: dot(pair_of(g_gu, a, b), merge(w_mlp[pl.ds(i * part, part)]), NT)
    sum_theirs(product, mlp_copies, psend)
    sum_ours(product, pown)

    sum_turn(mlp_copies, pown, r1)

    ag_drain(MLP)

    def send_side(k, p):
        @pl.loop(0, part // 2)
        def _(j):
            zz = p * (part // 2) + j
            rs_side(k, zz).start()

    @pl.loop(0, 4)
    def _(p):
        at = pl.ds(pl.multiple_of(p * quarter, quarter), quarter)
        size = units // 2

        @pl.loop(0, 4)
        def _(j):
            to = pl.ds(pl.multiple_of(j * size, size), size)
            value = dot(mlp_in[:, :, at].reshape(tokens, quarter), g_gu[:, :, to].reshape(tokens, size), TN)
            w_mlp[pl.ds(p * part, part), :, to] = value.reshape(part, w_mlp.shape[1], size).astype(BF)

    total = sum_end(mlp_copies, pown, r2)
    value = middle[...]
    scale = lax.rsqrt(mean_of(value * value) + 1e-06)
    normed = value * scale
    prod = total * normed
    g_second = row_sum(prod)
    mean = mean_of(prod * gain_second[...])
    value = g_ref[...].astype(F32) + scale * (total * gain_second[...] - normed * mean)
    g_middle[...] = value
    g_attn[me] = (valid_ref[...] * value).astype(BF)
    gather_start((g_attn,), 21)
    out_copies = (rep_copy(psend2, r1b, 19, sibling), rep_copy(ysend, r2b, 20, across))
    product = lambda a, b, i: dot(pair_of(hidden, a, b), merge(w_down[:, :, column_chunk(i)]))
    sum_theirs(product, out_copies, psend2)
    sum_ours(product, pown2)
    ag_drain(DOWN)

    @pl.loop(0, 4)
    def _(i):
        span_units = units // 4
        at = pl.ds(pl.multiple_of(i * span_units, span_units), span_units)
        value = dot(hidden[:, :, at].reshape(tokens, span_units), g_mlp[...].reshape(tokens, d), TN)
        w_down[pl.ds(i * part, part)] = value.reshape(part, w_down.shape[1], d).astype(BF)

    pl.loop(0, lines)(lambda zz: rs_side(DOWN, zz).wait_send())
    pl.semaphore_signal(credit, inc=1, device_id=(me, partner), device_id_type=MESH)

    pl.semaphore_wait(credit, 1)
    pl.loop(1, lines)(lambda s: rs_side(MLP, target_of(s)).start())
    rs_side(MLP, z).start()

    gather_pass((g_attn,), 21)
    gather_end((g_attn,), 21)

    @pl.loop(0, 2)
    def _(i):
        both = pl.ds(2 * i, 2)
        value = dot(g_attn[both].reshape(2 * t, d), merge(w_out[...]), NT)
        g_hin[both] = value.reshape(2, t, width)

    d_out = w_out

    @pl.loop(0, 4)
    def _(i):
        value = dot(head_in[...].reshape(tokens, width), g_attn[:, :, column_chunk(i)].reshape(tokens, quarter), TN)
        d_out[:, :, column_chunk(i)] = value.reshape(part, w_first.shape[1], quarter).astype(BF)


    def d_out_copy(peer, slot):
        return rep_copy(
            d_out.at[:, :, pl.ds(pl.multiple_of(peer * quarter, quarter), quarter)],
            d_out_in.at[pl.ds(me * part, part)],
            slot, peer,
        )

    for i, peer in enumerate((sibling, across, diagonal)):
        d_out_copy(peer, 24 + i).start()
    own_d_out = pltpu.make_async_copy(
        d_out.at[:, :, pl.ds(pl.multiple_of(me * quarter, quarter), quarter)],
        d_out_in.at[pl.ds(me * part, part)], local.at[4],
    )
    own_d_out.start()
    pl.loop(1, lines)(lambda s: rs_turn(DOWN, s))

    corr[...] = jnp.zeros_like(corr)
    g_mix[...] = jnp.zeros_like(g_mix)
    lanes[...] = jnp.zeros_like(lanes)

    @pl.loop(0, 4)
    def _(row):
        allowed = allowed_of(seg_all[row][0:1, :], rows, cols)
        g_wide[...] = g_hin[row] * gain_head[...]
        for pair in range(heads // 2):
            g_heads, g_mixed = [], []
            both = [probs[row, 2 * pair + c] for c in range(2)]
            for e in range(2):
                h = 2 * pair + e
                scaled = g_wide[:, h * hd : (h + 1) * hd]
                own_hat = hat[row, :, h * hd : (h + 1) * hd]
                g = inv[row, :, h : h + 1] * (scaled - mean_of(scaled) - own_hat * mean_of(scaled * own_hat))
                g = g.astype(BF)
                g_heads.append(g)
                g_mixed.append(dot(g, split(qkv, row, 2, h), NT))
            for e in range(2):
                h = 2 * pair + e
                mixed = (mix_ref[me * heads + h, 0] * both[0] + mix_ref[me * heads + h, 1] * both[1]).astype(BF)
                g_v = dot(mixed, g_heads[e], TN)
                g_qkv[row, :, 2 * width + h * hd : 2 * width + (h + 1) * hd] = g_v.astype(BF)
                for c in range(2):
                    place = (2 * pair + e) * 2 + c
                    g_mix[place : place + 1, :] += row_sum(g_mixed[e] * both[c])
            for c in range(2):
                h = 2 * pair + c
                g_probs = mix_ref[me * heads + 2 * pair, c] * g_mixed[0] + mix_ref[me * heads + 2 * pair + 1, c] * g_mixed[1]
                weighted = both[c] * g_probs
                g_conv = weighted - both[c] * jnp.sum(weighted, axis=1, keepdims=True)
                corr[h] += dot(lagged(masked[row, h].astype(F32), taps, rows), g_conv.astype(BF), TN)
                g_kept = dot(g_conv.astype(BF), bands[h, 0:t, :], NT)
                for a in range(1, taps):
                    lead = jnp.where(rows < t - a, pltpu.roll(g_conv, t - a, 0), 0.0).astype(BF)
                    g_kept += dot(lead, bands[h, a * t : (a + 1) * t, :], NT)
                g_raw = jnp.where(allowed, g_kept, 0.0).astype(BF)
                g_q = dot(g_raw, split(qkv, row, 1, h)) * hd**-0.5
                g_k = dot(g_raw, split(qkv, row, 0, h), TN) * hd**-0.5
                g_qkv[row, :, h * hd : (h + 1) * hd] = g_q.astype(BF)
                g_qkv[row, :, width + h * hd : width + (h + 1) * hd] = g_k.astype(BF)

    rs_turn(MLP, 1)
    in_copies = sum_copies(27, psend, r1, r2)
    product = lambda a, b, i: dot(pair_of(g_qkv, a, b), merge(w_first[pl.ds(i * part, part), :, 0 : 3 * quarter]), NT)
    sum_theirs(product, in_copies, psend)
    sum_ours(product, pown)
    sum_turn(in_copies, pown, r1)

    ag_drain(FIRST)
    for i, peer in enumerate((sibling, across, diagonal)):
        w_out_copy(peer, 9 + i).wait_send()
        d_out_copy(peer, 24 + i).wait_recv()
    own_d_out.wait()

    @pl.loop(0, 4)
    def _(i):
        p = in_turn(i)
        at = pl.ds(pl.multiple_of(p * quarter, quarter), quarter)
        value = dot(attn_in[:, :, at].reshape(tokens, quarter), g_qkv[...].reshape(tokens, 3 * quarter), TN)
        w_first[pl.ds(p * part, part), :, 0 : 3 * quarter] = value.reshape(part, w_first.shape[1], 3 * quarter).astype(BF)
        w_first[pl.ds(p * part, part), :, 3 * quarter :] = d_out_in[pl.ds(p * part, part)]
        send_side(FIRST, p)

    rs_turn(MLP, 2)
    total = sum_end(in_copies, pown, r2)
    value = x_ref[...].astype(F32)
    scale = lax.rsqrt(mean_of(value * value) + 1e-06)
    normed = value * scale
    prod = total * normed
    g_first = row_sum(prod)
    mean = mean_of(prod * gain_first[...])
    grad_in_ref[...] = (g_middle[...] + scale * (total * gain_first[...] - normed * mean)).astype(BF)

    sum_turn(out_copies, pown2, r1b)
    total = sum_end(out_copies, pown2, r2b)
    mlp_part = valid_ref[...] * total
    value = middle[...] + mlp_part
    out_ref[...] = value.astype(BF)
    stat_out = jnp.sum(row_sum(valid_ref[...] * value * value), axis=1, keepdims=True)
    stat_mlp = jnp.sum(row_sum(mlp_part * mlp_part), axis=1, keepdims=True)

    strips = d // 128
    small_ref[...] = jnp.zeros_like(small_ref)
    for i in range(strips):
        at = slice(128 * i, 128 * (i + 1))
        small_ref[i : i + 1, :] = g_first[:, at]
        small_ref[strips + i : strips + i + 1, :] = g_second[:, at]
    own_gain = row_sum((g_hin[...] * hat[...]).reshape(tokens, width))
    for i in range(width // 128):
        small_ref[pl.ds(2 * strips + me * (width // 128) + i, 1), :] = own_gain[:, 128 * i : 128 * (i + 1)]
    base = 3 * strips
    for h in range(heads):
        for a in range(taps):
            tile = corr[h, a * t : (a + 1) * t, :]
            for b in range(span):
                lanes[a * span + b : a * span + b + 1, :] = row_sum(jnp.where(diff == b, tile, 0.0))
        small_ref[pl.ds(base + me * heads + h, 1), :] = row_sum(jnp.transpose(lanes[...]))
    base += 4 * heads
    lanes[0 : 2 * heads, :] = g_mix[...]
    lanes[2 * heads :, :] = jnp.zeros((t - 2 * heads, t), F32)
    small_ref[pl.ds(base + me, 1), :] = row_sum(jnp.transpose(lanes[...]))
    base += 4
    lane = lax.broadcasted_iota(jnp.int32, (1, 128), 1)
    count = jnp.sum(row_sum(jnp.broadcast_to(valid_ref[...], (t, 128))), axis=1, keepdims=True) * (1.0 / 128.0)
    stats = jnp.zeros((1, 128), F32)
    for i, stat in enumerate((stat_out, stat_attn, stat_mlp, count)):
        stats = jnp.where(lane == i, stat, stats)
    small_ref[base : base + 1, :] = stats

    peers = [(sibling, f), (across, f)] + [(me, flip(bit)) for bit in bits]

    def small_copy(i):
        return pltpu.make_async_remote_copy(
            src_ref=small_send.at[i], dst_ref=small_recv.at[i],
            send_sem=rep_send.at[40 + i], recv_sem=rep_recv.at[40 + i],
            device_id=peers[i], device_id_type=MESH,
        )

    def small_step(i):
        small_send[i] = small_ref[...]
        small_copy(i).start()

    def small_take(i):
        small_copy(i).wait_recv()
        small_ref[...] = small_ref[...] + small_recv[i]

    rs_close(DOWN)
    final_start(DOWN, 30)
    pl.loop(3, lines)(lambda s: rs_turn(MLP, s))
    final_pass(DOWN, 30)
    small_step(0)
    small_take(0)
    small_step(1)
    rs_turn(FIRST, 1)
    rs_close(MLP)
    final_start(MLP, 33)
    small_take(1)
    small_step(2)
    pl.loop(2, lines)(lambda s: rs_turn(FIRST, s))
    final_pass(MLP, 33)
    rs_close(FIRST)
    final_start(FIRST, 36)
    for i in range(2, len(peers)):
        small_take(i)
        if i + 1 < len(peers):
            small_step(i + 1)
    final_pass(FIRST, 36)
    grad_first_norm[...] = small_ref[0:strips, :]
    grad_second_norm[...] = small_ref[strips : 2 * strips, :]
    grad_head_norm[...] = small_ref[2 * strips : 3 * strips, :]
    at = 3 * strips
    grad_score[...] = small_ref[at : at + 4 * heads, :]
    grad_mix[...] = small_ref[at + 4 * heads : at + 4 * heads + 4, :]
    sums = small_ref[at + 4 * heads + 4 : at + 4 * heads + 5, :]
    means[...] = jnp.sqrt(sums / (sums[:, 3:4] * float(d)))
    for k in range(3):
        final_end(k, (36, 33, 30)[k])
    for k in range(3):
        rs_drain(k)
    for i in range(len(peers)):
        small_copy(i).wait_send()
    for i, peer in enumerate((sibling, across, diagonal)):
        d_out_copy(peer, 24 + i).wait_send()


def run_layer(cfg, vectors, scalars, first_in, down_in, mlp_in, sizes):
    heads, hd, taps, span, docs, shards, units = cfg
    t, d = vectors[0].shape
    width = heads * hd
    first, mlp, down = shards_in = sizes
    bits = shards.bit_length() - 1
    lines = shards // 2
    slots = lines if lines == 4 else lines + 4

    def shape(dtype, *dims):
        return jax.ShapeDtypeStruct(dims, dtype)

    v = pltpu.VMEM
    dma = pltpu.SemaphoreType.DMA
    out_shape = (
        shape(BF, t, d), shape(BF, t, d), *(shape(F32, d // 128, 128) for _ in range(3)),
        shape(F32, 4 * heads, 128), shape(F32, 4, 128), shape(F32, 1, 128),
        *(shape(BF, 4, *s.shape) for s in shards_in),
    )
    scratch = [
        *(v((shards, *s.shape), BF) for s in shards_in),
        v((4, t, d), BF), v((4, t, d), BF), v((4, 8, t), F32), v((4, t, d), BF), v((4, t, 3 * width), BF),
        v((4, t, width), F32), v((4, t, 128), F32), v((4, heads, t, t), F32), v((4, heads, t, t), BF),
        v((4, t, width), BF), v((shards // 4, first.shape[0], d), BF),
        v((t, d), F32), v((4 * t, units), BF), v((4 * t, units), BF), v((4, t, units), BF), v((4, t, 2 * units), BF),
        v((4, t, d), BF), v((t, d), F32), v((4, t, 3 * width), BF), v((4, t, width), F32),
        v((shards, first.shape[0], width), BF),
        v((2, t, d), BF), v((2, t, d), BF), v((2, t, d), BF), v((t, d), BF), v((t, d), BF),
        v((2, t, d), BF), v((2, t, d), BF), v((2, t, d), BF), v((t, d), BF),
        v((heads, taps * t, t), BF), v((heads, taps * t, t), F32), v((t, width), F32), v((t, t), F32), v((2 * heads, t), F32),
        *(v((lines, *s.shape), BF) for s in shards_in), *(v((slots, *s.shape), BF) for s in shards_in), v((2 + bits, 64, 128), F32), v((2 + bits, 64, 128), F32),
        v((64, 128), F32), v((t, 1), F32), v((1, d), F32), v((1, d), F32), v((1, d), F32), v((1, width), F32),
        dma((3, 3, shards)), dma((3, shards)), dma((3, 2, shards)), dma((3, slots)), dma((3, lines)), dma((48,)), dma((48,)), dma((10 + 2 * shards,)), pltpu.SemaphoreType.REGULAR,
    ]
    return pl.pallas_call(
        functools.partial(layer_kernel, cfg),
        out_shape=out_shape,
        in_specs=[vmem_spec()] * 5 + [smem_spec()] * 3 + [hbm_spec()] * (5 + len(mlp_in)),
        out_specs=(vmem_spec(),) * 8 + (hbm_spec(),) * 3,
        scratch_shapes=scratch,
        compiler_params=pltpu.CompilerParams(
            collective_id=0, has_side_effects=True, vmem_limit_bytes=VMEM_LIMIT
        ),
    )(*vectors, *scalars, *first_in, down_in, *mlp_in)


def widen_kernel(strip, count, first_ref, mlp_ref, down_ref, *outs):
    quarter = first_ref.shape[2] // 4
    for r in range(4):
        for k in range(4):
            outs[k][:, r * quarter : (r + 1) * quarter] = first_ref[r, :, k * quarter : (k + 1) * quarter].astype(F32)
        outs[6][r] = down_ref[r].astype(F32)
        for k in range(2):
            for i in range(count):
                at = (4 * i + r) * strip
                outs[4 + k][:, at : at + strip] = mlp_ref[r, :, (k * count + i) * strip : (k * count + i + 1) * strip].astype(F32)


def widen(first, mlp, down, strip, count):
    _, rows, d = first.shape
    steps = 4 if rows % 64 == 0 and down.shape[1] % 64 == 0 else 1
    hidden = 4 * strip * count
    rows_step, down_step = rows // steps, down.shape[1] // steps

    def taken(array, size):
        return pl.BlockSpec((4, size, array.shape[2]), lambda i: (0, i, 0))

    def given(size, width):
        return pl.BlockSpec((size, width), lambda i: (i, 0))

    return pl.pallas_call(
        functools.partial(widen_kernel, strip, count),
        grid=(steps,),
        out_shape=tuple(jax.ShapeDtypeStruct((rows, d), F32) for _ in range(4))
        + tuple(jax.ShapeDtypeStruct((rows, hidden), F32) for _ in range(2))
        + (jax.ShapeDtypeStruct(down.shape, F32),),
        in_specs=[taken(first, rows_step), taken(mlp, rows_step), taken(down, down_step)],
        out_specs=tuple(given(rows_step, d) for _ in range(4))
        + tuple(given(rows_step, hidden) for _ in range(2))
        + (taken(down, down_step),),
        compiler_params=pltpu.CompilerParams(vmem_limit_bytes=VMEM_LIMIT),
    )(first, mlp, down)


def per_device(
    hidden_in,
    doc_lengths,
    w_query,
    w_key,
    w_value,
    w_output,
    w_gate,
    w_up,
    w_down,
    attn_norm,
    mlp_norm,
    head_norm,
    score_kernel,
    head_mixing,
    grad_out,
):
    _, t, d = hidden_in.shape
    reps = lax.axis_size("rep")
    shards = lax.axis_size("fsdp")
    me = lax.axis_index("rep")
    hidden = w_gate.shape[1]
    heads = H // reps
    hd = d // H
    quarter = d // reps
    units = hidden // reps
    strip = units // shards
    taps, span = score_kernel.shape[1:]
    docs = doc_lengths.shape[1] - 1
    rows_here = w_gate.shape[0]

    def mine(array, size, axis):
        return lax.dynamic_slice_in_dim(array, me * size, size, axis)

    def strips(w):
        return mine(w.reshape(rows_here, shards, reps, strip), 1, 2).reshape(rows_here, units)

    if strip % 128 == 0:
        mlp_in = (w_gate, w_up)
    else:
        mlp_in = (jnp.concatenate([strips(w_gate), strips(w_up)], axis=1),)
    lines = d // 128
    cfg = (heads, hd, taps, span, docs, shards, units)
    shape_of = jax.ShapeDtypeStruct
    block_out, grad_in, n_first, n_second, n_head, g_score, g_mix, means, a_first, a_mlp, a_down = run_layer(
        cfg,
        (hidden_in.reshape(t, d), grad_out.reshape(t, d), *(n.reshape(lines, 128) for n in (attn_norm, mlp_norm, head_norm))),
        (doc_lengths, score_kernel, head_mixing),
        (w_query, w_key, w_value, w_output),
        w_down,
        mlp_in,
        (shape_of((rows_here, d), BF), shape_of((rows_here, 2 * units), BF), shape_of((strip, d), BF)),
    )
    if strip % 128 == 0:
        g_q, g_k, g_v, g_o, g_gate, g_up, g_down = widen(a_first, a_mlp, a_down, strip, shards)
    else:
        first = a_first.astype(F32).reshape(reps, rows_here, 4, quarter)
        first = jnp.moveaxis(first, 0, 2).reshape(rows_here, 4, d)
        g_q, g_k, g_v, g_o = (first[:, k] for k in range(4))
        mlp = a_mlp.astype(F32).reshape(reps, rows_here, 2, shards, strip)
        mlp = jnp.moveaxis(mlp, 0, 3).reshape(rows_here, 2, hidden)
        g_gate, g_up = mlp[:, 0], mlp[:, 1]
        g_down = a_down.astype(F32)
    return (
        block_out.reshape(hidden_in.shape),
        grad_in.reshape(hidden_in.shape),
        g_q,
        g_k,
        g_v,
        g_o,
        g_gate,
        g_up,
        g_down.reshape(w_down.shape),
        n_first.reshape(d),
        n_second.reshape(d),
        n_head.reshape(d),
        g_score[:, : taps * span].reshape(score_kernel.shape),
        g_mix[:, : 2 * heads].reshape(head_mixing.shape),
        means[0, :3],
    )


def solution(mesh):
    rows = P(("rep", "fsdp"), None, None)
    split = P("fsdp", None)
    placed = (rows, P(("rep", "fsdp"), None)) + (split,) * 7 + (P(),) * 5 + (rows,)
    return jax.shard_map(
        per_device,
        mesh=mesh,
        in_specs=placed,
        out_specs=(rows, rows) + (split,) * 7 + (P(),) * 6,
        check_vma=False,
    )
```

```python
import functools

import jax
import jax.numpy as jnp
from jax import lax
from jax.experimental import pallas as pl
from jax.experimental.pallas import tpu as pltpu
from jax.sharding import PartitionSpec as P

H = 16
BF = jnp.bfloat16
F32 = jnp.float32
MESH = pl.DeviceIdType.MESH
VMEM_LIMIT = 63 * 1024 * 1024
NN = (((1,), (0,)), ((), ()))
NT = (((1,), (1,)), ((), ()))
TN = (((0,), (0,)), ((), ()))
FIRST, MLP, DOWN = 0, 1, 2
UP, DN, SIDE = 0, 1, 2
STATS = 4


def dot(a, b, dims=NN):
    return lax.dot_general(a, b, dims, preferred_element_type=F32)


def merge(value):
    n, rows, width = value.shape
    if rows % 16 == 0:
        return value.reshape(n * rows, width)
    return value.astype(F32).reshape(n * rows, width).astype(value.dtype)


def vmem_spec():
    return pl.BlockSpec(memory_space=pltpu.VMEM)


def smem_spec():
    return pl.BlockSpec(memory_space=pltpu.SMEM)


def hbm_spec():
    return pl.BlockSpec(memory_space=pl.ANY)


def grids(t):
    rows = lax.broadcasted_iota(jnp.int32, (t, t), 0)
    cols = lax.broadcasted_iota(jnp.int32, (t, t), 1)
    return rows, cols


def allowed_of(seg_row, rows, cols):
    t = rows.shape[0]
    along = jnp.broadcast_to(seg_row, (t, t))
    return (along == jnp.transpose(along)) & (cols <= rows)


def lagged(masked, taps, rows):
    parts = [masked.astype(BF)]
    for a in range(1, taps):
        parts.append(jnp.where(rows >= a, pltpu.roll(masked, a, 0), 0.0).astype(BF))
    return jnp.concatenate(parts, axis=1)


def row_sum(value):
    return jnp.sum(value, axis=0, keepdims=True)


def mean_of(value):
    return jnp.mean(value, axis=1, keepdims=True)


def layer_kernel(cfg, *refs):
    heads, hd, taps, span, docs, shards, units = cfg
    strip = units // shards
    mlp_parts = 2 if strip % 128 == 0 else 1
    given, refs = refs[: 13 + mlp_parts], refs[13 + mlp_parts :]
    x_ref, g_ref, first_norm, second_norm, head_norm, docs_ref, score_ref, mix_ref = given[:8]
    own_first, own_down, own_mlp = given[8:12], given[12], given[13:]
    (
        out_ref, grad_in_ref, grad_first_norm, grad_second_norm, grad_head_norm, grad_score, grad_mix, means,
        all_first, all_mlp, all_down,
        w_first, w_mlp, w_down, wide, g_mlp, seg_all, attn_in, qkv, hat, inv, probs, masked, head_in, w_out,
        middle, slope, silu, hidden, g_gu, g_attn, g_middle, g_qkv, g_hin, d_out_in,
        psend, pown, r1, ysend, r2, psend2, pown2, r1b, r2b, bands, corr, g_wide, lanes, g_mix,
        x_first, x_mlp, x_down, z_first, z_mlp, z_down, small_send, small_recv, small_ref, valid_ref, gain_first, gain_second, gain_all, gain_head,
        ag_send, ag_recv, rs_send, rs_recv, rs_side_recv, rep_send, rep_recv, local, credit,
    ) = refs
    t, d = x_ref.shape
    width = heads * hd
    quarter = d // 4
    lines = shards // 2
    me = lax.axis_index("rep")
    f = lax.axis_index("fsdp")
    plane, core = me // 2, me % 2
    sibling, across = plane * 2 + (1 - core), (1 - plane) * 2 + core
    diagonal = (1 - plane) * 2 + (1 - core)
    z, side = f // 2, f % 2
    partner = 2 * z + (1 - side)
    weights = (w_first, w_mlp, w_down)
    x_lands, z_lands = (x_first, x_mlp, x_down), (z_first, z_mlp, z_down)
    peer_of = (f + 2, f - 2, partner)
    tokens = 4 * t
    part = shards // 4
    rows, cols = grids(t)

    def flip(bit):
        return f + (1 - 2 * ((f // bit) % 2)) * bit

    bits = []
    bit = 1
    while bit < shards:
        bits.append(bit)
        bit *= 2

    barrier = pltpu.get_barrier_semaphore()

    def greet(r, s):
        pl.semaphore_signal(barrier, inc=1, device_id=(r, s), device_id_type=MESH)

    for r in (sibling, across, diagonal):
        greet(r, f)
    greet(me, partner)

    @pl.loop(1, lines)
    def _(s):
        greet(me, 2 * ((z + s) % lines) + side)

    pl.semaphore_wait(barrier, 3 + lines)

    def rep_copy(src, dst, slot, peer):
        return pltpu.make_async_remote_copy(
            src_ref=src, dst_ref=dst, send_sem=rep_send.at[slot], recv_sem=rep_recv.at[slot],
            device_id=(peer, f), device_id_type=MESH,
        )

    def ag(k, block, way):
        return pltpu.make_async_remote_copy(
            src_ref=weights[k].at[block], dst_ref=weights[k].at[block],
            send_sem=ag_send.at[k, way, block], recv_sem=ag_recv.at[k, block],
            device_id=(me, peer_of[way]), device_id_type=MESH,
        )

    def ag_walk(k, s, first, act):
        sides = (side, 1 - side) if k == DOWN else (side,)
        if isinstance(s, int) and s == 0:
            for q in sides:
                block = 2 * z + q
                if k == DOWN and q is not side:
                    first(k, block)

                @pl.when(z < lines - 1)
                def _():
                    act(k, block, UP)

                @pl.when(z > 0)
                def _():
                    act(k, block, DN)

                if k != DOWN:
                    act(k, block, SIDE)
            return

        @pl.when(z - s >= 0)
        def _():
            for q in sides:
                block = 2 * (z - s) + q
                first(k, block)

                @pl.when(z < lines - 1)
                def _():
                    act(k, block, UP)

                if k != DOWN:
                    act(k, block, SIDE)

        @pl.when(z + s < lines)
        def _():
            for q in sides:
                block = 2 * (z + s) + q
                first(k, block)

                @pl.when(z > 0)
                def _():
                    act(k, block, DN)

                if k != DOWN:
                    act(k, block, SIDE)

    def arrived(k, block):
        ag(k, block, SIDE).wait_recv()

    def go(k, block, way):
        ag(k, block, way).start()

    def gone(k, block, way):
        ag(k, block, way).wait_send()

    def ag_steps(k, low, high):
        if low == 0:
            ag_walk(k, 0, arrived, go)
        else:
            pl.loop(low, high)(lambda s: ag_walk(k, s, arrived, go))

    def ag_done(k):
        if k != DOWN:
            pl.loop(0, lines)(lambda zz: arrived(k, 2 * zz + (1 - side)))

    def ag_drain(k):
        nothing = lambda *_: None
        if k == DOWN:
            gone(k, f, SIDE)
        ag_walk(k, 0, nothing, gone)
        pl.loop(1, lines)(lambda s: ag_walk(k, s, nothing, gone))

    def gather_start(fulls, slot):
        for i, full in enumerate(fulls):
            rep_copy(full.at[me], full.at[me], slot + 3 * i, across).start()
            rep_copy(full.at[me], full.at[me], slot + 3 * i + 1, sibling).start()

    def gather_pass(fulls, slot):
        for i, full in enumerate(fulls):
            rep_copy(full.at[me], full.at[me], slot + 3 * i, across).wait_recv()
            rep_copy(full.at[across], full.at[across], slot + 3 * i + 2, sibling).start()

    def gather_end(fulls, slot):
        for i, full in enumerate(fulls):
            rep_copy(full.at[me], full.at[me], slot + 3 * i + 1, sibling).wait_recv()
            rep_copy(full.at[across], full.at[across], slot + 3 * i + 2, sibling).wait_recv()
        for i, full in enumerate(fulls):
            rep_copy(full.at[me], full.at[me], slot + 3 * i, across).wait_send()
            rep_copy(full.at[me], full.at[me], slot + 3 * i + 1, sibling).wait_send()
            rep_copy(full.at[across], full.at[across], slot + 3 * i + 2, sibling).wait_send()

    def pair_of(ref, a, b):
        return jnp.concatenate([ref[a], ref[b]], axis=0)

    def sum_copies(slot, send_buf, first_land, second_land):
        return (
            rep_copy(send_buf, first_land, slot, sibling),
            rep_copy(ysend, second_land, slot + 1, across),
        )

    def column_chunk(i):
        return pl.ds(pl.multiple_of(i * quarter, quarter), quarter)

    def sum_theirs(product, copies, send_buf):
        @pl.loop(0, 4)
        def _(i):
            value = product(1 - core, 2 + (1 - core), i)
            send_buf[0, :, column_chunk(i)] = value[:t].astype(BF)
            send_buf[1, :, column_chunk(i)] = value[t:].astype(BF)

        copies[0].start()

    def sum_ours(product, own_buf):
        @pl.loop(0, 4)
        def _(i):
            value = product(across, me, i)
            own_buf[0, :, column_chunk(i)] = value[:t].astype(own_buf.dtype)
            own_buf[1, :, column_chunk(i)] = value[t:].astype(own_buf.dtype)

    def sum_turn(copies, own_buf, first_land):
        copies[0].wait_recv()
        ysend[...] = (own_buf[0].astype(F32) + first_land[1 - plane].astype(F32)).astype(BF)
        copies[1].start()
        own_buf[1] = (own_buf[1].astype(F32) + first_land[plane].astype(F32)).astype(own_buf.dtype)

    def sum_end(copies, own_buf, second_land):
        copies[1].wait_recv()
        total = own_buf[1].astype(F32) + second_land[...].astype(F32)
        copies[0].wait_send()
        copies[1].wait_send()
        return total

    def yes(condition):
        return int(condition) if isinstance(condition, bool) else condition.astype(jnp.int32)

    def far_slot(at, target):
        return at if lines == 4 else target

    def near_slot(source, target):
        return source if lines == 4 else lines + source - target + 2 - yes(source > target)

    def target_of(s):
        ahead = lines - 1 - z
        first_end, last_end = yes(z == 0), yes(z == lines - 1)
        inner = 1 - first_end - last_end
        if lines == 4:
            near = yes(s == 1) * (z + 1) + yes(s == 2) * (z - 1) + yes(s == 3) * (3 * (2 - z))
        else:
            near = yes(s <= ahead) * (z + s) + yes(s > ahead) * (z - (s - ahead))
        return first_end * (lines - s) + last_end * (s - 1) + inner * near

    def rs_side(k, zz):
        source = weights[k].at[2 * zz + (1 - side)]
        if k == DOWN:
            source = x_mlp.at[zz, pl.ds(0, strip), pl.ds(0, d)]
        return pltpu.make_async_remote_copy(
            src_ref=source, dst_ref=x_lands[k].at[zz],
            send_sem=rs_send.at[k, 0, zz], recv_sem=rs_side_recv.at[k, zz],
            device_id=(me, partner), device_id_type=MESH,
        )

    def rs_hop(k, target):
        up = yes(target > z)
        toward = z + 2 * up - 1
        distance = up * (target - z) + (1 - up) * (z - target)
        far = yes(distance >= 3)
        to = far * toward + (1 - far) * target
        slot = far * far_slot(toward, target) + (1 - far) * near_slot(z, target)
        at = slot
        return pltpu.make_async_remote_copy(
            src_ref=weights[k].at[2 * target + side], dst_ref=z_lands[k].at[at],
            send_sem=rs_send.at[k, 1, 2 * target], recv_sem=rs_recv.at[k, at],
            device_id=(me, 2 * to + side), device_id_type=MESH,
        )

    def rs_landed(k, slot):
        at = slot
        pltpu.make_async_remote_copy(
            src_ref=weights[k].at[f], dst_ref=z_lands[k].at[at],
            send_sem=rs_send.at[k, 1, f], recv_sem=rs_recv.at[k, at],
            device_id=(me, partner), device_id_type=MESH,
        ).wait_recv()
        return z_lands[k], at

    def rs_add(k, block, landed):
        grad = weights[k]
        high = grad.shape[1]
        step = 16 if high % 16 == 0 else high

        @pl.loop(0, high // step)
        def _(i):
            at = pl.ds(pl.multiple_of(i * step, step), step)
            total = grad[block, at, :].astype(F32)
            for land, slot in landed:
                total = total + land[slot, at, :].astype(F32)
            grad[block, at, :] = total.astype(BF)

    def rs_turn(k, s):
        target = target_of(s)
        up = yes(target > z)
        distance = up * (target - z) + (1 - up) * (z - target)
        behind = up * yes(z > 0) + (1 - up) * yes(z < lines - 1)
        rs_side(k, target).wait_recv()
        handed = (distance >= 2) & (behind == 1)

        @pl.when(handed)
        def _():
            land = rs_landed(k, far_slot(z, target))
            rs_add(k, 2 * target + side, [(x_lands[k], target), land])

        @pl.when(jnp.logical_not(handed))
        def _():
            rs_add(k, 2 * target + side, [(x_lands[k], target)])

        rs_hop(k, target).start()

    def rs_close(k):
        first_end, last_end = yes(z == 0), yes(z == lines - 1)
        inner = 1 - first_end - last_end
        one = first_end * 1 + (1 - first_end) * (z - 1)
        two = first_end * 2 + last_end * (lines - 3) + inner * (z + 1)
        rs_side(k, z).wait_recv()
        rs_add(k, f, [(x_lands[k], z), rs_landed(k, near_slot(one, z)), rs_landed(k, near_slot(two, z))])

        @pl.when((z > 0) & (z + 2 < lines))
        def _():
            rs_add(k, f, [rs_landed(k, near_slot(z + 2, z))])

        @pl.when((z < lines - 1) & (z >= 2))
        def _():
            rs_add(k, f, [rs_landed(k, near_slot(z - 2, z))])

    def rs_drain(k):
        if k != DOWN:
            pl.loop(0, lines)(lambda zz: rs_side(k, zz).wait_send())
        pl.loop(1, lines)(lambda s: rs_hop(k, target_of(s)).wait_send())

    outs = (all_first, all_mlp, all_down)

    def final_copies(k, slot):
        own = weights[k].at[f]
        full = outs[k]
        return (
            rep_copy(own, full.at[me], slot, across),
            rep_copy(own, full.at[me], slot + 1, sibling),
            rep_copy(full.at[across], full.at[across], slot + 2, sibling),
            pltpu.make_async_copy(own, full.at[me], local.at[1 + k]),
        )

    def final_start(k, slot):
        a, b, _, here = final_copies(k, slot)
        a.start()
        b.start()
        here.start()

    def final_pass(k, slot):
        a, _, c, _ = final_copies(k, slot)
        a.wait_recv()
        c.start()

    def final_end(k, slot):
        a, b, c, here = final_copies(k, slot)
        b.wait_recv()
        c.wait_recv()
        a.wait_send()
        b.wait_send()
        c.wait_send()
        here.wait()

    def cut(ref, at, size):
        return ref.at[:, pl.ds(pl.multiple_of(at, size), size)]

    sources = [
        [(cut(own_first[i], me * quarter, quarter), w_first.at[f, :, pl.ds(i * quarter, quarter)]) for i in range(4)],
        [(own_mlp[0], w_mlp.at[f])],
        [(own_down.at[pl.ds(pl.multiple_of(me * strip, strip), strip), :], w_down.at[f])],
    ]
    if mlp_parts == 2:
        sources[MLP] = [
            (cut(own_mlp[i // shards], (4 * (i % shards) + me) * strip, strip), w_mlp.at[f, :, pl.ds(i * strip, strip)])
            for i in range(2 * shards)
        ]
    loads, used = [], 4
    for pairs in sources:
        loads.append([pltpu.make_async_copy(a, b, local.at[used + i]) for i, (a, b) in enumerate(pairs)])
        used += len(pairs)
    for k in range(3):
        for load in loads[k]:
            load.start()

    def load_wait(k):
        for load in loads[k]:
            load.wait()

    load_wait(FIRST)
    ag_steps(FIRST, 0, 1)
    load_wait(DOWN)
    ag(DOWN, f, SIDE).start()

    lane = lax.broadcasted_iota(jnp.int32, (1, t), 1)
    seg = jnp.zeros((1, t), F32)
    edge = 0
    for i in range(docs):
        edge = edge + docs_ref[0, i]
        seg = seg + jnp.where(lane >= edge, 1.0, 0.0)
    valid = jnp.where(jnp.transpose(jnp.broadcast_to(seg, (t, t))) < float(docs), 1.0, 0.0)
    valid_ref[...] = valid[:, 0:1]

    def as_row(ref):
        return jnp.concatenate([ref[i : i + 1, :] for i in range(ref.shape[0])], axis=1)

    gain_first[...] = as_row(first_norm)
    gain_second[...] = as_row(second_norm)
    gain_all[...] = as_row(head_norm)
    gain_head[...] = gain_all[:, pl.ds(pl.multiple_of(me * quarter, quarter), quarter)]
    wide[me] = x_ref[...]
    g_mlp[me] = g_ref[...]
    seg_all[me] = jnp.broadcast_to(seg, (8, t))
    entering = (seg_all, wide)
    gather_start(entering, 0)

    diff = cols - rows + (span - 1) // 2

    @pl.loop(0, heads)
    def _(h):
        for a in range(taps):
            band = jnp.zeros((t, t), F32)
            for b in range(span):
                band = jnp.where(diff == b, score_ref[me * heads + h, a, b], band)
            bands[h, a * t : (a + 1) * t, :] = band.astype(BF)

    gather_pass(entering, 0)
    gather_start((g_mlp,), 6)
    ag_steps(FIRST, 1, 2)
    gather_end(entering, 0)

    @pl.loop(0, 4)
    def _(r):
        value = wide[r].astype(F32)
        scale = lax.rsqrt(mean_of(value * value) + 1e-06)
        attn_in[r] = (value * scale * gain_first[...]).astype(BF)

    ag_steps(FIRST, 2, 3)
    load_wait(MLP)
    ag_steps(MLP, 0, 1)
    gather_pass((g_mlp,), 6)
    gather_end((g_mlp,), 6)

    @pl.loop(0, 4)
    def _(r):
        valid = jnp.transpose(jnp.broadcast_to(seg_all[r][0:1, :], (t, t)))[:, 0:1] < float(docs)
        g_mlp[r] = jnp.where(valid, g_mlp[r].astype(F32), 0.0).astype(BF)

    ag_steps(FIRST, 3, lines)
    ag_steps(MLP, 1, 2)
    ag_done(FIRST)

    def w_out_copy(peer, slot):
        return rep_copy(
            w_first.at[pl.ds(peer * part, part), :, pl.ds(3 * quarter, quarter)],
            w_out.at[:, :, pl.ds(pl.multiple_of(me * quarter, quarter), quarter)],
            slot, peer,
        )

    for i, peer in enumerate((sibling, across, diagonal)):
        w_out_copy(peer, 9 + i).start()
    own_out = pltpu.make_async_copy(
        w_first.at[pl.ds(me * part, part), :, pl.ds(3 * quarter, quarter)],
        w_out.at[:, :, pl.ds(pl.multiple_of(me * quarter, quarter), quarter)],
        local.at[0],
    )
    own_out.start()

    for i in range(3):
        value = dot(attn_in[...].reshape(tokens, d), merge(w_first[:, :, i * quarter : (i + 1) * quarter]))
        qkv[:, :, i * quarter : (i + 1) * quarter] = value.astype(BF).reshape(4, t, quarter)
    ag_steps(MLP, 2, 3)
    ag_steps(DOWN, 0, 1)

    def split(ref, row, kind, h):
        return ref[row, :, kind * width + h * hd : kind * width + (h + 1) * hd]

    @pl.loop(0, 4)
    def _(row):
        allowed = allowed_of(seg_all[row][0:1, :], rows, cols)
        for pair in range(heads // 2):
            both = []
            for c in range(2):
                h = 2 * pair + c
                scores = dot(split(qkv, row, 0, h), split(qkv, row, 1, h), NT) * hd**-0.5
                kept = jnp.where(allowed, scores, 0.0)
                masked[row, h] = kept.astype(BF)
                logits = jnp.where(allowed, dot(lagged(kept, taps, rows), bands[h]), -1e30)
                e = jnp.exp(logits - jnp.max(logits, axis=1, keepdims=True))
                p = e / jnp.sum(e, axis=1, keepdims=True)
                probs[row, h] = p
                both.append(p)
            for e in range(2):
                h = 2 * pair + e
                mixed = (mix_ref[me * heads + h, 0] * both[0] + mix_ref[me * heads + h, 1] * both[1]).astype(BF)
                out = dot(mixed, split(qkv, row, 2, h))
                centred = out - mean_of(out)
                scale = lax.rsqrt(mean_of(centred * centred) + 1e-05)
                hat[row, :, h * hd : (h + 1) * hd] = centred * scale
                inv[row, :, h : h + 1] = scale
        head_in[row] = (hat[row] * gain_head[...]).astype(BF)

    for i, peer in enumerate((sibling, across, diagonal)):
        w_out_copy(peer, 9 + i).wait_recv()
    own_out.wait()

    copies = sum_copies(12, psend, r1, r2)
    product = lambda a, b, i: dot(pair_of(head_in, a, b), merge(w_out[:, :, column_chunk(i)]))
    sum_theirs(product, copies, psend)
    sum_ours(product, pown)
    ag_steps(MLP, 3, lines)
    sum_turn(copies, pown, r1)
    total = sum_end(copies, pown, r2)
    attn_part = valid_ref[...] * total
    value = x_ref[...].astype(F32) + attn_part
    middle[...] = value
    stat_attn = jnp.sum(row_sum(attn_part * attn_part), axis=1, keepdims=True)
    scale = lax.rsqrt(mean_of(value * value) + 1e-06)
    wide[me] = (value * scale * gain_second[...]).astype(BF)
    gather_start((wide,), 14)
    ag_steps(DOWN, 1, 2)
    gather_pass((wide,), 14)
    gather_end((wide,), 14)
    mlp_in = wide
    ag_steps(DOWN, 2, 3)
    ag_done(MLP)

    chunk = units // 4

    def in_turn(i):
        if lines != 4:
            return i
        return yes(i < 3) * target_of(i + 1) + yes(i == 3) * z


    @pl.loop(0, 4)
    def _(i):
        p = in_turn(i)
        at = pl.ds(pl.multiple_of(p * chunk, chunk), chunk)
        after = pl.ds(pl.multiple_of(units + p * chunk, chunk), chunk)
        operand = mlp_in[...].reshape(tokens, d)
        gate = dot(operand, merge(w_mlp[:, :, at]))
        upper = dot(operand, merge(w_mlp[:, :, after]))
        sig = 1.0 / (1.0 + jnp.exp(-gate))
        act = gate * sig
        product = (act * upper).astype(BF)
        hidden[:, :, at] = product.reshape(4, t, chunk)
        silu[:, at] = act.astype(BF)
        slope[:, at] = (upper * sig * (1.0 + gate * (1.0 - sig))).astype(BF)
        value = dot(product, g_mlp[...].reshape(tokens, d), TN).reshape(part, strip, d)
        for j in range(part // 2):
            half = jnp.where(side == 0, value[2 * j + 1], value[2 * j])
            x_mlp[p * (part // 2) + j, 0:strip, 0:d] = half.astype(BF)
        pl.loop(0, part // 2)(lambda j: rs_side(DOWN, p * (part // 2) + j).start())

    ag_steps(DOWN, 3, lines)

    @pl.loop(0, 4)
    def _(i):
        span_units = units // 4
        at = pl.ds(pl.multiple_of(i * span_units, span_units), span_units)
        after = pl.ds(pl.multiple_of(units + i * span_units, span_units), span_units)
        g_hidden = dot(g_mlp[...].reshape(tokens, d), merge(w_down[pl.ds(i * part, part)]), NT)
        g_gu[:, :, at] = (g_hidden * slope[:, at].astype(F32)).astype(BF).reshape(4, t, span_units)
        g_gu[:, :, after] = (g_hidden * silu[:, at].astype(F32)).astype(BF).reshape(4, t, span_units)

    mlp_copies = sum_copies(17, psend, r1, r2)
    product = lambda a, b, i: dot(pair_of(g_gu, a, b), merge(w_mlp[pl.ds(i * part, part)]), NT)
    sum_theirs(product, mlp_copies, psend)
    sum_ours(product, pown)

    sum_turn(mlp_copies, pown, r1)

    ag_drain(MLP)

    def send_side(k, p):
        @pl.loop(0, part // 2)
        def _(j):
            zz = p * (part // 2) + j
            rs_side(k, zz).start()

    @pl.loop(0, 4)
    def _(p):
        at = pl.ds(pl.multiple_of(p * quarter, quarter), quarter)
        size = units // 2

        @pl.loop(0, 4)
        def _(j):
            to = pl.ds(pl.multiple_of(j * size, size), size)
            value = dot(mlp_in[:, :, at].reshape(tokens, quarter), g_gu[:, :, to].reshape(tokens, size), TN)
            w_mlp[pl.ds(p * part, part), :, to] = value.reshape(part, w_mlp.shape[1], size).astype(BF)

    total = sum_end(mlp_copies, pown, r2)
    value = middle[...]
    scale = lax.rsqrt(mean_of(value * value) + 1e-06)
    normed = value * scale
    prod = total * normed
    g_second = row_sum(prod)
    mean = mean_of(prod * gain_second[...])
    value = g_ref[...].astype(F32) + scale * (total * gain_second[...] - normed * mean)
    g_middle[...] = value
    g_attn[me] = (valid_ref[...] * value).astype(BF)
    gather_start((g_attn,), 21)
    out_copies = (rep_copy(psend2, r1b, 19, sibling), rep_copy(ysend, r2b, 20, across))
    product = lambda a, b, i: dot(pair_of(hidden, a, b), merge(w_down[:, :, column_chunk(i)]))
    sum_theirs(product, out_copies, psend2)
    sum_ours(product, pown2)
    ag_drain(DOWN)

    @pl.loop(0, 4)
    def _(i):
        span_units = units // 4
        at = pl.ds(pl.multiple_of(i * span_units, span_units), span_units)
        value = dot(hidden[:, :, at].reshape(tokens, span_units), g_mlp[...].reshape(tokens, d), TN)
        w_down[pl.ds(i * part, part)] = value.reshape(part, w_down.shape[1], d).astype(BF)

    pl.loop(0, lines)(lambda zz: rs_side(DOWN, zz).wait_send())
    pl.semaphore_signal(credit, inc=1, device_id=(me, partner), device_id_type=MESH)

    pl.semaphore_wait(credit, 1)
    pl.loop(1, lines)(lambda s: rs_side(MLP, target_of(s)).start())
    rs_side(MLP, z).start()

    gather_pass((g_attn,), 21)
    gather_end((g_attn,), 21)

    @pl.loop(0, 2)
    def _(i):
        both = pl.ds(2 * i, 2)
        value = dot(g_attn[both].reshape(2 * t, d), merge(w_out[...]), NT)
        g_hin[both] = value.reshape(2, t, width)

    d_out = w_out

    @pl.loop(0, 4)
    def _(i):
        value = dot(head_in[...].reshape(tokens, width), g_attn[:, :, column_chunk(i)].reshape(tokens, quarter), TN)
        d_out[:, :, column_chunk(i)] = value.reshape(part, w_first.shape[1], quarter).astype(BF)


    def d_out_copy(peer, slot):
        return rep_copy(
            d_out.at[:, :, pl.ds(pl.multiple_of(peer * quarter, quarter), quarter)],
            d_out_in.at[pl.ds(me * part, part)],
            slot, peer,
        )

    for i, peer in enumerate((sibling, across, diagonal)):
        d_out_copy(peer, 24 + i).start()
    own_d_out = pltpu.make_async_copy(
        d_out.at[:, :, pl.ds(pl.multiple_of(me * quarter, quarter), quarter)],
        d_out_in.at[pl.ds(me * part, part)], local.at[4],
    )
    own_d_out.start()
    pl.loop(1, lines)(lambda s: rs_turn(DOWN, s))

    corr[...] = jnp.zeros_like(corr)
    g_mix[...] = jnp.zeros_like(g_mix)
    lanes[...] = jnp.zeros_like(lanes)

    @pl.loop(0, 4)
    def _(row):
        allowed = allowed_of(seg_all[row][0:1, :], rows, cols)
        g_wide[...] = g_hin[row] * gain_head[...]
        for pair in range(heads // 2):
            g_heads, g_mixed = [], []
            both = [probs[row, 2 * pair + c] for c in range(2)]
            for e in range(2):
                h = 2 * pair + e
                scaled = g_wide[:, h * hd : (h + 1) * hd]
                own_hat = hat[row, :, h * hd : (h + 1) * hd]
                g = inv[row, :, h : h + 1] * (scaled - mean_of(scaled) - own_hat * mean_of(scaled * own_hat))
                g = g.astype(BF)
                g_heads.append(g)
                g_mixed.append(dot(g, split(qkv, row, 2, h), NT))
            for e in range(2):
                h = 2 * pair + e
                mixed = (mix_ref[me * heads + h, 0] * both[0] + mix_ref[me * heads + h, 1] * both[1]).astype(BF)
                g_v = dot(mixed, g_heads[e], TN)
                g_qkv[row, :, 2 * width + h * hd : 2 * width + (h + 1) * hd] = g_v.astype(BF)
                for c in range(2):
                    place = (2 * pair + e) * 2 + c
                    g_mix[place : place + 1, :] += row_sum(g_mixed[e] * both[c])
            for c in range(2):
                h = 2 * pair + c
                g_probs = mix_ref[me * heads + 2 * pair, c] * g_mixed[0] + mix_ref[me * heads + 2 * pair + 1, c] * g_mixed[1]
                weighted = both[c] * g_probs
                g_conv = weighted - both[c] * jnp.sum(weighted, axis=1, keepdims=True)
                corr[h] += dot(lagged(masked[row, h].astype(F32), taps, rows), g_conv.astype(BF), TN)
                g_kept = dot(g_conv.astype(BF), bands[h, 0:t, :], NT)
                for a in range(1, taps):
                    lead = jnp.where(rows < t - a, pltpu.roll(g_conv, t - a, 0), 0.0).astype(BF)
                    g_kept += dot(lead, bands[h, a * t : (a + 1) * t, :], NT)
                g_raw = jnp.where(allowed, g_kept, 0.0).astype(BF)
                g_q = dot(g_raw, split(qkv, row, 1, h)) * hd**-0.5
                g_k = dot(g_raw, split(qkv, row, 0, h), TN) * hd**-0.5
                g_qkv[row, :, h * hd : (h + 1) * hd] = g_q.astype(BF)
                g_qkv[row, :, width + h * hd : width + (h + 1) * hd] = g_k.astype(BF)

    in_copies = sum_copies(27, psend, r1, r2)
    product = lambda a, b, i: dot(pair_of(g_qkv, a, b), merge(w_first[pl.ds(i * part, part), :, 0 : 3 * quarter]), NT)
    sum_theirs(product, in_copies, psend)
    sum_ours(product, pown)
    rs_turn(MLP, 1)
    sum_turn(in_copies, pown, r1)

    ag_drain(FIRST)
    for i, peer in enumerate((sibling, across, diagonal)):
        w_out_copy(peer, 9 + i).wait_send()
        d_out_copy(peer, 24 + i).wait_recv()
    own_d_out.wait()

    @pl.loop(0, 4)
    def _(i):
        p = in_turn(i)
        at = pl.ds(pl.multiple_of(p * quarter, quarter), quarter)
        value = dot(attn_in[:, :, at].reshape(tokens, quarter), g_qkv[...].reshape(tokens, 3 * quarter), TN)
        w_first[pl.ds(p * part, part), :, 0 : 3 * quarter] = value.reshape(part, w_first.shape[1], 3 * quarter).astype(BF)
        w_first[pl.ds(p * part, part), :, 3 * quarter :] = d_out_in[pl.ds(p * part, part)]
        send_side(FIRST, p)

    rs_turn(MLP, 2)
    total = sum_end(in_copies, pown, r2)
    value = x_ref[...].astype(F32)
    scale = lax.rsqrt(mean_of(value * value) + 1e-06)
    normed = value * scale
    prod = total * normed
    g_first = row_sum(prod)
    mean = mean_of(prod * gain_first[...])
    grad_in_ref[...] = (g_middle[...] + scale * (total * gain_first[...] - normed * mean)).astype(BF)

    sum_turn(out_copies, pown2, r1b)
    total = sum_end(out_copies, pown2, r2b)
    mlp_part = valid_ref[...] * total
    value = middle[...] + mlp_part
    out_ref[...] = value.astype(BF)
    stat_out = jnp.sum(row_sum(valid_ref[...] * value * value), axis=1, keepdims=True)
    stat_mlp = jnp.sum(row_sum(mlp_part * mlp_part), axis=1, keepdims=True)

    strips = d // 128
    small_ref[...] = jnp.zeros_like(small_ref)
    for i in range(strips):
        at = slice(128 * i, 128 * (i + 1))
        small_ref[i : i + 1, :] = g_first[:, at]
        small_ref[strips + i : strips + i + 1, :] = g_second[:, at]
    own_gain = row_sum((g_hin[...] * hat[...]).reshape(tokens, width))
    for i in range(width // 128):
        small_ref[pl.ds(2 * strips + me * (width // 128) + i, 1), :] = own_gain[:, 128 * i : 128 * (i + 1)]
    base = 3 * strips
    for h in range(heads):
        for a in range(taps):
            tile = corr[h, a * t : (a + 1) * t, :]
            for b in range(span):
                lanes[a * span + b : a * span + b + 1, :] = row_sum(jnp.where(diff == b, tile, 0.0))
        small_ref[pl.ds(base + me * heads + h, 1), :] = row_sum(jnp.transpose(lanes[...]))
    base += 4 * heads
    lanes[0 : 2 * heads, :] = g_mix[...]
    lanes[2 * heads :, :] = jnp.zeros((t - 2 * heads, t), F32)
    small_ref[pl.ds(base + me, 1), :] = row_sum(jnp.transpose(lanes[...]))
    base += 4
    lane = lax.broadcasted_iota(jnp.int32, (1, 128), 1)
    count = jnp.sum(row_sum(jnp.broadcast_to(valid_ref[...], (t, 128))), axis=1, keepdims=True) * (1.0 / 128.0)
    stats = jnp.zeros((1, 128), F32)
    for i, stat in enumerate((stat_out, stat_attn, stat_mlp, count)):
        stats = jnp.where(lane == i, stat, stats)
    small_ref[base : base + 1, :] = stats

    peers = [(sibling, f), (across, f)] + [(me, flip(bit)) for bit in bits]

    def small_copy(i):
        return pltpu.make_async_remote_copy(
            src_ref=small_send.at[i], dst_ref=small_recv.at[i],
            send_sem=rep_send.at[40 + i], recv_sem=rep_recv.at[40 + i],
            device_id=peers[i], device_id_type=MESH,
        )

    def small_step(i):
        small_send[i] = small_ref[...]
        small_copy(i).start()

    def small_take(i):
        small_copy(i).wait_recv()
        small_ref[...] = small_ref[...] + small_recv[i]

    rs_close(DOWN)
    final_start(DOWN, 30)
    pl.loop(3, lines)(lambda s: rs_turn(MLP, s))
    final_pass(DOWN, 30)
    small_step(0)
    small_take(0)
    small_step(1)
    rs_turn(FIRST, 1)
    rs_close(MLP)
    final_start(MLP, 33)
    small_take(1)
    small_step(2)
    pl.loop(2, lines)(lambda s: rs_turn(FIRST, s))
    final_pass(MLP, 33)
    rs_close(FIRST)
    final_start(FIRST, 36)
    for i in range(2, len(peers)):
        small_take(i)
        if i + 1 < len(peers):
            small_step(i + 1)
    final_pass(FIRST, 36)
    grad_first_norm[...] = small_ref[0:strips, :]
    grad_second_norm[...] = small_ref[strips : 2 * strips, :]
    grad_head_norm[...] = small_ref[2 * strips : 3 * strips, :]
    at = 3 * strips
    grad_score[...] = small_ref[at : at + 4 * heads, :]
    grad_mix[...] = small_ref[at + 4 * heads : at + 4 * heads + 4, :]
    sums = small_ref[at + 4 * heads + 4 : at + 4 * heads + 5, :]
    means[...] = jnp.sqrt(sums / (sums[:, 3:4] * float(d)))
    for k in range(3):
        final_end(k, (36, 33, 30)[k])
    for k in range(3):
        rs_drain(k)
    for i in range(len(peers)):
        small_copy(i).wait_send()
    for i, peer in enumerate((sibling, across, diagonal)):
        d_out_copy(peer, 24 + i).wait_send()


def run_layer(cfg, vectors, scalars, first_in, down_in, mlp_in, sizes):
    heads, hd, taps, span, docs, shards, units = cfg
    t, d = vectors[0].shape
    width = heads * hd
    first, mlp, down = shards_in = sizes
    bits = shards.bit_length() - 1
    lines = shards // 2
    slots = lines if lines == 4 else lines + 4

    def shape(dtype, *dims):
        return jax.ShapeDtypeStruct(dims, dtype)

    v = pltpu.VMEM
    dma = pltpu.SemaphoreType.DMA
    out_shape = (
        shape(BF, t, d), shape(BF, t, d), *(shape(F32, d // 128, 128) for _ in range(3)),
        shape(F32, 4 * heads, 128), shape(F32, 4, 128), shape(F32, 1, 128),
        *(shape(BF, 4, *s.shape) for s in shards_in),
    )
    scratch = [
        *(v((shards, *s.shape), BF) for s in shards_in),
        v((4, t, d), BF), v((4, t, d), BF), v((4, 8, t), F32), v((4, t, d), BF), v((4, t, 3 * width), BF),
        v((4, t, width), F32), v((4, t, 128), F32), v((4, heads, t, t), F32), v((4, heads, t, t), BF),
        v((4, t, width), BF), v((shards // 4, first.shape[0], d), BF),
        v((t, d), F32), v((4 * t, units), BF), v((4 * t, units), BF), v((4, t, units), BF), v((4, t, 2 * units), BF),
        v((4, t, d), BF), v((t, d), F32), v((4, t, 3 * width), BF), v((4, t, width), F32),
        v((shards, first.shape[0], width), BF),
        v((2, t, d), BF), v((2, t, d), BF), v((2, t, d), BF), v((t, d), BF), v((t, d), BF),
        v((2, t, d), BF), v((2, t, d), BF), v((2, t, d), BF), v((t, d), BF),
        v((heads, taps * t, t), BF), v((heads, taps * t, t), F32), v((t, width), F32), v((t, t), F32), v((2 * heads, t), F32),
        *(v((lines, *s.shape), BF) for s in shards_in), *(v((slots, *s.shape), BF) for s in shards_in), v((2 + bits, 64, 128), F32), v((2 + bits, 64, 128), F32),
        v((64, 128), F32), v((t, 1), F32), v((1, d), F32), v((1, d), F32), v((1, d), F32), v((1, width), F32),
        dma((3, 3, shards)), dma((3, shards)), dma((3, 2, shards)), dma((3, slots)), dma((3, lines)), dma((48,)), dma((48,)), dma((10 + 2 * shards,)), pltpu.SemaphoreType.REGULAR,
    ]
    return pl.pallas_call(
        functools.partial(layer_kernel, cfg),
        out_shape=out_shape,
        in_specs=[vmem_spec()] * 5 + [smem_spec()] * 3 + [hbm_spec()] * (5 + len(mlp_in)),
        out_specs=(vmem_spec(),) * 8 + (hbm_spec(),) * 3,
        scratch_shapes=scratch,
        compiler_params=pltpu.CompilerParams(
            collective_id=0, has_side_effects=True, vmem_limit_bytes=VMEM_LIMIT
        ),
    )(*vectors, *scalars, *first_in, down_in, *mlp_in)


def widen_kernel(strip, count, first_ref, mlp_ref, down_ref, *outs):
    quarter = first_ref.shape[2] // 4
    for r in range(4):
        for k in range(4):
            outs[k][:, r * quarter : (r + 1) * quarter] = first_ref[r, :, k * quarter : (k + 1) * quarter].astype(F32)
        outs[6][r] = down_ref[r].astype(F32)
        for k in range(2):
            for i in range(count):
                at = (4 * i + r) * strip
                outs[4 + k][:, at : at + strip] = mlp_ref[r, :, (k * count + i) * strip : (k * count + i + 1) * strip].astype(F32)


def widen(first, mlp, down, strip, count):
    _, rows, d = first.shape
    steps = 4 if rows % 64 == 0 and down.shape[1] % 64 == 0 else 1
    hidden = 4 * strip * count
    rows_step, down_step = rows // steps, down.shape[1] // steps

    def taken(array, size):
        return pl.BlockSpec((4, size, array.shape[2]), lambda i: (0, i, 0))

    def given(size, width):
        return pl.BlockSpec((size, width), lambda i: (i, 0))

    return pl.pallas_call(
        functools.partial(widen_kernel, strip, count),
        grid=(steps,),
        out_shape=tuple(jax.ShapeDtypeStruct((rows, d), F32) for _ in range(4))
        + tuple(jax.ShapeDtypeStruct((rows, hidden), F32) for _ in range(2))
        + (jax.ShapeDtypeStruct(down.shape, F32),),
        in_specs=[taken(first, rows_step), taken(mlp, rows_step), taken(down, down_step)],
        out_specs=tuple(given(rows_step, d) for _ in range(4))
        + tuple(given(rows_step, hidden) for _ in range(2))
        + (taken(down, down_step),),
        compiler_params=pltpu.CompilerParams(vmem_limit_bytes=VMEM_LIMIT),
    )(first, mlp, down)


def per_device(
    hidden_in,
    doc_lengths,
    w_query,
    w_key,
    w_value,
    w_output,
    w_gate,
    w_up,
    w_down,
    attn_norm,
    mlp_norm,
    head_norm,
    score_kernel,
    head_mixing,
    grad_out,
):
    _, t, d = hidden_in.shape
    reps = lax.axis_size("rep")
    shards = lax.axis_size("fsdp")
    me = lax.axis_index("rep")
    hidden = w_gate.shape[1]
    heads = H // reps
    hd = d // H
    quarter = d // reps
    units = hidden // reps
    strip = units // shards
    taps, span = score_kernel.shape[1:]
    docs = doc_lengths.shape[1] - 1
    rows_here = w_gate.shape[0]

    def mine(array, size, axis):
        return lax.dynamic_slice_in_dim(array, me * size, size, axis)

    def strips(w):
        return mine(w.reshape(rows_here, shards, reps, strip), 1, 2).reshape(rows_here, units)

    if strip % 128 == 0:
        mlp_in = (w_gate, w_up)
    else:
        mlp_in = (jnp.concatenate([strips(w_gate), strips(w_up)], axis=1),)
    lines = d // 128
    cfg = (heads, hd, taps, span, docs, shards, units)
    shape_of = jax.ShapeDtypeStruct
    block_out, grad_in, n_first, n_second, n_head, g_score, g_mix, means, a_first, a_mlp, a_down = run_layer(
        cfg,
        (hidden_in.reshape(t, d), grad_out.reshape(t, d), *(n.reshape(lines, 128) for n in (attn_norm, mlp_norm, head_norm))),
        (doc_lengths, score_kernel, head_mixing),
        (w_query, w_key, w_value, w_output),
        w_down,
        mlp_in,
        (shape_of((rows_here, d), BF), shape_of((rows_here, 2 * units), BF), shape_of((strip, d), BF)),
    )
    if strip % 128 == 0:
        g_q, g_k, g_v, g_o, g_gate, g_up, g_down = widen(a_first, a_mlp, a_down, strip, shards)
    else:
        first = a_first.astype(F32).reshape(reps, rows_here, 4, quarter)
        first = jnp.moveaxis(first, 0, 2).reshape(rows_here, 4, d)
        g_q, g_k, g_v, g_o = (first[:, k] for k in range(4))
        mlp = a_mlp.astype(F32).reshape(reps, rows_here, 2, shards, strip)
        mlp = jnp.moveaxis(mlp, 0, 3).reshape(rows_here, 2, hidden)
        g_gate, g_up = mlp[:, 0], mlp[:, 1]
        g_down = a_down.astype(F32)
    return (
        block_out.reshape(hidden_in.shape),
        grad_in.reshape(hidden_in.shape),
        g_q,
        g_k,
        g_v,
        g_o,
        g_gate,
        g_up,
        g_down.reshape(w_down.shape),
        n_first.reshape(d),
        n_second.reshape(d),
        n_head.reshape(d),
        g_score[:, : taps * span].reshape(score_kernel.shape),
        g_mix[:, : 2 * heads].reshape(head_mixing.shape),
        means[0, :3],
    )


def solution(mesh):
    rows = P(("rep", "fsdp"), None, None)
    split = P("fsdp", None)
    placed = (rows, P(("rep", "fsdp"), None)) + (split,) * 7 + (P(),) * 5 + (rows,)
    return jax.shard_map(
        per_device,
        mesh=mesh,
        in_specs=placed,
        out_specs=(rows, rows) + (split,) * 7 + (P(),) * 6,
        check_vma=False,
    )
```
